32 devices in a mesh: cross: 8 (over z, y), along: 4 (over x, core).
Axes of the slice: x: 2, y: 2, z: 4, core: 2. Of those that a mesh axis runs over, the one named last changes fastest.
Arguments:
- source: float32 [16, 64, 2048], P(None, 'along', 'cross'), may hold values from -6 to 6
- inv_density: float32 [16, 64, 2048], P(None, 'along', 'cross'), may hold values from 0.3 to 3
Outputs:
- pressure: float32 [16, 64, 2048], P(None, 'along', 'cross')
- residual: float32 [16, 64, 2048], P(None, 'along', 'cross')
The draws below stay inside these ranges and needn't reach their ends.
All inputs are finite; a program needn't handle non-finite values.
Results may differ from the reference program's by a relative error of at most 0.0003.
Values sent between devices are 32-bit elements; how exact they have to be, the bound alone decides.
No kernel may reach another device: no remote copies, remote signals or barrier semaphores. Data moves between devices by JAX's collectives and lax.ppermute only.
A program may use at most 128 MiB of HBM per device.

```python
import math
import jax
import jax.numpy as jnp

NZ = 16
SWEEPS = 4
NX = 64
NY = 2048
LEVELS = 5


def draw_source(key, part):
    key = jax.random.fold_in(key, 7)
    return jnp.clip(jax.random.normal(key, (NZ, NX, NY), jnp.float32), -5.0, 5.0)


def block_levels(stream_key, dims, shards, smallest, top_value):
    level = 1.0
    for position, shards_of in shards:
        steps = jax.random.uniform(jax.random.fold_in(jax.random.fold_in(stream_key, 6), position), (shards_of,), jnp.float32, smallest / len(shards), top_value / len(shards))
        level = level * jnp.repeat(jnp.exp(steps), dims[position] // shards_of).reshape((-1,) + (1,) * (len(dims) - 1 - position))
    return level


def setup_inputs(seed: int = 0) -> dict:
    key_of = jax.random.split(jax.random.key(seed), 3)
    source = draw_source(jax.random.fold_in(key_of[2], 71), 0)
    inv_density = jnp.clip(jnp.exp(math.log(3.0) - 2.3025851 * jax.random.uniform(key_of[1], (NZ, NX, NY), jnp.float32) ** block_levels(key_of[1], (NZ, NX, NY), ((1, 4), (2, 8)), -0.2, 0.2)), 0.3, 3.0)
    return dict(source=source, inv_density=inv_density)


along_weight = 0.25
cross_weight = 1.0
vertical_weight = 0.5
relaxation = 0.8


def harmonic(first, second):
    return 2.0 * first * second / (first + second)


def faces_from(density, padded):
    west_face = along_weight * harmonic(density, padded[:, :-2, 1:-1])
    east_face = along_weight * harmonic(density, padded[:, 2:, 1:-1])
    south_face = cross_weight * harmonic(density, padded[:, 1:-1, :-2])
    north_face = cross_weight * harmonic(density, padded[:, 1:-1, 2:])
    upper_face = jnp.concatenate([2.0 * vertical_weight * density[:1], vertical_weight * harmonic(density[1:], density[:-1])], 0)
    return (west_face, east_face, south_face, north_face, upper_face)


def below_of(upper_face):
    return jnp.concatenate([upper_face[1:], jnp.zeros_like(upper_face[:1])], 0)


def paired(values):
    return values[:, :, 0::2] + values[:, :, 1::2]


def coarsen(face_set):
    west_face, east_face, south_face, north_face, upper_face = face_set
    return (paired(west_face), paired(east_face), 0.5 * south_face[:, :, 0::2], 0.5 * north_face[:, :, 1::2], paired(upper_face))


def centre_of(face_set):
    west_face, east_face, south_face, north_face, upper_face = face_set
    return west_face + east_face + south_face + north_face + upper_face + below_of(upper_face)


def pivots_of(centre, upper_face):
    lower_face = below_of(upper_face)
    pivot_rows = [centre[0]]
    for layer_no in range(1, centre.shape[0]):
        pivot_rows.append(centre[layer_no] - upper_face[layer_no] * lower_face[layer_no - 1] / pivot_rows[-1])
    return jnp.stack(pivot_rows)


def column_solve(pivot_rows, upper_face, remain):
    lower_face = below_of(upper_face)
    layer_count = remain.shape[0]
    forward = [remain[0]]
    for layer_no in range(1, layer_count):
        forward.append(remain[layer_no] + upper_face[layer_no] * forward[-1] / pivot_rows[layer_no - 1])
    result = [None] * layer_count
    result[layer_count - 1] = forward[layer_count - 1] / pivot_rows[layer_count - 1]
    for layer_no in range(layer_count - 2, -1, -1):
        result[layer_no] = (forward[layer_no] + lower_face[layer_no] * result[layer_no + 1]) / pivot_rows[layer_no]
    return jnp.stack(result)


def apply_operator(face_set, centre, current, west_side, east_side, south_side, north_side):
    west_face, east_face, south_face, north_face, upper_face = face_set
    above = jnp.concatenate([jnp.zeros_like(current[:1]), current[:-1]], 0)
    beneath = jnp.concatenate([current[1:], jnp.zeros_like(current[:1])], 0)
    return (centre * current - west_face * west_side - east_face * east_side - south_face * south_side
            - north_face * north_side - upper_face * above - below_of(upper_face) * beneath)


def reference(source, inv_density):
    padded = jnp.pad(inv_density, ((0, 0), (1, 1), (1, 1)))
    face_list = [faces_from(inv_density, padded)]
    for level_no in range(1, LEVELS):
        face_list.append(coarsen(face_list[-1]))
    centre_list = [centre_of(face_set) for face_set in face_list]
    pivot_list = [pivots_of(centre_list[level_no], face_list[level_no][4]) for level_no in range(LEVELS)]

    def operate(level_no, current):
        padded_now = jnp.pad(current, ((0, 0), (1, 1), (1, 1)))
        return apply_operator(face_list[level_no], centre_list[level_no], current,
                              padded_now[:, :-2, 1:-1], padded_now[:, 2:, 1:-1],
                              padded_now[:, 1:-1, :-2], padded_now[:, 1:-1, 2:])

    def smooth(level_no, current, forcing):
        if current is None:
            return relaxation * column_solve(pivot_list[level_no], face_list[level_no][4], forcing)
        remain = forcing - operate(level_no, current)
        return current + relaxation * column_solve(pivot_list[level_no], face_list[level_no][4], remain)

    def cycle(level_no, forcing):
        current = smooth(level_no, None, forcing)
        if level_no == LEVELS - 1:
            for sweep_no in range(SWEEPS - 1):
                current = smooth(level_no, current, forcing)
            return current
        remain = forcing - operate(level_no, current)
        coarse = cycle(level_no + 1, paired(remain))
        current = current + jnp.repeat(coarse, 2, axis=2)
        return smooth(level_no, current, forcing)

    pressure = cycle(0, source)
    return pressure, source - operate(0, pressure)
```

```python
import functools
import math

import jax
import jax.numpy as jnp
from jax import lax
from jax.experimental import pallas as pl
from jax.experimental.pallas import tpu as pltpu
from jax.sharding import PartitionSpec as P

SWEEPS = 4

along_weight = 0.25
cross_weight = 1.0
vertical_weight = 0.5
relaxation = 0.8

LANES = 128
GUARD = 8
TINY = 1e-30


def rounded_up(count, step):
    return -(-count // step) * step


def shifted(array, axis, by):
    devices = lax.axis_size(axis)
    pairs = [(i, i + by) for i in range(devices) if 0 <= i + by < devices]
    return lax.ppermute(array, axis, pairs)


def beside(block, axis, dim, width):
    size = block.shape[dim]
    before, after = [], []
    hop = 1
    while width > 0:
        take = min(width, size)
        tail = lax.slice_in_dim(block, size - take, size, axis=dim)
        head = lax.slice_in_dim(block, 0, take, axis=dim)
        before.insert(0, shifted(tail, axis, hop))
        after.append(shifted(head, axis, -hop))
        width -= take
        hop += 1
    if len(before) == 1:
        return before[0], after[0]
    return jnp.concatenate(before, dim), jnp.concatenate(after, dim)


class Plan:
    def __init__(self, cross_count, layers, rows, cols):
        self.coarsest = cross_count.bit_length()
        self.layers, self.own_rows, self.own_cols = layers, rows, cols
        self.row_reach = SWEEPS + 2 * self.coarsest
        reach = SWEEPS
        for _ in range(self.coarsest):
            reach = 2 * reach + 1
        self.col_reach = reach + 1
        chunks = 1
        while (chunks * LANES - cols) // 2 < self.col_reach:
            chunks *= 2
        self.chunks = chunks
        self.side_cols = (chunks * LANES - cols) // 2
        self.rows = rounded_up(rows + 2 * self.row_reach, 8)
        self.side_rows = rounded_up(self.row_reach + 1, 8)

    def level_chunks(self, level_no):
        return max(1, self.chunks >> level_no)

    def spread(self, level_no):
        return max(1, (1 << level_no) // self.chunks)


def lane_numbers(rows):
    return lax.broadcasted_iota(jnp.int32, (rows, LANES), 1)


def window_kernel(plan, own_ref, before_ref, after_ref, out_ref):
    chunks, rows = plan.chunks, plan.own_rows
    lane = lane_numbers(rows)
    picks = [(chunks * lane + chunk) % LANES for chunk in range(chunks)]
    part = lane // (LANES // chunks)

    def layer_step(which, layer_no):
        tiles = []
        for ref in (before_ref, own_ref, after_ref):
            for first in range(0, ref.shape[3], LANES):
                tiles.append(ref[which, layer_no, :, first : first + LANES])
        for chunk in range(chunks):
            value = jnp.take_along_axis(tiles[0], picks[chunk], axis=1)
            for tile_no in range(1, chunks):
                other = jnp.take_along_axis(tiles[tile_no], picks[chunk], axis=1)
                value = jnp.where(part == tile_no, other, value)
            out_ref[which, layer_no, chunk] = value

    for which in range(2):
        pl.loop(0, plan.layers)(functools.partial(layer_step, which))


def reciprocal(value):
    guess = pl.reciprocal(value, approx=True)
    return guess * (2.0 - value * guess)


def ratio(first, second):
    return first * second * reciprocal(jnp.maximum(first + second, TINY))


def previous_of(cells, spread):
    return [pltpu.roll(cells[-1], spread, 1)] + cells[:-1]


def next_of(cells, spread):
    return cells[1:] + [pltpu.roll(cells[0], LANES - spread, 1)]


def first_of_pair(value, spread):
    lane = lane_numbers(value.shape[0])
    return (lane // spread) % 2 == 0


def paired(cells, spread):
    if len(cells) > 1:
        return [cells[2 * k] + cells[2 * k + 1] for k in range(len(cells) // 2)]
    value = cells[0]
    other = jnp.where(
        first_of_pair(value, spread),
        pltpu.roll(value, LANES - spread, 1),
        pltpu.roll(value, spread, 1),
    )
    return [value + other]


def firsts(cells, spread):
    if len(cells) > 1:
        return cells[0::2]
    value = cells[0]
    return [jnp.where(first_of_pair(value, spread), value, pltpu.roll(value, spread, 1))]


def cycle_kernel(plan, own_ref, before_ref, after_ref, pressure_ref, residual_ref, *scratch):
    levels = plan.coarsest + 1
    coarsest = plan.coarsest
    layers, rows = plan.layers, plan.rows
    reach, own_rows = plan.row_reach, plan.own_rows
    scratch = list(scratch)
    upright, centre0, upper0 = scratch[:3]
    rest = scratch[3:]
    west, south, factor, inverse, value, forcing = [
        rest[i * levels : (i + 1) * levels] for i in range(6)
    ]
    upper = [upper0] + forcing[1:]
    density = value[0]
    count = [plan.level_chunks(m) for m in range(levels)]
    spread = [plan.spread(m) for m in range(levels)]

    side = before_ref.shape[3]

    def assemble(layer_no):
        zeros = jnp.zeros((GUARD, LANES), jnp.float32)
        for c in range(count[0]):
            density[layer_no, c, 0:GUARD] = zeros
            tail = rounded_up(GUARD + reach + own_rows + reach + 1, 8)
            density[layer_no, c, tail - 8 : tail] = zeros
            density[layer_no, c, GUARD - 1 : GUARD + reach] = before_ref[
                0, layer_no, c, side - reach - 1 : side
            ]
            density[layer_no, c, GUARD + reach : GUARD + reach + own_rows] = own_ref[0, layer_no, c]
            start = GUARD + reach + own_rows
            density[layer_no, c, start : start + reach + 1] = after_ref[0, layer_no, c, 0 : reach + 1]
            forcing[0][layer_no, c, rows - 8 : rows] = zeros
            forcing[0][layer_no, c, 0:reach] = before_ref[1, layer_no, c, side - reach : side]
            forcing[0][layer_no, c, reach : reach + own_rows] = own_ref[1, layer_no, c]
            start = reach + own_rows
            forcing[0][layer_no, c, start : start + reach] = after_ref[1, layer_no, c, 0:reach]

    pl.loop(0, layers)(assemble)

    def faces(layer_no, first):
        wests, souths, uppers = [], [], []
        cells = [density[layer_no, c, GUARD : GUARD + rows] for c in range(count[0])]
        southern = previous_of(cells, 1)
        for c in range(count[0]):
            wests.append(
                2.0
                * along_weight
                * ratio(
                    density[layer_no, c, GUARD : 2 * GUARD + rows],
                    density[layer_no, c, GUARD - 1 : 2 * GUARD + rows - 1],
                )
            )
            souths.append(2.0 * cross_weight * ratio(cells[c], southern[c]))
            if first:
                uppers.append(2.0 * vertical_weight * cells[c])
            else:
                uppers.append(
                    2.0
                    * vertical_weight
                    * ratio(cells[c], density[layer_no - 1, c, GUARD : GUARD + rows])
                )
        for m in range(levels):
            if m > 0:
                wests = paired(wests, spread[m - 1])
                souths = [0.5 * each for each in firsts(souths, spread[m - 1])]
                uppers = paired(uppers, spread[m - 1])
            for c in range(count[m]):
                west[m][layer_no, c] = wests[c]
                south[m][layer_no, c] = souths[c]
                upper[m][layer_no, c] = uppers[c]
            south[m][layer_no, count[m]] = pltpu.roll(souths[0], LANES - spread[m], 1)

    faces(0, True)
    pl.loop(1, layers)(lambda layer_no: faces(layer_no, False))
    for m in range(levels):
        for c in range(count[m]):
            upper[m][layers, c] = jnp.zeros((rows, LANES), jnp.float32)

    def clear_guards(layer_no):
        zeros = jnp.zeros((GUARD, LANES), jnp.float32)
        for m in range(levels):
            for c in range(count[m]):
                value[m][layer_no, c, 0:GUARD] = zeros
                value[m][layer_no, c, GUARD + rows : 2 * GUARD + rows] = zeros

    pl.loop(0, layers)(clear_guards)

    def pivots(layer_no, before, first):
        after = []
        for m in range(levels):
            for c in range(count[m]):
                above = upper[m][layer_no, c]
                centre = (
                    west[m][layer_no, c, 0:rows]
                    + west[m][layer_no, c, 1 : rows + 1]
                    + south[m][layer_no, c]
                    + south[m][layer_no, c + 1]
                    + above
                    + upper[m][layer_no + 1, c]
                )
                if m == 0:
                    centre0[layer_no, c] = centre[reach : reach + own_rows]
                if first:
                    pivot = centre
                else:
                    share = above * before[len(after)]
                    factor[m][layer_no, c] = share
                    pivot = centre - above * share
                inverted = reciprocal(jnp.maximum(pivot, TINY))
                inverse[m][layer_no, c] = relaxation * inverted
                after.append(inverted)
        return tuple(after)

    lax.fori_loop(1, layers, lambda z, before: pivots(z, before, False), pivots(0, None, True))

    def around(m, layer_no, low, high):
        cells = [value[m][layer_no, c, GUARD + low : GUARD + high] for c in range(count[m])]
        behind, ahead = previous_of(cells, spread[m]), next_of(cells, spread[m])
        out = []
        for c in range(count[m]):
            out.append(
                west[m][layer_no, c, low:high]
                * value[m][layer_no, c, GUARD + low - 1 : GUARD + high - 1]
                + west[m][layer_no, c, low + 1 : high + 1]
                * value[m][layer_no, c, GUARD + low + 1 : GUARD + high + 1]
                + south[m][layer_no, c, low:high] * behind[c]
                + south[m][layer_no, c + 1, low:high] * ahead[c]
            )
        return out

    def solve(m, low, high, right_side, held, offset, store):
        span = slice(offset + low, offset + high)

        def down(layer_no, before):
            now = right_side(layer_no)
            if before is not None:
                now = [
                    now[c] + factor[m][layer_no, c, low:high] * before[c] for c in range(count[m])
                ]
            for c in range(count[m]):
                held[layer_no, c, span] = now[c] * inverse[m][layer_no, c, low:high]
            return tuple(now)

        def up(step, below):
            layer_no = layers - 1 - step
            now = [held[layer_no, c, span] for c in range(count[m])]
            if below is not None:
                now = [
                    now[c] + factor[m][layer_no + 1, c, low:high] * below[c]
                    for c in range(count[m])
                ]
            store(layer_no, now)
            return tuple(now)

        lax.fori_loop(1, layers, down, down(0, None))
        lax.fori_loop(1, layers, up, up(0, None))

    def first_sweep(m):
        def right_side(layer_no):
            return [forcing[m][layer_no, c] for c in range(count[m])]

        def store(layer_no, now):
            for c in range(count[m]):
                value[m][layer_no, c, GUARD : GUARD + rows] = now[c]

        solve(m, 0, rows, right_side, value[m], GUARD, store)

    def later_sweep(m, low, high, prolong):
        def right_side(layer_no):
            flow = around(m, layer_no, low, high)
            return [forcing[m][layer_no, c, low:high] + flow[c] for c in range(count[m])]

        def store(layer_no, now):
            for c in range(count[m]):
                span = slice(GUARD + low, GUARD + high)
                new = (1.0 - relaxation) * value[m][layer_no, c, span] + now[c]
                value[m][layer_no, c, span] = new
                if prolong:
                    children = (2 * c, 2 * c + 1) if count[m - 1] > count[m] else (c,)
                    for child in children:
                        value[m - 1][layer_no, child, span] += new

        held = upright if m == coarsest else inverse[m]
        solve(m, low, high, right_side, held, 0, store)

    for m in range(coarsest):
        first_sweep(m)

        def restrict(layer_no, m=m):
            flow = around(m, layer_no, 0, rows)
            remain = [
                (1.0 - relaxation) * forcing[m][layer_no, c] + flow[c] for c in range(count[m])
            ]
            for c, each in enumerate(paired(remain, spread[m])):
                forcing[m + 1][layer_no, c] = each

        pl.loop(0, layers)(restrict)

    first_sweep(coarsest)
    for sweep_no in range(1, SWEEPS):
        later_sweep(coarsest, 0, rows, sweep_no == SWEEPS - 1)

    for m in range(coarsest - 1, -1, -1):
        low = (reach - m - 1) // 8 * 8
        high = rounded_up(reach + own_rows + m + 1, 8)
        later_sweep(m, low, high, m > 0)

    chunks = count[0]
    lane = lane_numbers(own_rows)

    def in_order(cells, tile_no):
        start = (plan.side_cols + tile_no * LANES) // chunks
        pick = start + lane // chunks
        out = jnp.take_along_axis(cells[0], pick, axis=1)
        for c in range(1, chunks):
            out = jnp.where(lane % chunks == c, jnp.take_along_axis(cells[c], pick, axis=1), out)
        return out

    def finish(layer_no, top, bottom):
        low, high = reach, reach + own_rows
        span = slice(GUARD + low, GUARD + high)
        flow = around(0, layer_no, low, high)
        cells, remains = [], []
        for c in range(chunks):
            now = value[0][layer_no, c, span]
            remain = forcing[0][layer_no, c, low:high] - centre0[layer_no, c] * now + flow[c]
            if not top:
                remain += upper[0][layer_no, c, low:high] * value[0][layer_no - 1, c, span]
            if not bottom:
                remain += upper[0][layer_no + 1, c, low:high] * value[0][layer_no + 1, c, span]
            cells.append(now)
            remains.append(remain)
        for tile_no in range(plan.own_cols // LANES):
            columns = slice(tile_no * LANES, (tile_no + 1) * LANES)
            pressure_ref[layer_no, :, columns] = in_order(cells, tile_no)
            residual_ref[layer_no, :, columns] = in_order(remains, tile_no)

    finish(0, True, False)
    pl.loop(1, layers - 1)(lambda layer_no: finish(layer_no, False, False))
    finish(layers - 1, False, True)


def per_device(source, inv_density):
    layers, rows, cols = source.shape
    plan = Plan(lax.axis_size("cross"), layers, rows, cols)
    levels = plan.coarsest + 1
    both = jnp.stack([inv_density, source])
    before, after = beside(both, "cross", 3, plan.side_cols)
    vmem = pl.BlockSpec(memory_space=pltpu.VMEM)
    window = pl.pallas_call(
        functools.partial(window_kernel, plan),
        out_shape=jax.ShapeDtypeStruct((2, layers, plan.chunks, rows, LANES), jnp.float32),
        in_specs=[vmem] * 3,
        out_specs=vmem,
        compiler_params=pltpu.CompilerParams(vmem_limit_bytes=48 << 20),
    )(both, before, after)
    before, after = beside(window, "along", 3, plan.side_rows)

    def room(*shape):
        return pltpu.VMEM(shape + (LANES,), jnp.float32)

    total, high = plan.rows, plan.rows + GUARD
    counts = [plan.level_chunks(m) for m in range(levels)]
    scratch = [
        room(layers, counts[-1], total),
        room(layers, counts[0], rows),
        room(layers + 1, counts[0], total),
    ]
    scratch += [room(layers, n, high) for n in counts]
    scratch += [room(layers, n + 1, total) for n in counts]
    scratch += [room(layers, n, total) for n in counts]
    scratch += [room(layers, n, total) for n in counts]
    scratch += [room(layers, n, high + GUARD) for n in counts]
    scratch += [room(layers, counts[0], total)]
    scratch += [room(layers + 1, n, total) for n in counts[1:]]
    held = sum(math.prod(each.shape) for each in scratch) + window.size + 2 * before.size
    held = 4 * (held + 2 * source.size)
    return pl.pallas_call(
        functools.partial(cycle_kernel, plan),
        out_shape=[jax.ShapeDtypeStruct((layers, rows, cols), jnp.float32)] * 2,
        in_specs=[vmem] * 3,
        out_specs=[vmem] * 2,
        scratch_shapes=scratch,
        compiler_params=pltpu.CompilerParams(vmem_limit_bytes=held + (2 << 20)),
    )(window, before, after)


def solution(mesh):
    return jax.shard_map(
        per_device,
        mesh=mesh,
        in_specs=(P(None, "along", "cross"), P(None, "along", "cross")),
        out_specs=(P(None, "along", "cross"), P(None, "along", "cross")),
        check_vma=False,
    )
```

```python
import functools
import math

import jax
import jax.numpy as jnp
from jax import lax
from jax.experimental import pallas as pl
from jax.experimental.pallas import tpu as pltpu
from jax.sharding import PartitionSpec as P

SWEEPS = 4

along_weight = 0.25
cross_weight = 1.0
vertical_weight = 0.5
relaxation = 0.8

LANES = 128
GUARD = 8
TINY = 1e-30


def rounded_up(count, step):
    return -(-count // step) * step


def shifted(array, axis, by):
    devices = lax.axis_size(axis)
    pairs = [(i, i + by) for i in range(devices) if 0 <= i + by < devices]
    return lax.ppermute(array, axis, pairs)


def beside(block, axis, dim, width):
    size = block.shape[dim]
    before, after = [], []
    hop = 1
    while width > 0:
        take = min(width, size)
        tail = lax.slice_in_dim(block, size - take, size, axis=dim)
        head = lax.slice_in_dim(block, 0, take, axis=dim)
        before.insert(0, shifted(tail, axis, hop))
        after.append(shifted(head, axis, -hop))
        width -= take
        hop += 1
    if len(before) == 1:
        return before[0], after[0]
    return jnp.concatenate(before, dim), jnp.concatenate(after, dim)


class Plan:
    def __init__(self, cross_count, layers, rows, cols):
        self.coarsest = cross_count.bit_length()
        self.layers, self.own_rows, self.own_cols = layers, rows, cols
        self.row_reach = SWEEPS + 2 * self.coarsest
        reach = SWEEPS
        for _ in range(self.coarsest):
            reach = 2 * reach + 1
        self.col_reach = reach + 1
        chunks = 1
        while (chunks * LANES - cols) // 2 < self.col_reach:
            chunks *= 2
        self.chunks = chunks
        self.side_cols = (chunks * LANES - cols) // 2
        self.rows = rounded_up(rows + 2 * self.row_reach, 8)
        self.side_rows = rounded_up(self.row_reach + 1, 8)

    def level_chunks(self, level_no):
        return max(1, self.chunks >> level_no)

    def spread(self, level_no):
        return max(1, (1 << level_no) // self.chunks)


def lane_numbers(rows):
    return lax.broadcasted_iota(jnp.int32, (rows, LANES), 1)


def taken(value, pick):
    return jnp.take_along_axis(value, pick, axis=1, mode="promise_in_bounds")


def window_kernel(plan, own_ref, before_ref, after_ref, out_ref):
    chunks, rows = plan.chunks, plan.own_rows
    lane = lane_numbers(rows)
    picks = [(chunks * lane + chunk) % LANES for chunk in range(chunks)]
    part = lane // (LANES // chunks)

    def layer_step(which, layer_no):
        tiles = []
        for ref in (before_ref, own_ref, after_ref):
            for first in range(0, ref.shape[3], LANES):
                tiles.append(ref[which, layer_no, :, first : first + LANES])
        for chunk in range(chunks):
            value = taken(tiles[0], picks[chunk])
            for tile_no in range(1, chunks):
                other = taken(tiles[tile_no], picks[chunk])
                value = jnp.where(part == tile_no, other, value)
            out_ref[which, layer_no, chunk] = value

    for which in range(2):
        pl.loop(0, plan.layers, unroll=4)(functools.partial(layer_step, which))


def reciprocal(value):
    guess = pl.reciprocal(value, approx=True)
    return guess * (2.0 - value * guess)


def ratio(first, second):
    return first * second * reciprocal(jnp.maximum(first + second, TINY))


def previous_of(cells, spread):
    return [pltpu.roll(cells[-1], spread, 1)] + cells[:-1]


def next_of(cells, spread):
    return cells[1:] + [pltpu.roll(cells[0], LANES - spread, 1)]


def first_of_pair(value, spread):
    lane = lane_numbers(value.shape[0])
    return (lane & spread) == 0


def paired(cells, spread):
    if len(cells) > 1:
        return [cells[2 * k] + cells[2 * k + 1] for k in range(len(cells) // 2)]
    value = cells[0]
    other = jnp.where(
        first_of_pair(value, spread),
        pltpu.roll(value, LANES - spread, 1),
        pltpu.roll(value, spread, 1),
    )
    return [value + other]


def firsts(cells, spread):
    if len(cells) > 1:
        return cells[0::2]
    value = cells[0]
    return [jnp.where(first_of_pair(value, spread), value, pltpu.roll(value, spread, 1))]


def cycle_kernel(plan, own_ref, before_ref, after_ref, pressure_ref, residual_ref, *scratch):
    levels = plan.coarsest + 1
    coarsest = plan.coarsest
    layers, rows = plan.layers, plan.rows
    reach, own_rows = plan.row_reach, plan.own_rows
    scratch = list(scratch)
    upright, centre0, upper0, origin = scratch[:4]
    rest = scratch[4:]
    west, south, factor, inverse, value, forcing = [
        rest[i * levels : (i + 1) * levels] for i in range(6)
    ]
    upper = [upper0] + forcing[1:]
    density = value[0]
    count = [plan.level_chunks(m) for m in range(levels)]
    spread = [plan.spread(m) for m in range(levels)]

    origin[0] = 0
    start0 = origin[0]

    def span(low, high):
        if low % 8 == 0 and high % 8 == 0:
            return pl.ds(low, high - low)
        return pl.ds(start0 + low, high - low)

    side = before_ref.shape[3]

    def assemble(layer_no):
        zeros = jnp.zeros((GUARD, LANES), jnp.float32)
        for c in range(count[0]):
            density[layer_no, c, 0:GUARD] = zeros
            tail = rounded_up(GUARD + reach + own_rows + reach + 1, 8)
            density[layer_no, c, tail - 8 : tail] = zeros
            density[layer_no, c, span(GUARD - 1, GUARD + reach)] = before_ref[
                0, layer_no, c, span(side - reach - 1, side)
            ]
            density[layer_no, c, span(GUARD + reach, GUARD + reach + own_rows)] = own_ref[0, layer_no, c]
            start = GUARD + reach + own_rows
            density[layer_no, c, span(start, start + reach + 1)] = after_ref[
                0, layer_no, c, span(0, reach + 1)
            ]
            forcing[0][layer_no, c, rows - 8 : rows] = zeros
            forcing[0][layer_no, c, span(0, reach)] = before_ref[1, layer_no, c, span(side - reach, side)]
            forcing[0][layer_no, c, span(reach, reach + own_rows)] = own_ref[1, layer_no, c]
            start = reach + own_rows
            forcing[0][layer_no, c, span(start, start + reach)] = after_ref[
                1, layer_no, c, span(0, reach)
            ]

    pl.loop(0, layers, unroll=2)(assemble)

    def faces(layer_no, first):
        wests, souths, uppers = [], [], []
        cells = [density[layer_no, c, GUARD : GUARD + rows] for c in range(count[0])]
        southern = previous_of(cells, 1)
        for c in range(count[0]):
            wests.append(
                2.0
                * along_weight
                * ratio(
                    density[layer_no, c, GUARD : 2 * GUARD + rows],
                    density[layer_no, c, span(GUARD - 1, 2 * GUARD + rows - 1)],
                )
            )
            souths.append(2.0 * cross_weight * ratio(cells[c], southern[c]))
            if first:
                uppers.append(2.0 * vertical_weight * cells[c])
            else:
                uppers.append(
                    2.0
                    * vertical_weight
                    * ratio(cells[c], density[layer_no - 1, c, GUARD : GUARD + rows])
                )
        for m in range(levels):
            if m > 0:
                wests = paired(wests, spread[m - 1])
                souths = [0.5 * each for each in firsts(souths, spread[m - 1])]
                uppers = paired(uppers, spread[m - 1])
            for c in range(count[m]):
                west[m][layer_no, c] = wests[c]
                south[m][layer_no, c] = souths[c]
                upper[m][layer_no, c] = uppers[c]
            south[m][layer_no, count[m]] = pltpu.roll(souths[0], LANES - spread[m], 1)

    faces(0, True)
    pl.loop(1, layers, unroll=3)(lambda layer_no: faces(layer_no, False))
    for m in range(levels):
        for c in range(count[m]):
            upper[m][layers, c] = jnp.zeros((rows, LANES), jnp.float32)

    def clear_guards(layer_no):
        zeros = jnp.zeros((GUARD, LANES), jnp.float32)
        for m in range(levels):
            for c in range(count[m]):
                value[m][layer_no, c, 0:GUARD] = zeros
                value[m][layer_no, c, GUARD + rows : 2 * GUARD + rows] = zeros

    pl.loop(0, layers, unroll=4)(clear_guards)

    def pivots(layer_no, before, first):
        after = []
        for m in range(levels):
            for c in range(count[m]):
                above = upper[m][layer_no, c]
                centre = (
                    west[m][layer_no, c, 0:rows]
                    + west[m][layer_no, c, span(1, rows + 1)]
                    + south[m][layer_no, c]
                    + south[m][layer_no, c + 1]
                    + above
                    + upper[m][layer_no + 1, c]
                )
                if m == 0:
                    centre0[layer_no, c] = centre
                if first:
                    pivot = centre
                else:
                    share = above * before[len(after)]
                    factor[m][layer_no, c] = share
                    pivot = centre - above * share
                inverted = reciprocal(jnp.maximum(pivot, TINY))
                inverse[m][layer_no, c] = relaxation * inverted
                after.append(inverted)
        return tuple(after)

    lax.fori_loop(
        1, layers, lambda z, before: pivots(z, before, False), pivots(0, None, True), unroll=3
    )

    def around(m, layer_no, low, high):
        cells = [value[m][layer_no, c, span(GUARD + low, GUARD + high)] for c in range(count[m])]
        behind, ahead = previous_of(cells, spread[m]), next_of(cells, spread[m])
        out = []
        for c in range(count[m]):
            out.append(
                west[m][layer_no, c, span(low, high)]
                * value[m][layer_no, c, span(GUARD + low - 1, GUARD + high - 1)]
                + west[m][layer_no, c, span(low + 1, high + 1)]
                * value[m][layer_no, c, span(GUARD + low + 1, GUARD + high + 1)]
                + south[m][layer_no, c, span(low, high)] * behind[c]
                + south[m][layer_no, c + 1, span(low, high)] * ahead[c]
            )
        return out

    def solve(m, low, high, right_side, held, offset, store):
        place = slice(offset + low, offset + high)

        def down(layer_no, before):
            now = right_side(layer_no)
            if before is not None:
                now = [
                    now[c] + factor[m][layer_no, c, low:high] * before[c] for c in range(count[m])
                ]
            for c in range(count[m]):
                held[layer_no, c, place] = now[c] * inverse[m][layer_no, c, low:high]
            return tuple(now)

        def up(step, below):
            layer_no = layers - 1 - step
            now = [held[layer_no, c, place] for c in range(count[m])]
            if below is not None:
                now = [
                    now[c] + factor[m][layer_no + 1, c, low:high] * below[c]
                    for c in range(count[m])
                ]
            store(layer_no, now)
            return tuple(now)

        now = None
        for layer_no in range(layers):
            now = down(layer_no, now)
        now = None
        for step in range(layers):
            now = up(step, now)

    def first_sweep(m):
        def right_side(layer_no):
            return [forcing[m][layer_no, c] for c in range(count[m])]

        def store(layer_no, now):
            for c in range(count[m]):
                value[m][layer_no, c, GUARD : GUARD + rows] = now[c]

        solve(m, 0, rows, right_side, value[m], GUARD, store)

    def later_sweep(m, low, high, prolong):
        def right_side(layer_no):
            flow = around(m, layer_no, low, high)
            return [forcing[m][layer_no, c, low:high] + flow[c] for c in range(count[m])]

        def store(layer_no, now):
            for c in range(count[m]):
                place = slice(GUARD + low, GUARD + high)
                new = (1.0 - relaxation) * value[m][layer_no, c, place] + now[c]
                value[m][layer_no, c, place] = new
                if prolong:
                    children = (2 * c, 2 * c + 1) if count[m - 1] > count[m] else (c,)
                    for child in children:
                        value[m - 1][layer_no, child, place] += new

        held = upright if m == coarsest else inverse[m]
        solve(m, low, high, right_side, held, 0, store)

    for m in range(coarsest):
        first_sweep(m)

        def restrict(layer_no, m=m):
            flow = around(m, layer_no, 0, rows)
            remain = [
                (1.0 - relaxation) * forcing[m][layer_no, c] + flow[c] for c in range(count[m])
            ]
            for c, each in enumerate(paired(remain, spread[m])):
                forcing[m + 1][layer_no, c] = each

        pl.loop(0, layers, unroll=layers if count[m] == 1 else 4)(restrict)

    first_sweep(coarsest)
    for sweep_no in range(1, SWEEPS):
        later_sweep(coarsest, 0, rows, sweep_no == SWEEPS - 1)

    for m in range(coarsest - 1, -1, -1):
        low = (reach - m - 1) // 8 * 8
        high = rounded_up(reach + own_rows + m + 1, 8)
        later_sweep(m, low, high, m > 0)

    chunks = count[0]
    lane = lane_numbers(own_rows)

    def in_order(cells, tile_no):
        start = (plan.side_cols + tile_no * LANES) // chunks
        pick = start + lane // chunks
        out = taken(cells[0], pick)
        for c in range(1, chunks):
            out = jnp.where(lane % chunks == c, taken(cells[c], pick), out)
        return out

    def finish(layer_no, top, bottom):
        low, high = reach, reach + own_rows
        own = span(GUARD + low, GUARD + high)
        plain = span(low, high)
        flow = around(0, layer_no, low, high)
        cells, remains = [], []
        for c in range(chunks):
            now = value[0][layer_no, c, own]
            remain = forcing[0][layer_no, c, plain] - centre0[layer_no, c, plain] * now + flow[c]
            if not top:
                remain += upper[0][layer_no, c, plain] * value[0][layer_no - 1, c, own]
            if not bottom:
                remain += upper[0][layer_no + 1, c, plain] * value[0][layer_no + 1, c, own]
            cells.append(now)
            remains.append(remain)
        for tile_no in range(plan.own_cols // LANES):
            columns = slice(tile_no * LANES, (tile_no + 1) * LANES)
            pressure_ref[layer_no, :, columns] = in_order(cells, tile_no)
            residual_ref[layer_no, :, columns] = in_order(remains, tile_no)

    finish(0, True, False)
    pl.loop(1, layers - 1, unroll=2)(lambda layer_no: finish(layer_no, False, False))
    finish(layers - 1, False, True)


def per_device(source, inv_density):
    layers, rows, cols = source.shape
    plan = Plan(lax.axis_size("cross"), layers, rows, cols)
    levels = plan.coarsest + 1
    both = jnp.stack([inv_density, source])
    before, after = beside(both, "cross", 3, plan.side_cols)
    vmem = pl.BlockSpec(memory_space=pltpu.VMEM)
    window = pl.pallas_call(
        functools.partial(window_kernel, plan),
        out_shape=jax.ShapeDtypeStruct((2, layers, plan.chunks, rows, LANES), jnp.float32),
        in_specs=[vmem] * 3,
        out_specs=vmem,
        compiler_params=pltpu.CompilerParams(vmem_limit_bytes=48 << 20),
    )(both, before, after)
    before, after = beside(window, "along", 3, plan.side_rows)

    def room(*shape):
        return pltpu.VMEM(shape + (LANES,), jnp.float32)

    total, high = plan.rows, plan.rows + GUARD
    counts = [plan.level_chunks(m) for m in range(levels)]
    scratch = [
        room(layers, counts[-1], total),
        room(layers, counts[0], total),
        room(layers + 1, counts[0], total),
        pltpu.SMEM((1,), jnp.int32),
    ]
    scratch += [room(layers, n, high) for n in counts]
    scratch += [room(layers, n + 1, total) for n in counts]
    scratch += [room(layers, n, total) for n in counts]
    scratch += [room(layers, n, total) for n in counts]
    scratch += [room(layers, n, high + GUARD) for n in counts]
    scratch += [room(layers, counts[0], total)]
    scratch += [room(layers + 1, n, total) for n in counts[1:]]
    held = sum(math.prod(each.shape) for each in scratch) + window.size + 2 * before.size
    held = 4 * (held + 2 * source.size)
    return pl.pallas_call(
        functools.partial(cycle_kernel, plan),
        out_shape=[jax.ShapeDtypeStruct((layers, rows, cols), jnp.float32)] * 2,
        in_specs=[vmem] * 3,
        out_specs=[vmem] * 2,
        scratch_shapes=scratch,
        compiler_params=pltpu.CompilerParams(vmem_limit_bytes=held + (2 << 20)),
    )(window, before, after)


def solution(mesh):
    return jax.shard_map(
        per_device,
        mesh=mesh,
        in_specs=(P(None, "along", "cross"), P(None, "along", "cross")),
        out_specs=(P(None, "along", "cross"), P(None, "along", "cross")),
        check_vma=False,
    )
```

```python
import functools
import math

import jax
import jax.numpy as jnp
from jax import lax
from jax.experimental import pallas as pl
from jax.experimental.pallas import tpu as pltpu
from jax.sharding import PartitionSpec as P

SWEEPS = 4

along_weight = 0.25
cross_weight = 1.0
vertical_weight = 0.5
relaxation = 0.8

LANES = 128
GUARD = 8
TINY = 1e-30


def rounded_up(count, step):
    return -(-count // step) * step


def shifted(array, axis, by):
    devices = lax.axis_size(axis)
    pairs = [(i, i + by) for i in range(devices) if 0 <= i + by < devices]
    return lax.ppermute(array, axis, pairs)


def runs_of(first, count, widest):
    runs, last = [], first + count
    while first < last:
        run = widest
        while first % run or first + run > last:
            run //= 2
        runs.append((first, run))
        first += run
    return runs


class Packing:
    def __init__(self, layers, widest, parts):
        self.pieces, self.size = [], 0
        for which, first, count in parts:
            for start, run in runs_of(first, count, widest):
                share = widest // run
                self.pieces.append((which, start, run, share, self.size))
                self.size += layers // share

    def place(self, piece, layer_no):
        which, start, run, share, base = piece
        return base + layer_no // share, layer_no % share * run


def hops_of(size, reach):
    hops = []
    while reach > 0:
        hops.append(min(size, reach))
        reach -= hops[-1]
    return hops


class Plan:
    def __init__(self, cross_count, layers, rows, cols):
        self.coarsest = cross_count.bit_length()
        self.layers, self.own_rows, self.own_cols = layers, rows, cols
        self.row_reach = SWEEPS + 2 * self.coarsest
        reach = SWEEPS
        for _ in range(self.coarsest):
            reach = 2 * reach + 1
        self.col_reach = reach + 1
        chunks = 1
        while (chunks * LANES - cols) // 2 < self.col_reach:
            chunks *= 2
        self.chunks = chunks
        self.side_cols = (chunks * LANES - cols) // 2
        self.rows = rounded_up(rows + 2 * self.row_reach, 8)
        self.cross_hops = hops_of(cols, rounded_up(self.col_reach, chunks))
        self.cross_tails = [
            Packing(layers, LANES, [(0, cols - n, n), (1, cols - n, n)]) for n in self.cross_hops
        ]
        self.cross_heads = [Packing(layers, LANES, [(0, 0, n), (1, 0, n)]) for n in self.cross_hops]
        dense, plain = hops_of(rows, self.row_reach + 1), hops_of(rows, self.row_reach)
        plain += [0] * (len(dense) - len(plain))
        self.along_hops = list(zip(dense, plain))
        self.along_tails = [
            Packing(layers, 8, [(0, rows - n, n), (1, rows - k, k)]) for n, k in self.along_hops
        ]
        self.along_heads = [Packing(layers, 8, [(0, 0, n), (1, 0, k)]) for n, k in self.along_hops]

    def level_chunks(self, level_no):
        return max(1, self.chunks >> level_no)

    def spread(self, level_no):
        return max(1, (1 << level_no) // self.chunks)


def lane_numbers(rows):
    return lax.broadcasted_iota(jnp.int32, (rows, LANES), 1)


def taken(value, pick):
    return jnp.take_along_axis(value, pick, axis=1, mode="promise_in_bounds")


def edge_kernel(plan, density_ref, source_ref, *out_refs):
    lane = lane_numbers(plan.own_rows)
    arrays = (density_ref, source_ref)
    for packing, out_ref in zip(plan.cross_tails + plan.cross_heads, out_refs):
        for piece in packing.pieces:
            which, start, run, share, _ = piece
            tile = slice(start // LANES * LANES, start // LANES * LANES + LANES)
            for first in range(0, plan.layers, share):
                value = None
                for layer_no in range(first, first + share):
                    row, offset = packing.place(piece, layer_no)
                    each = arrays[which][layer_no, :, tile]
                    turn = (offset - start) % LANES
                    if turn:
                        each = pltpu.roll(each, turn, 1)
                    value = each if value is None else jnp.where(lane >= offset, each, value)
                out_ref[row] = value


def window_kernel(plan, density_ref, source_ref, *refs):
    hops = len(plan.cross_hops)
    before_refs, after_refs = refs[:hops], refs[hops : 2 * hops]
    out_ref, send_refs = refs[2 * hops], refs[2 * hops + 1 :]
    chunks, rows, cols = plan.chunks, plan.own_rows, plan.own_cols
    lane = lane_numbers(rows)
    own_first = plan.side_cols
    for which, own_ref in enumerate((density_ref, source_ref)):
        for layer_no in range(plan.layers):
            sources = []
            for start in range(0, cols, LANES):
                sources.append(
                    (own_first + start, LANES, own_ref[layer_no, :, start : start + LANES], 0)
                )
            for refs_of, packings, side in (
                (before_refs, plan.cross_tails, -1),
                (after_refs, plan.cross_heads, 1),
            ):
                for hop in range(hops):
                    block = own_first + side * (hop + 1) * cols
                    for piece in packings[hop].pieces:
                        if piece[0] == which:
                            row, offset = packings[hop].place(piece, layer_no)
                            sources.append((block + piece[1], piece[2], refs_of[hop][row], offset))
            for chunk in range(chunks):
                value = jnp.zeros((rows, LANES), jnp.float32)
                for first, count, cells, offset in sources:
                    pick = (chunks * lane + (chunk - first + offset)) & (LANES - 1)
                    inside = (lane >= first // chunks) & (lane < (first + count) // chunks)
                    value = jnp.where(inside, taken(cells, pick), value)
                out_ref[which, layer_no, chunk] = value
                for packing, send_ref in zip(plan.along_tails + plan.along_heads, send_refs):
                    for piece in packing.pieces:
                        if piece[0] == which:
                            start, run = piece[1], piece[2]
                            tile, offset = packing.place(piece, layer_no)
                            send_ref[tile, chunk, offset : offset + run] = value[start : start + run]


def reciprocal(value):
    guess = pl.reciprocal(value, approx=True)
    return guess * (2.0 - value * guess)


def ratio(first, second):
    return first * second * reciprocal(jnp.maximum(first + second, TINY))


def previous_of(cells, spread):
    return [pltpu.roll(cells[-1], spread, 1)] + cells[:-1]


def next_of(cells, spread):
    return cells[1:] + [pltpu.roll(cells[0], LANES - spread, 1)]


def first_of_pair(value, spread):
    lane = lane_numbers(value.shape[0])
    return (lane & spread) == 0


def paired(cells, spread):
    if len(cells) > 1:
        return [cells[2 * k] + cells[2 * k + 1] for k in range(len(cells) // 2)]
    value = cells[0]
    return [value + taken(value, lane_numbers(value.shape[0]) ^ spread)]


def firsts(cells, spread):
    if len(cells) > 1:
        return cells[0::2]
    value = cells[0]
    return [jnp.where(first_of_pair(value, spread), value, pltpu.roll(value, spread, 1))]


def cycle_kernel(plan, own_ref, *refs):
    hops = len(plan.along_hops)
    before_refs, after_refs = refs[:hops], refs[hops : 2 * hops]
    pressure_ref, residual_ref = refs[2 * hops : 2 * hops + 2]
    scratch = refs[2 * hops + 2 :]
    levels = plan.coarsest + 1
    coarsest = plan.coarsest
    layers, rows = plan.layers, plan.rows
    reach, own_rows = plan.row_reach, plan.own_rows
    scratch = list(scratch)
    upright, centre0, upper0, origin = scratch[:4]
    rest = scratch[4:]
    west, south, factor, inverse, value, forcing = [
        rest[i * levels : (i + 1) * levels] for i in range(6)
    ]
    upper = [upper0] + forcing[1:]
    density = value[0]
    count = [plan.level_chunks(m) for m in range(levels)]
    spread = [plan.spread(m) for m in range(levels)]

    origin[0] = 0
    start0 = origin[0]

    def span(low, high):
        if low % 8 == 0 and high % 8 == 0:
            return pl.ds(low, high - low)
        return pl.ds(start0 + low, high - low)

    for layer_no in range(layers):
        zeros = jnp.zeros((GUARD, LANES), jnp.float32)
        tail = rounded_up(GUARD + reach + own_rows + reach + 1, 8)
        for c in range(count[0]):
            density[layer_no, c, 0:GUARD] = zeros
            density[layer_no, c, tail - 8 : tail] = zeros
            forcing[0][layer_no, c, rows - 8 : rows] = zeros
        for which, target, base in ((0, density, GUARD + reach), (1, forcing[0], reach)):
            for c in range(count[0]):
                target[layer_no, c, span(base, base + own_rows)] = own_ref[which, layer_no, c]
            for refs_of, packings, side in (
                (before_refs, plan.along_tails, -1),
                (after_refs, plan.along_heads, 1),
            ):
                for hop in range(hops):
                    block = base + side * (hop + 1) * own_rows
                    for piece in packings[hop].pieces:
                        if piece[0] != which:
                            continue
                        start, run = piece[1], piece[2]
                        tile, offset = packings[hop].place(piece, layer_no)
                        for c in range(count[0]):
                            target[layer_no, c, span(block + start, block + start + run)] = refs_of[
                                hop
                            ][tile, c, span(offset, offset + run)]

    def faces(layer_no, first):
        wests, souths, uppers = [], [], []
        cells = [density[layer_no, c, GUARD : GUARD + rows] for c in range(count[0])]
        southern = previous_of(cells, 1)
        for c in range(count[0]):
            wests.append(
                2.0
                * along_weight
                * ratio(
                    density[layer_no, c, GUARD : 2 * GUARD + rows],
                    density[layer_no, c, span(GUARD - 1, 2 * GUARD + rows - 1)],
                )
            )
            souths.append(2.0 * cross_weight * ratio(cells[c], southern[c]))
            if first:
                uppers.append(2.0 * vertical_weight * cells[c])
            else:
                uppers.append(
                    2.0
                    * vertical_weight
                    * ratio(cells[c], density[layer_no - 1, c, GUARD : GUARD + rows])
                )
        for m in range(levels):
            if m > 0:
                wests = paired(wests, spread[m - 1])
                souths = [0.5 * each for each in firsts(souths, spread[m - 1])]
                uppers = paired(uppers, spread[m - 1])
            for c in range(count[m]):
                west[m][layer_no, c] = wests[c]
                south[m][layer_no, c] = souths[c]
                upper[m][layer_no, c] = uppers[c]
            south[m][layer_no, count[m]] = pltpu.roll(souths[0], LANES - spread[m], 1)

    faces(0, True)
    pl.loop(1, layers, unroll=3)(lambda layer_no: faces(layer_no, False))
    for m in range(levels):
        for c in range(count[m]):
            upper[m][layers, c] = jnp.zeros((rows, LANES), jnp.float32)

    def clear_guards(layer_no):
        zeros = jnp.zeros((GUARD, LANES), jnp.float32)
        for m in range(levels):
            for c in range(count[m]):
                value[m][layer_no, c, 0:GUARD] = zeros
                value[m][layer_no, c, GUARD + rows : 2 * GUARD + rows] = zeros

    pl.loop(0, layers, unroll=4)(clear_guards)

    def pivots(layer_no, before, first):
        after = []
        for m in range(levels):
            for c in range(count[m]):
                above = upper[m][layer_no, c]
                centre = (
                    west[m][layer_no, c, 0:rows]
                    + west[m][layer_no, c, span(1, rows + 1)]
                    + south[m][layer_no, c]
                    + south[m][layer_no, c + 1]
                    + above
                    + upper[m][layer_no + 1, c]
                )
                if m == 0:
                    centre0[layer_no, c] = centre
                if first:
                    pivot = centre
                else:
                    share = above * before[len(after)]
                    factor[m][layer_no, c] = share
                    pivot = centre - above * share
                inverted = reciprocal(jnp.maximum(pivot, TINY))
                inverse[m][layer_no, c] = relaxation * inverted
                after.append(inverted)
        return tuple(after)

    lax.fori_loop(
        1, layers, lambda z, before: pivots(z, before, False), pivots(0, None, True), unroll=3
    )

    def around(m, layer_no, low, high):
        cells = [value[m][layer_no, c, span(GUARD + low, GUARD + high)] for c in range(count[m])]
        behind, ahead = previous_of(cells, spread[m]), next_of(cells, spread[m])
        out = []
        for c in range(count[m]):
            out.append(
                west[m][layer_no, c, span(low, high)]
                * value[m][layer_no, c, span(GUARD + low - 1, GUARD + high - 1)]
                + west[m][layer_no, c, span(low + 1, high + 1)]
                * value[m][layer_no, c, span(GUARD + low + 1, GUARD + high + 1)]
                + south[m][layer_no, c, span(low, high)] * behind[c]
                + south[m][layer_no, c + 1, span(low, high)] * ahead[c]
            )
        return out

    def solve(m, low, high, right_side, held, offset, store):
        place = slice(offset + low, offset + high)

        def down(layer_no, before):
            now = right_side(layer_no)
            if before is not None:
                now = [
                    now[c] + factor[m][layer_no, c, low:high] * before[c] for c in range(count[m])
                ]
            for c in range(count[m]):
                held[layer_no, c, place] = now[c] * inverse[m][layer_no, c, low:high]
            return tuple(now)

        def up(step, below):
            layer_no = layers - 1 - step
            now = [held[layer_no, c, place] for c in range(count[m])]
            if below is not None:
                now = [
                    now[c] + factor[m][layer_no + 1, c, low:high] * below[c]
                    for c in range(count[m])
                ]
            store(layer_no, now)
            return tuple(now)

        now = None
        for layer_no in range(layers):
            now = down(layer_no, now)
        now = None
        for step in range(layers):
            now = up(step, now)

    def first_sweep(m):
        def right_side(layer_no):
            return [forcing[m][layer_no, c] for c in range(count[m])]

        def store(layer_no, now):
            for c in range(count[m]):
                value[m][layer_no, c, GUARD : GUARD + rows] = now[c]

        solve(m, 0, rows, right_side, value[m], GUARD, store)

    def later_sweep(m, low, high, prolong):
        def right_side(layer_no):
            flow = around(m, layer_no, low, high)
            return [forcing[m][layer_no, c, low:high] + flow[c] for c in range(count[m])]

        def store(layer_no, now):
            for c in range(count[m]):
                place = slice(GUARD + low, GUARD + high)
                new = (1.0 - relaxation) * value[m][layer_no, c, place] + now[c]
                value[m][layer_no, c, place] = new
                if prolong:
                    children = (2 * c, 2 * c + 1) if count[m - 1] > count[m] else (c,)
                    for child in children:
                        value[m - 1][layer_no, child, place] += new

        held = upright if m == coarsest else inverse[m]
        solve(m, low, high, right_side, held, 0, store)

    for m in range(coarsest):
        first_sweep(m)

        def restrict(layer_no, m=m):
            flow = around(m, layer_no, 0, rows)
            remain = [
                (1.0 - relaxation) * forcing[m][layer_no, c] + flow[c] for c in range(count[m])
            ]
            for c, each in enumerate(paired(remain, spread[m])):
                forcing[m + 1][layer_no, c] = each

        pl.loop(0, layers, unroll=layers if count[m] == 1 else 4)(restrict)

    first_sweep(coarsest)
    for sweep_no in range(1, SWEEPS):
        later_sweep(coarsest, 0, rows, sweep_no == SWEEPS - 1)

    for m in range(coarsest - 1, -1, -1):
        low = (reach - m - 1) // 8 * 8
        high = rounded_up(reach + own_rows + m + 1, 8)
        later_sweep(m, low, high, m > 0)

    chunks = count[0]
    lane = lane_numbers(own_rows)

    def in_order(cells, tile_no):
        start = (plan.side_cols + tile_no * LANES) // chunks
        pick = start + lane // chunks
        out = taken(cells[0], pick)
        for c in range(1, chunks):
            out = jnp.where(lane % chunks == c, taken(cells[c], pick), out)
        return out

    def finish(layer_no, top, bottom):
        low, high = reach, reach + own_rows
        own = span(GUARD + low, GUARD + high)
        plain = span(low, high)
        flow = around(0, layer_no, low, high)
        cells, remains = [], []
        for c in range(chunks):
            now = value[0][layer_no, c, own]
            remain = forcing[0][layer_no, c, plain] - centre0[layer_no, c, plain] * now + flow[c]
            if not top:
                remain += upper[0][layer_no, c, plain] * value[0][layer_no - 1, c, own]
            if not bottom:
                remain += upper[0][layer_no + 1, c, plain] * value[0][layer_no + 1, c, own]
            cells.append(now)
            remains.append(remain)
        for tile_no in range(plan.own_cols // LANES):
            columns = slice(tile_no * LANES, (tile_no + 1) * LANES)
            pressure_ref[layer_no, :, columns] = in_order(cells, tile_no)
            residual_ref[layer_no, :, columns] = in_order(remains, tile_no)

    finish(0, True, False)
    pl.loop(1, layers - 1, unroll=2)(lambda layer_no: finish(layer_no, False, False))
    finish(layers - 1, False, True)


def per_device(source, inv_density):
    layers, rows, cols = source.shape
    plan = Plan(lax.axis_size("cross"), layers, rows, cols)
    levels = plan.coarsest + 1
    vmem = pl.BlockSpec(memory_space=pltpu.VMEM)

    def exchange(sent, axis):
        hops = len(sent) // 2
        got = [shifted(sent[hop], axis, hop + 1) for hop in range(hops)]
        return got + [shifted(sent[hops + hop], axis, -hop - 1) for hop in range(hops)]

    sent = pl.pallas_call(
        functools.partial(edge_kernel, plan),
        out_shape=[
            jax.ShapeDtypeStruct((each.size, rows, LANES), jnp.float32)
            for each in plan.cross_tails + plan.cross_heads
        ],
        in_specs=[vmem] * 2,
        out_specs=[vmem] * (2 * len(plan.cross_hops)),
        compiler_params=pltpu.CompilerParams(vmem_limit_bytes=16 << 20),
    )(inv_density, source)
    got = exchange(sent, "cross")
    window, *sent = pl.pallas_call(
        functools.partial(window_kernel, plan),
        out_shape=[jax.ShapeDtypeStruct((2, layers, plan.chunks, rows, LANES), jnp.float32)]
        + [
            jax.ShapeDtypeStruct((each.size, plan.chunks, 8, LANES), jnp.float32)
            for each in plan.along_tails + plan.along_heads
        ],
        in_specs=[vmem] * (2 + len(got)),
        out_specs=[vmem] * (1 + 2 * len(plan.along_hops)),
        compiler_params=pltpu.CompilerParams(vmem_limit_bytes=32 << 20),
    )(inv_density, source, *got)
    got = exchange(sent, "along")

    def room(*shape):
        return pltpu.VMEM(shape + (LANES,), jnp.float32)

    total, high = plan.rows, plan.rows + GUARD
    counts = [plan.level_chunks(m) for m in range(levels)]
    scratch = [
        room(layers, counts[-1], total),
        room(layers, counts[0], total),
        room(layers + 1, counts[0], total),
        pltpu.SMEM((1,), jnp.int32),
    ]
    scratch += [room(layers, n, high) for n in counts]
    scratch += [room(layers, n + 1, total) for n in counts]
    scratch += [room(layers, n, total) for n in counts]
    scratch += [room(layers, n, total) for n in counts]
    scratch += [room(layers, n, high + GUARD) for n in counts]
    scratch += [room(layers, counts[0], total)]
    scratch += [room(layers + 1, n, total) for n in counts[1:]]
    held = sum(math.prod(each.shape) for each in scratch) + window.size + sum(each.size for each in got)
    held = 4 * (held + 2 * source.size)
    return pl.pallas_call(
        functools.partial(cycle_kernel, plan),
        out_shape=[jax.ShapeDtypeStruct((layers, rows, cols), jnp.float32)] * 2,
        in_specs=[vmem] * (1 + len(got)),
        out_specs=[vmem] * 2,
        scratch_shapes=scratch,
        compiler_params=pltpu.CompilerParams(vmem_limit_bytes=held + (2 << 20)),
    )(window, *got)


def solution(mesh):
    return jax.shard_map(
        per_device,
        mesh=mesh,
        in_specs=(P(None, "along", "cross"), P(None, "along", "cross")),
        out_specs=(P(None, "along", "cross"), P(None, "along", "cross")),
        check_vma=False,
    )
```

```python
import functools
import math

import jax
import jax.numpy as jnp
from jax import lax
from jax.experimental import pallas as pl
from jax.experimental.pallas import tpu as pltpu
from jax.sharding import PartitionSpec as P

SWEEPS = 4

along_weight = 0.25
cross_weight = 1.0
vertical_weight = 0.5
relaxation = 0.8

LANES = 128
GUARD = 8
TINY = 1e-30


def rounded_up(count, step):
    return -(-count // step) * step


def shifted(array, axis, by):
    devices = lax.axis_size(axis)
    pairs = [(i, i + by) for i in range(devices) if 0 <= i + by < devices]
    return lax.ppermute(array, axis, pairs)


class Packing:
    def __init__(self, layers, chunks, first, count):
        self.first, self.lanes, self.chunks = first, count // chunks, chunks
        self.share = LANES // self.lanes
        self.each = -(-layers * chunks // self.share)
        self.size = 2 * self.each

    def place(self, which, layer_no, chunk):
        item = layer_no * self.chunks + chunk
        return which * self.each + item // self.share, item % self.share * self.lanes


def hops_of(size, reach):
    hops = []
    while reach > 0:
        hops.append(min(size, reach))
        reach -= hops[-1]
    return hops


class Plan:
    def __init__(self, cross_count, layers, rows, cols):
        self.coarsest = cross_count.bit_length()
        self.layers, self.own_rows, self.own_cols = layers, rows, cols
        self.row_reach = SWEEPS + 2 * self.coarsest
        reach = SWEEPS
        for _ in range(self.coarsest):
            reach = 2 * reach + 1
        self.col_reach = reach + 1
        chunks = 1
        while (chunks * LANES - cols) // 2 < self.col_reach:
            chunks *= 2
        self.chunks = chunks
        self.side_cols = (chunks * LANES - cols) // 2
        self.rows = rounded_up(rows + 2 * self.row_reach, 8)
        cross_hops = hops_of(cols, rounded_up(self.col_reach, chunks))
        self.cross_count = len(cross_hops)
        self.cross = [Packing(layers, chunks, cols - n, n) for n in cross_hops]
        self.cross += [Packing(layers, chunks, 0, n) for n in cross_hops]
        self.halo_size = sum(each.size for each in self.cross)
        own_lane, own_lanes = self.side_cols // chunks, cols // chunks
        self.own_lane, self.own_lanes = own_lane, own_lanes
        self.cross_lane = [
            own_lane - hop * own_lanes - self.cross[hop].lanes for hop in range(len(cross_hops))
        ] + [own_lane + (hop + 1) * own_lanes for hop in range(len(cross_hops))]
        self.along_hops = hops_of(rows, rounded_up(self.row_reach + 1, 8))
        self.side_rows = sum(self.along_hops)
        self.lead = rounded_up(max(0, self.along_hops[0] - self.row_reach), 8)

    def level_chunks(self, level_no):
        return max(1, self.chunks >> level_no)

    def spread(self, level_no):
        return max(1, (1 << level_no) // self.chunks)


def lane_numbers(rows):
    return lax.broadcasted_iota(jnp.int32, (rows, LANES), 1)


def taken(value, pick):
    return jnp.take_along_axis(value, pick, axis=1, mode="promise_in_bounds")


def edge_kernel(plan, density_ref, source_ref, both_ref, *refs):
    out_refs, semaphore = refs[:-1], refs[-1]
    copies = [
        pltpu.make_async_copy(ref, both_ref.at[which], semaphore.at[which])
        for which, ref in enumerate((density_ref, source_ref))
    ]
    for copy in copies:
        copy.start()
    for copy in copies:
        copy.wait()
    lane = lane_numbers(plan.own_rows)
    chunks, layers = plan.chunks, plan.layers
    for packing, out_ref in zip(plan.cross, out_refs):
        lanes, share = packing.lanes, packing.share
        for which in range(2):
            for group in range(packing.each):
                items = range(group * share, min(group * share + share, layers * chunks))
                value = None
                for layer_no in sorted({item // chunks for item in items}):
                    low = max(layer_no * chunks - group * share, 0)
                    slot = lane // lanes
                    cell = packing.first + chunks * (lane - slot * lanes)
                    cell = cell + (slot + group * share) % chunks
                    for start in range(0, plan.own_cols, LANES):
                        if start + LANES <= packing.first:
                            continue
                        if start >= packing.first + lanes * chunks:
                            continue
                        each = taken(
                            both_ref[which, layer_no, :, start : start + LANES], cell & (LANES - 1)
                        )
                        if value is None:
                            value = each
                        else:
                            value = jnp.where((slot >= low) & (cell >= start), each, value)
                out_ref[which * packing.each + group] = value


def halo_kernel(plan, *refs):
    base = 0
    for ref in refs[:-1]:
        refs[-1][base : base + ref.shape[0]] = ref[...]
        base += ref.shape[0]


def with_halos(plan, value, which, layer_no, chunk, halo_of):
    lane = lane_numbers(value.shape[0])
    hops = plan.cross_count
    for message, packing in enumerate(plan.cross):
        group, offset = packing.place(which, layer_no, chunk)
        first = plan.cross_lane[message]
        turn = (first - offset) % LANES
        cells = halo_of(message, group)
        if turn:
            cells = pltpu.roll(cells, turn, 1)
        if message < hops:
            inside = lane < first + packing.lanes
        else:
            inside = lane >= first
        value = jnp.where(inside, cells, value)
    return value


def window_kernel(plan, both_ref, *refs):
    hops, halos = len(plan.along_hops), len(plan.cross)
    before_refs, after_refs = refs[:hops], refs[hops : 2 * hops]
    halo_refs, out_ref = refs[2 * hops : 2 * hops + halos], refs[-1]
    chunks, rows, cols = plan.chunks, plan.own_rows, plan.own_cols
    parts = [(both_ref, plan.side_rows, rows)]
    row = plan.side_rows
    for ref in before_refs:
        row -= ref.shape[2]
        parts.append((ref, row, ref.shape[2]))
    row = plan.side_rows + rows
    for ref in after_refs:
        parts.append((ref, row, ref.shape[2]))
        row += ref.shape[2]

    def layer_step(which, layer_no):
        for ref, row, height in parts:
            lane = lane_numbers(height)
            tiles = [ref[which, layer_no, :, i : i + LANES] for i in range(0, cols, LANES)]
            for chunk in range(chunks):
                pick = (chunks * (lane - plan.own_lane) + chunk) & (LANES - 1)
                value = taken(tiles[0], pick)
                for tile_no in range(1, len(tiles)):
                    inside = lane >= plan.own_lane + tile_no * LANES // chunks
                    value = jnp.where(inside, taken(tiles[tile_no], pick), value)
                if ref is both_ref:
                    value = with_halos(
                        plan, value, which, layer_no, chunk, lambda k, group: halo_refs[k][group]
                    )
                out_ref[which, layer_no, chunk, row : row + height] = value

    for which in range(2):
        for layer_no in range(plan.layers):
            layer_step(which, layer_no)


def reciprocal(value):
    guess = pl.reciprocal(value, approx=True)
    return guess * (2.0 - value * guess)


def ratio(first, second):
    return first * second * reciprocal(jnp.maximum(first + second, TINY))


def previous_of(cells, spread):
    return [pltpu.roll(cells[-1], spread, 1)] + cells[:-1]


def next_of(cells, spread):
    return cells[1:] + [pltpu.roll(cells[0], LANES - spread, 1)]


def first_of_pair(value, spread):
    lane = lane_numbers(value.shape[0])
    return (lane & spread) == 0


def paired(cells, spread):
    if len(cells) > 1:
        return [cells[2 * k] + cells[2 * k + 1] for k in range(len(cells) // 2)]
    value = cells[0]
    return [value + taken(value, lane_numbers(value.shape[0]) ^ spread)]


def firsts(cells, spread):
    if len(cells) > 1:
        return cells[0::2]
    value = cells[0]
    return [jnp.where(first_of_pair(value, spread), value, pltpu.roll(value, spread, 1))]


def cycle_kernel(plan, window_ref, *refs):
    hops = len(plan.along_hops)
    before_refs, after_refs = refs[:hops], refs[hops : 2 * hops]
    pressure_ref, residual_ref = refs[2 * hops : 2 * hops + 2]
    scratch = refs[2 * hops + 2 :]
    levels = plan.coarsest + 1
    coarsest = plan.coarsest
    layers, rows = plan.layers, plan.rows
    reach, own_rows = plan.row_reach, plan.own_rows
    scratch = list(scratch)
    upright, upper0, origin = scratch[:3]
    rest = scratch[3:]
    west, south, factor, inverse, value, forcing = [
        rest[i * levels : (i + 1) * levels] for i in range(6)
    ]
    upper = [upper0] + forcing[1:]
    density = value[0]
    count = [plan.level_chunks(m) for m in range(levels)]
    spread = [plan.spread(m) for m in range(levels)]

    origin[0] = 0
    start0 = origin[0]

    def span(low, high):
        if low % 8 == 0 and high % 8 == 0:
            return pl.ds(low, high - low)
        return pl.ds(start0 + low, high - low)

    def forced(m, layer_no, c, low, high):
        base = plan.lead if m == 0 else 0
        return forcing[m][layer_no, c, span(base + low, base + high)]

    starts = {}
    for message, packing in enumerate(plan.cross):
        starts[message] = sum(each.size for each in plan.cross[:message])
    parts = [(None, plan.side_rows, own_rows)]
    row = plan.side_rows
    for ref in before_refs:
        row -= ref.shape[1]
        parts.append((ref, row, ref.shape[1]))
    row = plan.side_rows + own_rows
    for ref in after_refs:
        parts.append((ref, row, ref.shape[1]))
        row += ref.shape[1]
    for which, target, guard in ((0, density, GUARD), (1, forcing[0], plan.lead)):
        for layer_no in range(layers):
            for c in range(count[0]):
                for ref, row, height in parts:
                    first = guard + reach - plan.side_rows + row
                    if which == 1 and (first + height <= guard or first >= guard + rows):
                        continue
                    value_now = window_ref[which, layer_no, c, row : row + height]
                    if ref is not None:
                        value_now = with_halos(
                            plan,
                            value_now,
                            which,
                            layer_no,
                            c,
                            lambda k, group, ref=ref: ref[starts[k] + group],
                        )
                    target[layer_no, c, span(first, first + height)] = value_now

    def faces(layer_no, first):
        wests, souths, uppers = [], [], []
        cells = [density[layer_no, c, GUARD : GUARD + rows] for c in range(count[0])]
        southern = previous_of(cells, 1)
        for c in range(count[0]):
            wests.append(
                2.0
                * along_weight
                * ratio(
                    density[layer_no, c, GUARD : 2 * GUARD + rows],
                    density[layer_no, c, span(GUARD - 1, 2 * GUARD + rows - 1)],
                )
            )
            souths.append(2.0 * cross_weight * ratio(cells[c], southern[c]))
            if first:
                uppers.append(2.0 * vertical_weight * cells[c])
            else:
                uppers.append(
                    2.0
                    * vertical_weight
                    * ratio(cells[c], density[layer_no - 1, c, GUARD : GUARD + rows])
                )
        for m in range(levels):
            if m > 0:
                wests = paired(wests, spread[m - 1])
                souths = [0.5 * each for each in firsts(souths, spread[m - 1])]
                uppers = paired(uppers, spread[m - 1])
            for c in range(count[m]):
                west[m][layer_no, c] = wests[c]
                south[m][layer_no, c] = souths[c]
                upper[m][layer_no, c] = uppers[c]
            south[m][layer_no, count[m]] = pltpu.roll(souths[0], LANES - spread[m], 1)

    faces(0, True)
    pl.loop(1, layers, unroll=3)(lambda layer_no: faces(layer_no, False))
    for m in range(levels):
        for c in range(count[m]):
            upper[m][layers, c] = jnp.zeros((rows, LANES), jnp.float32)

    def clear_guards(layer_no):
        zeros = jnp.zeros((GUARD, LANES), jnp.float32)
        for m in range(levels):
            for c in range(count[m]):
                value[m][layer_no, c, 0:GUARD] = zeros
                value[m][layer_no, c, GUARD + rows : 2 * GUARD + rows] = zeros

    pl.loop(0, layers, unroll=4)(clear_guards)

    def pivots(layer_no, before, first):
        after = []
        for m in range(levels):
            for c in range(count[m]):
                above = upper[m][layer_no, c]
                centre = (
                    west[m][layer_no, c, 0:rows]
                    + west[m][layer_no, c, span(1, rows + 1)]
                    + south[m][layer_no, c]
                    + south[m][layer_no, c + 1]
                    + above
                    + upper[m][layer_no + 1, c]
                )
                if first:
                    pivot = centre
                else:
                    share = above * before[len(after)]
                    factor[m][layer_no, c] = share
                    pivot = centre - above * share
                inverted = reciprocal(jnp.maximum(pivot, TINY))
                inverse[m][layer_no, c] = relaxation * inverted
                after.append(inverted)
        return tuple(after)

    lax.fori_loop(
        1, layers, lambda z, before: pivots(z, before, False), pivots(0, None, True), unroll=3
    )

    def around(m, layer_no, low, high):
        cells = [value[m][layer_no, c, span(GUARD + low, GUARD + high)] for c in range(count[m])]
        behind, ahead = previous_of(cells, spread[m]), next_of(cells, spread[m])
        out = []
        for c in range(count[m]):
            out.append(
                west[m][layer_no, c, span(low, high)]
                * value[m][layer_no, c, span(GUARD + low - 1, GUARD + high - 1)]
                + west[m][layer_no, c, span(low + 1, high + 1)]
                * value[m][layer_no, c, span(GUARD + low + 1, GUARD + high + 1)]
                + south[m][layer_no, c, span(low, high)] * behind[c]
                + south[m][layer_no, c + 1, span(low, high)] * ahead[c]
            )
        return out

    def solve(m, low, high, right_side, held, offset, store):
        place = slice(offset + low, offset + high)

        def down(layer_no, before):
            now = right_side(layer_no)
            if before is not None:
                now = [
                    now[c] + factor[m][layer_no, c, low:high] * before[c] for c in range(count[m])
                ]
            for c in range(count[m]):
                held[layer_no, c, place] = now[c] * inverse[m][layer_no, c, low:high]
            return tuple(now)

        def up(step, below):
            layer_no = layers - 1 - step
            now = [held[layer_no, c, place] for c in range(count[m])]
            if below is not None:
                now = [
                    now[c] + factor[m][layer_no + 1, c, low:high] * below[c]
                    for c in range(count[m])
                ]
            store(layer_no, now)
            return tuple(now)

        now = None
        for layer_no in range(layers):
            now = down(layer_no, now)
        now = None
        for step in range(layers):
            now = up(step, now)

    def first_sweep(m):
        def right_side(layer_no):
            return [forced(m, layer_no, c, 0, rows) for c in range(count[m])]

        def store(layer_no, now):
            for c in range(count[m]):
                value[m][layer_no, c, GUARD : GUARD + rows] = now[c]

        solve(m, 0, rows, right_side, value[m], GUARD, store)

    def later_sweep(m, low, high, prolong):
        def right_side(layer_no):
            flow = around(m, layer_no, low, high)
            return [forced(m, layer_no, c, low, high) + flow[c] for c in range(count[m])]

        def store(layer_no, now):
            for c in range(count[m]):
                place = slice(GUARD + low, GUARD + high)
                new = (1.0 - relaxation) * value[m][layer_no, c, place] + now[c]
                value[m][layer_no, c, place] = new
                if prolong:
                    children = (2 * c, 2 * c + 1) if count[m - 1] > count[m] else (c,)
                    for child in children:
                        value[m - 1][layer_no, child, place] += new

        held = upright if m == coarsest else inverse[m]
        solve(m, low, high, right_side, held, 0, store)

    for m in range(coarsest):
        first_sweep(m)

        def restrict(layer_no, m=m):
            flow = around(m, layer_no, 0, rows)
            remain = [
                (1.0 - relaxation) * forced(m, layer_no, c, 0, rows) + flow[c] for c in range(count[m])
            ]
            for c, each in enumerate(paired(remain, spread[m])):
                forcing[m + 1][layer_no, c] = each

        pl.loop(0, layers, unroll=layers if count[m] == 1 else 4)(restrict)

    first_sweep(coarsest)
    for sweep_no in range(1, SWEEPS):
        later_sweep(coarsest, 0, rows, sweep_no == SWEEPS - 1)

    for m in range(coarsest - 1, -1, -1):
        low = (reach - m - 1) // 8 * 8
        high = rounded_up(reach + own_rows + m + 1, 8)
        later_sweep(m, low, high, m > 0)

    chunks = count[0]
    lane = lane_numbers(own_rows)

    def in_order(cells, tile_no):
        start = (plan.side_cols + tile_no * LANES) // chunks
        pick = start + lane // chunks
        out = taken(cells[0], pick)
        for c in range(1, chunks):
            out = jnp.where(lane % chunks == c, taken(cells[c], pick), out)
        return out

    def finish(layer_no, top, bottom):
        low, high = reach, reach + own_rows
        own = span(GUARD + low, GUARD + high)
        plain = span(low, high)
        flow = around(0, layer_no, low, high)
        cells, remains = [], []
        for c in range(chunks):
            now = value[0][layer_no, c, own]
            centre = (
                west[0][layer_no, c, plain]
                + west[0][layer_no, c, span(low + 1, high + 1)]
                + south[0][layer_no, c, plain]
                + south[0][layer_no, c + 1, plain]
                + upper[0][layer_no, c, plain]
                + upper[0][layer_no + 1, c, plain]
            )
            remain = forced(0, layer_no, c, low, high) - centre * now + flow[c]
            if not top:
                remain += upper[0][layer_no, c, plain] * value[0][layer_no - 1, c, own]
            if not bottom:
                remain += upper[0][layer_no + 1, c, plain] * value[0][layer_no + 1, c, own]
            cells.append(now)
            remains.append(remain)
        for tile_no in range(plan.own_cols // LANES):
            columns = slice(tile_no * LANES, (tile_no + 1) * LANES)
            pressure_ref[layer_no, :, columns] = in_order(cells, tile_no)
            residual_ref[layer_no, :, columns] = in_order(remains, tile_no)

    finish(0, True, False)
    pl.loop(1, layers - 1, unroll=2)(lambda layer_no: finish(layer_no, False, False))
    finish(layers - 1, False, True)


def per_device(source, inv_density):
    layers, rows, cols = source.shape
    plan = Plan(lax.axis_size("cross"), layers, rows, cols)
    levels = plan.coarsest + 1
    vmem = pl.BlockSpec(memory_space=pltpu.VMEM)

    shape = functools.partial(jax.ShapeDtypeStruct, dtype=jnp.float32)
    outside = pl.BlockSpec(memory_space=pltpu.HBM)
    both, *sent = pl.pallas_call(
        functools.partial(edge_kernel, plan),
        out_shape=[shape((2, layers, rows, cols))]
        + [shape((each.size, rows, LANES)) for each in plan.cross],
        in_specs=[outside] * 2,
        out_specs=[vmem] * (1 + len(plan.cross)),
        scratch_shapes=[pltpu.SemaphoreType.DMA((2,))],
        compiler_params=pltpu.CompilerParams(vmem_limit_bytes=16 << 20),
    )(inv_density, source)

    def along(block, dim):
        got = []
        for side in (1, -1):
            for hop, height in enumerate(plan.along_hops):
                first = rows - height if side > 0 else 0
                part = lax.slice_in_dim(block, first, first + height, axis=dim)
                got.append(shifted(part, "along", side * (hop + 1)))
        return got

    hops = plan.cross_count
    halos = [shifted(sent[hop], "cross", hop + 1) for hop in range(hops)]
    halos += [shifted(sent[hops + hop], "cross", -hop - 1) for hop in range(hops)]
    beside = along(both, 2)
    halo = pl.pallas_call(
        functools.partial(halo_kernel, plan),
        out_shape=shape((plan.halo_size, rows, LANES)),
        in_specs=[vmem] * len(halos),
        out_specs=vmem,
        compiler_params=pltpu.CompilerParams(vmem_limit_bytes=16 << 20),
    )(*halos)
    got = along(halo, 1)
    height = rows + 2 * plan.side_rows
    window = pl.pallas_call(
        functools.partial(window_kernel, plan),
        out_shape=shape((2, layers, plan.chunks, height, LANES)),
        in_specs=[vmem] * (1 + len(beside) + len(halos)),
        out_specs=vmem,
        compiler_params=pltpu.CompilerParams(vmem_limit_bytes=32 << 20),
        cost_estimate=pl.CostEstimate(flops=10**7, bytes_accessed=4 << 20, transcendentals=0),
    )(both, *beside, *halos)

    def room(*shape):
        return pltpu.VMEM(shape + (LANES,), jnp.float32)

    total, high = plan.rows, plan.rows + GUARD
    counts = [plan.level_chunks(m) for m in range(levels)]
    scratch = [
        room(layers, counts[-1], total),
        room(layers + 1, counts[0], total),
        pltpu.SMEM((1,), jnp.int32),
    ]
    scratch += [room(layers, n, high) for n in counts]
    scratch += [room(layers, n + 1, total) for n in counts]
    scratch += [room(layers, n, total) for n in counts]
    scratch += [room(layers, n, total) for n in counts]
    scratch += [room(layers, n, high + GUARD) for n in counts]
    scratch += [room(layers, counts[0], total + 2 * plan.lead)]
    scratch += [room(layers + 1, n, total) for n in counts[1:]]
    held = sum(math.prod(each.shape) for each in scratch) + window.size + sum(each.size for each in got)
    held = 4 * (held + 2 * source.size)
    return pl.pallas_call(
        functools.partial(cycle_kernel, plan),
        out_shape=[jax.ShapeDtypeStruct((layers, rows, cols), jnp.float32)] * 2,
        in_specs=[vmem] * (1 + len(got)),
        out_specs=[vmem] * 2,
        scratch_shapes=scratch,
        compiler_params=pltpu.CompilerParams(vmem_limit_bytes=held + (1 << 20)),
    )(window, *got)


def solution(mesh):
    return jax.shard_map(
        per_device,
        mesh=mesh,
        in_specs=(P(None, "along", "cross"), P(None, "along", "cross")),
        out_specs=(P(None, "along", "cross"), P(None, "along", "cross")),
        check_vma=False,
    )
```

```python
import functools
import math

import jax
import jax.numpy as jnp
from jax import lax
from jax.experimental import pallas as pl
from jax.experimental.pallas import tpu as pltpu
from jax.sharding import PartitionSpec as P

SWEEPS = 4

along_weight = 0.25
cross_weight = 1.0
vertical_weight = 0.5
relaxation = 0.8

LANES = 128
GUARD = 8
TINY = 1e-30


def rounded_up(count, step):
    return -(-count // step) * step


def shifted(array, axis, by):
    devices = lax.axis_size(axis)
    pairs = [(i, i + by) for i in range(devices) if 0 <= i + by < devices]
    return lax.ppermute(array, axis, pairs)


def runs_of(first, count):
    runs, last = [], first + count
    while first < last:
        run = 8 if first % 8 == 0 and first + 8 <= last else 4
        runs.append((first, run))
        first += run
    return runs


def hops_of(size, reach):
    hops = []
    while reach > 0:
        hops.append(min(size, reach))
        reach -= hops[-1]
    return hops


class CrossMessage:
    def __init__(self, layers, chunks, first, count):
        self.first, self.lanes, self.chunks = first, count // chunks, chunks
        self.share = LANES // self.lanes
        self.items = layers // 2 * chunks
        self.each = -(-self.items // self.share)
        self.size = 4 * self.each

    def place(self, layer_no, chunk):
        item = layer_no // 2 * self.chunks + chunk
        return item // self.share, item % self.share * self.lanes


class RowMessage:
    def __init__(self, layers, first, count, extra, tiles_of):
        self.parts, self.size = [], 0
        for which in range(2):
            for start, run in runs_of(first, count):
                self.parts.append((which, start, run, self.size))
                self.size += tiles_of(run)
        if extra is not None:
            self.parts.append((0, extra, 1, self.size))
            self.size += tiles_of(1)


class Plan:
    def __init__(self, cross_count, layers, rows, cols):
        self.coarsest = cross_count.bit_length()
        self.layers, self.own_rows, self.own_cols = layers, rows, cols
        self.row_reach = rounded_up(SWEEPS + 2 * self.coarsest, 4)
        reach = SWEEPS
        for _ in range(self.coarsest):
            reach = 2 * reach + 1
        self.col_reach = reach + 1
        chunks = 1
        while (chunks * LANES - cols) // 2 < self.col_reach:
            chunks *= 2
        self.chunks = chunks
        self.side_cols = (chunks * LANES - cols) // 2
        self.rows = rounded_up(rows + 2 * self.row_reach, 8)
        self.own_lane, self.own_lanes = self.side_cols // chunks, cols // chunks
        self.fold = LANES // self.own_lanes
        self.halves = chunks // self.fold
        hops = hops_of(cols, rounded_up(self.col_reach, chunks))
        self.cross_count = len(hops)
        self.cross = [CrossMessage(layers, chunks, cols - n, n) for n in hops]
        self.cross += [CrossMessage(layers, chunks, 0, n) for n in hops]
        self.cross_lane = [
            self.own_lane - hop * self.own_lanes - self.cross[hop].lanes for hop in range(len(hops))
        ] + [self.own_lane + (hop + 1) * self.own_lanes for hop in range(len(hops))]
        counts = hops_of(rows, self.row_reach)
        extra_hop, extra_row = divmod(self.row_reach, rows)
        counts += [0] * (extra_hop + 1 - len(counts))
        self.along_count = len(counts)
        self.along, self.corners, self.along_row = [], [], []
        for side in (-1, 1):
            for hop, n in enumerate(counts):
                first = rows - n if side < 0 else 0
                extra = None
                if hop == extra_hop:
                    extra = rows - 1 - extra_row if side < 0 else extra_row
                self.along.append(
                    RowMessage(layers, first, n, extra, lambda run: layers * run // 8 * self.halves)
                )
                self.corners.append(
                    RowMessage(
                        layers,
                        first,
                        n,
                        None,
                        lambda run: sum(each.each * run // 4 for each in self.cross),
                    )
                )
                self.along_row.append(self.row_reach + side * (hop + 1) * rows)

    def level_chunks(self, level_no):
        return max(1, self.chunks >> level_no)

    def spread(self, level_no):
        return max(1, (1 << level_no) // self.chunks)

    def own_tile(self, part, layer_no, half):
        share = 8 // part[2]
        return part[3] + layer_no // share * self.halves + half

    def corner_tile(self, part, message, parity, group):
        wide = part[2] // 4
        base = sum(each.each for each in self.cross[:message]) * wide
        return part[3] + base + (parity * self.cross[message].each if wide == 2 else 0) + group


def lane_numbers(rows):
    return lax.broadcasted_iota(jnp.int32, (rows, LANES), 1)


def taken(value, pick):
    return jnp.take_along_axis(value, pick, axis=1, mode="promise_in_bounds")


def edge_kernel(plan, both_ref, cells_ref, *out_refs):
    lane = lane_numbers(plan.own_rows)
    chunks, layers, cols = plan.chunks, plan.layers, plan.own_cols
    tiles = range(0, cols, LANES)
    cross_refs, along_refs = out_refs[: len(plan.cross)], out_refs[len(plan.cross) :]
    for message, out_ref in zip(plan.cross, cross_refs):
        lanes, share = message.lanes, message.share
        slot = lane // lanes
        for which in range(2):
            for group in range(message.each):
                low_item = group * share
                cell = message.first + chunks * (lane - slot * lanes)
                cell = cell + ((slot + low_item) & (chunks - 1))
                items = range(low_item, min(low_item + share, message.items))
                for parity in range(2):
                    value = None
                    for pair in sorted({item // chunks for item in items}):
                        low = max(pair * chunks - low_item, 0)
                        for start in tiles:
                            if start + LANES <= message.first:
                                continue
                            if start >= message.first + lanes * chunks:
                                continue
                            each = both_ref[which, 2 * pair + parity, :, start : start + LANES]
                            each = taken(each, cell & (LANES - 1))
                            if value is None:
                                value = each
                            else:
                                value = jnp.where((slot >= low) & (cell >= start), each, value)
                    out_ref[(which * 2 + parity) * message.each + group] = value
    place = (lane - plan.own_lane) & (LANES - 1)
    within = place & (plan.own_lanes - 1)
    for half in range(plan.halves):
        cell = chunks * within + half * plan.fold + place // plan.own_lanes
        pick = cell & (LANES - 1)
        for which in range(2):
            for layer_no in range(layers):
                value = None
                for start in tiles:
                    each = taken(both_ref[which, layer_no, :, start : start + LANES], pick)
                    value = each if value is None else jnp.where(cell >= start, each, value)
                cells_ref[which, layer_no, half] = value
                for message, out_ref in zip(plan.along, along_refs):
                    for part in message.parts:
                        if part[0] == which:
                            start, run = part[1], part[2]
                            low = layer_no % (8 // run) * run
                            tile = plan.own_tile(part, layer_no, half)
                            out_ref[tile, low : low + run] = value[start : start + run]


def corner_kernel(plan, *refs):
    halo_refs, out_refs = refs[: len(plan.cross)], refs[len(plan.cross) :]
    for corner, out_ref in zip([each for each in plan.corners if each.size], out_refs):
        for part in corner.parts:
            which, start, run, _ = part
            for message, halo_ref in enumerate(halo_refs):
                each = plan.cross[message].each
                for parity in range(2):
                    low = parity * 4 if run == 4 else 0
                    for group in range(each):
                        tile = plan.corner_tile(part, message, parity, group)
                        out_ref[tile, low : low + run] = halo_ref[
                            (which * 2 + parity) * each + group, start : start + run
                        ]


def turned(value, by):
    by %= LANES
    return pltpu.roll(value, by, 1) if by else value


def with_halos(plan, value, layer_no, chunk, halo_of):
    lane = lane_numbers(value.shape[0])
    value = turned(value, -(chunk % plan.fold) * plan.own_lanes)
    for message, packed in enumerate(plan.cross):
        group, offset = packed.place(layer_no, chunk)
        first = plan.cross_lane[message]
        cells = turned(halo_of(message, group), first - offset)
        if message < plan.cross_count:
            inside = lane < first + packed.lanes
        else:
            inside = lane >= first
        value = jnp.where(inside, cells, value)
    return value


def reciprocal(value):
    guess = pl.reciprocal(value, approx=True)
    return guess * (2.0 - value * guess)


def ratio(first, second):
    return first * second * reciprocal(jnp.maximum(first + second, TINY))


def first_of_pair(value, spread):
    lane = lane_numbers(value.shape[0])
    return (lane & spread) == 0


def paired(cells, spread):
    if len(cells) > 1:
        return [cells[2 * k] + cells[2 * k + 1] for k in range(len(cells) // 2)]
    value = cells[0]
    return [value + taken(value, lane_numbers(value.shape[0]) ^ spread)]


def firsts(cells, spread):
    if len(cells) > 1:
        return cells[0::2]
    value = cells[0]
    return [jnp.where(first_of_pair(value, spread), value, pltpu.roll(value, spread, 1))]


def cycle_kernel(plan, cells_ref, *refs):
    halos, hops = len(plan.cross), len(plan.along)
    halo_refs, refs = refs[:halos], refs[halos:]
    along_refs, refs = refs[:hops], refs[hops:]
    sent = [each for each in plan.corners if each.size]
    corner_refs, refs = refs[: len(sent)], refs[len(sent) :]
    corner_refs = {id(each): ref for each, ref in zip(sent, corner_refs)}
    pressure_ref, residual_ref = refs[:2]
    upright, upper0, origin = refs[2:5]
    rest = refs[5:]
    levels = plan.coarsest + 1
    coarsest = plan.coarsest
    layers, rows = plan.layers, plan.rows
    reach, own_rows = plan.row_reach, plan.own_rows
    west, south, factor, inverse, value, forcing = [
        rest[i * levels : (i + 1) * levels] for i in range(6)
    ]
    upper = [upper0] + list(forcing[1:])
    density = value[0]
    count = [plan.level_chunks(m) for m in range(levels)]
    spread = [plan.spread(m) for m in range(levels)]

    origin[0] = 0
    start0 = origin[0]

    def span(low, high):
        if low % 8 == 0 and high % 8 == 0:
            return pl.ds(low, high - low)
        return pl.ds(start0 + low, high - low)

    for which, target, guard in ((0, density, GUARD), (1, forcing[0], 0)):
        for c in range(count[0]):
            half = c // plan.fold
            for layer_no in range(layers):
                parity = layer_no % 2
                target[layer_no, c, span(guard + reach, guard + reach + own_rows)] = with_halos(
                    plan,
                    cells_ref[which, layer_no, half],
                    layer_no,
                    c,
                    lambda k, group: halo_refs[k][
                        (which * 2 + parity) * plan.cross[k].each + group
                    ],
                )
            for message, corner, along_ref, row in zip(
                plan.along, plan.corners, along_refs, plan.along_row
            ):
                for index, part in enumerate(message.parts):
                    if part[0] != which:
                        continue
                    first, run = guard + row + part[1], part[2]
                    share = 8 // run
                    for layer_no in range(0, layers, share):
                        now = along_ref[plan.own_tile(part, layer_no, half)]
                        if run == 1:
                            now = turned(now, -(c % plan.fold) * plan.own_lanes)
                        else:
                            now = with_halos(
                                plan,
                                now,
                                layer_no,
                                c,
                                lambda k, group: corner_refs[id(corner)][
                                    plan.corner_tile(corner.parts[index], k, layer_no % 2, group)
                                ],
                            )
                        for i in range(share):
                            target[layer_no + i, c, span(first, first + run)] = now[
                                i * run : (i + 1) * run
                            ]

    def faces(layer_no, first):
        cells = [density[layer_no, c, GUARD : GUARD + rows] for c in range(count[0])]
        souths = []
        for c in range(count[0]):
            behind = cells[c - 1] if c else pltpu.roll(cells[-1], 1, 1)
            souths.append(2.0 * cross_weight * ratio(cells[c], behind))
        for m in range(levels):
            if m > 0:
                souths = [0.5 * each for each in firsts(souths, spread[m - 1])]
            for c in range(count[m]):
                south[m][layer_no, c] = souths[c]
            south[m][layer_no, count[m]] = pltpu.roll(souths[0], LANES - spread[m], 1)
        uppers = []
        for c in range(count[0]):
            if first:
                uppers.append(2.0 * vertical_weight * cells[c])
            else:
                above = density[layer_no - 1, c, GUARD : GUARD + rows]
                uppers.append(2.0 * vertical_weight * ratio(cells[c], above))
        for m in range(levels):
            if m > 0:
                uppers = paired(uppers, spread[m - 1])
            for c in range(count[m]):
                upper[m][layer_no, c] = uppers[c]
        wests = []
        for c in range(count[0]):
            here = density[layer_no, c, GUARD : 2 * GUARD + rows]
            behind = density[layer_no, c, span(GUARD - 1, 2 * GUARD + rows - 1)]
            wests.append(2.0 * along_weight * ratio(here, behind))
        for m in range(levels):
            if m > 0:
                wests = paired(wests, spread[m - 1])
            for c in range(count[m]):
                west[m][layer_no, c] = wests[c]

    faces(0, True)
    pl.loop(1, layers, unroll=3)(lambda layer_no: faces(layer_no, False))
    for m in range(levels):
        for c in range(count[m]):
            upper[m][layers, c] = jnp.zeros((rows, LANES), jnp.float32)

    def clear_guards(layer_no):
        zeros = jnp.zeros((GUARD, LANES), jnp.float32)
        for m in range(levels):
            for c in range(count[m]):
                value[m][layer_no, c, 0:GUARD] = zeros
                value[m][layer_no, c, GUARD + rows : 2 * GUARD + rows] = zeros

    pl.loop(0, layers, unroll=4)(clear_guards)

    def pivots(some, layer_no, before, first):
        after = []
        for m in some:
            for c in range(count[m]):
                above = upper[m][layer_no, c]
                centre = (
                    west[m][layer_no, c, 0:rows]
                    + west[m][layer_no, c, span(1, rows + 1)]
                    + south[m][layer_no, c]
                    + south[m][layer_no, c + 1]
                    + above
                    + upper[m][layer_no + 1, c]
                )
                if first:
                    pivot = centre
                else:
                    share = above * before[len(after)]
                    factor[m][layer_no, c] = share
                    pivot = centre - above * share
                inverted = reciprocal(jnp.maximum(pivot, TINY))
                inverse[m][layer_no, c] = relaxation * inverted
                after.append(inverted)
        return tuple(after)

    for some in (range(1), range(1, levels)):
        lax.fori_loop(
            1,
            layers,
            lambda z, before: pivots(some, z, before, False),
            pivots(some, 0, None, True),
            unroll=3,
        )

    def around(m, layer_no, c, low, high):
        own = span(GUARD + low, GUARD + high)
        last = count[m] - 1
        behind = value[m][layer_no, c - 1 if c else last, own]
        ahead = value[m][layer_no, 0 if c == last else c + 1, own]
        if c == 0:
            behind = pltpu.roll(behind, spread[m], 1)
        if c == last:
            ahead = pltpu.roll(ahead, LANES - spread[m], 1)
        return (
            west[m][layer_no, c, span(low, high)]
            * value[m][layer_no, c, span(GUARD + low - 1, GUARD + high - 1)]
            + west[m][layer_no, c, span(low + 1, high + 1)]
            * value[m][layer_no, c, span(GUARD + low + 1, GUARD + high + 1)]
            + south[m][layer_no, c, span(low, high)] * behind
            + south[m][layer_no, c + 1, span(low, high)] * ahead
        )

    def solve(m, low, high, right_side, held, offset, store):
        place = slice(offset + low, offset + high)
        now = [None] * count[m]
        for layer_no in range(layers):
            for c in range(count[m]):
                each = right_side(layer_no, c)
                if layer_no:
                    each = each + factor[m][layer_no, c, low:high] * now[c]
                now[c] = each
                held[layer_no, c, place] = each * inverse[m][layer_no, c, low:high]
        for layer_no in range(layers - 1, -1, -1):
            for c in range(count[m]):
                each = held[layer_no, c, place]
                if layer_no < layers - 1:
                    each = each + factor[m][layer_no + 1, c, low:high] * now[c]
                now[c] = each
                store(layer_no, c, each)

    def first_sweep(m):
        def store(layer_no, c, now):
            value[m][layer_no, c, GUARD : GUARD + rows] = now

        solve(m, 0, rows, lambda z, c: forcing[m][z, c], value[m], GUARD, store)

    def later_sweep(m, low, high, prolong):
        place = slice(GUARD + low, GUARD + high)

        def right_side(layer_no, c):
            return forcing[m][layer_no, c, low:high] + around(m, layer_no, c, low, high)

        def store(layer_no, c, now):
            new = (1.0 - relaxation) * value[m][layer_no, c, place] + now
            value[m][layer_no, c, place] = new
            if prolong:
                children = (2 * c, 2 * c + 1) if count[m - 1] > count[m] else (c,)
                for child in children:
                    value[m - 1][layer_no, child, place] += new

        held = upright if m == coarsest else inverse[m]
        solve(m, low, high, right_side, held, 0, store)

    for m in range(coarsest):
        first_sweep(m)

        def remain_of(layer_no, c, m=m):
            kept = (1.0 - relaxation) * forcing[m][layer_no, c]
            return kept + around(m, layer_no, c, 0, rows)

        def restrict(layer_no, m=m, remain_of=remain_of):
            for c in range(count[m + 1]):
                if count[m] > 1:
                    both = remain_of(layer_no, 2 * c) + remain_of(layer_no, 2 * c + 1)
                else:
                    (both,) = paired([remain_of(layer_no, c)], spread[m])
                forcing[m + 1][layer_no, c] = both

        pl.loop(0, layers, unroll=layers if count[m] == 1 else 4)(restrict)

    first_sweep(coarsest)
    for sweep_no in range(1, SWEEPS):
        later_sweep(coarsest, 0, rows, sweep_no == SWEEPS - 1)

    for m in range(coarsest - 1, -1, -1):
        low = (reach - m - 1) // 8 * 8
        high = rounded_up(reach + own_rows + m + 1, 8)
        later_sweep(m, low, high, m > 0)

    chunks = count[0]
    lane = lane_numbers(own_rows)

    def in_order(cells, tile_no):
        start = (plan.side_cols + tile_no * LANES) // chunks
        pick = start + lane // chunks
        out = taken(cells[0], pick)
        for c in range(1, chunks):
            out = jnp.where((lane & (chunks - 1)) == c, taken(cells[c], pick), out)
        return out

    def finish(layer_no, top, bottom):
        low, high = reach, reach + own_rows
        own = span(GUARD + low, GUARD + high)
        plain = span(low, high)
        cells, remains = [], []
        for c in range(chunks):
            now = value[0][layer_no, c, own]
            centre = (
                west[0][layer_no, c, plain]
                + west[0][layer_no, c, span(low + 1, high + 1)]
                + south[0][layer_no, c, plain]
                + south[0][layer_no, c + 1, plain]
                + upper[0][layer_no, c, plain]
                + upper[0][layer_no + 1, c, plain]
            )
            remain = (
                forcing[0][layer_no, c, plain] - centre * now + around(0, layer_no, c, low, high)
            )
            if not top:
                remain += upper[0][layer_no, c, plain] * value[0][layer_no - 1, c, own]
            if not bottom:
                remain += upper[0][layer_no + 1, c, plain] * value[0][layer_no + 1, c, own]
            cells.append(now)
            remains.append(remain)
        for tile_no in range(plan.own_cols // LANES):
            columns = slice(tile_no * LANES, (tile_no + 1) * LANES)
            pressure_ref[layer_no, :, columns] = in_order(cells, tile_no)
            residual_ref[layer_no, :, columns] = in_order(remains, tile_no)

    finish(0, True, False)
    pl.loop(1, layers - 1, unroll=2)(lambda layer_no: finish(layer_no, False, False))
    finish(layers - 1, False, True)


def per_device(source, inv_density):
    layers, rows, cols = source.shape
    plan = Plan(lax.axis_size("cross"), layers, rows, cols)
    levels = plan.coarsest + 1
    vmem = pl.BlockSpec(memory_space=pltpu.VMEM)

    shape = functools.partial(jax.ShapeDtypeStruct, dtype=jnp.float32)

    def kernel(body, inputs, outputs):
        return pl.pallas_call(
            functools.partial(body, plan),
            out_shape=outputs,
            in_specs=[vmem] * len(inputs),
            out_specs=[vmem] * len(outputs),
            compiler_params=pltpu.CompilerParams(vmem_limit_bytes=16 << 20),
        )(*inputs)

    def exchanged(sent, axis, hops):
        got = [shifted(sent[hop], axis, hop + 1) for hop in range(hops)]
        return got + [shifted(sent[hops + hop], axis, -hop - 1) for hop in range(len(sent) - hops)]

    cells, *sent = kernel(
        edge_kernel,
        [jnp.stack([inv_density, source])],
        [shape((2, layers, plan.halves, rows, LANES))]
        + [shape((each.size, rows, LANES)) for each in plan.cross]
        + [shape((each.size, 8, LANES)) for each in plan.along],
    )
    halos = exchanged(sent[: len(plan.cross)], "cross", plan.cross_count)
    beside = exchanged(sent[len(plan.cross) :], "along", plan.along_count)
    sizes = [each.size for each in plan.corners if each.size]
    sent = kernel(corner_kernel, halos, [shape((size, 8, LANES)) for size in sizes])
    corners = exchanged(sent, "along", len(sent) // 2)
    inputs = [cells, *halos, *beside, *corners]

    def room(*shape):
        return pltpu.VMEM(shape + (LANES,), jnp.float32)

    total, high = plan.rows, plan.rows + GUARD
    counts = [plan.level_chunks(m) for m in range(levels)]
    scratch = [
        room(layers, counts[-1], total),
        room(layers + 1, counts[0], total),
        pltpu.SMEM((1,), jnp.int32),
    ]
    scratch += [room(layers, n, high) for n in counts]
    scratch += [room(layers, n + 1, total) for n in counts]
    scratch += [room(layers, n, total) for n in counts]
    scratch += [room(layers, n, total) for n in counts]
    scratch += [room(layers, n, high + GUARD) for n in counts]
    scratch += [room(layers, counts[0], total)]
    scratch += [room(layers + 1, n, total) for n in counts[1:]]
    held = sum(math.prod(each.shape) for each in scratch) + sum(each.size for each in inputs)
    held = 4 * (held + 2 * source.size)
    return pl.pallas_call(
        functools.partial(cycle_kernel, plan),
        out_shape=[jax.ShapeDtypeStruct((layers, rows, cols), jnp.float32)] * 2,
        in_specs=[vmem] * len(inputs),
        out_specs=[vmem] * 2,
        scratch_shapes=scratch,
        compiler_params=pltpu.CompilerParams(vmem_limit_bytes=held + (3 << 20)),
    )(*inputs)


def solution(mesh):
    return jax.shard_map(
        per_device,
        mesh=mesh,
        in_specs=(P(None, "along", "cross"), P(None, "along", "cross")),
        out_specs=(P(None, "along", "cross"), P(None, "along", "cross")),
        check_vma=False,
    )
```

```python
import functools
import math

import jax
import jax.numpy as jnp
from jax import lax
from jax.experimental import pallas as pl
from jax.experimental.pallas import tpu as pltpu
from jax.sharding import PartitionSpec as P

SWEEPS = 4

along_weight = 0.25
cross_weight = 1.0
vertical_weight = 0.5
relaxation = 0.8

LANES = 128
GUARD = 8
TINY = 1e-30


def rounded_up(count, step):
    return -(-count // step) * step


def swapped(array, axis, distance, second):
    devices = lax.axis_size(axis)
    pairs = []
    for i in range(devices - distance):
        if i // distance % 2 == second:
            pairs += [(i, i + distance), (i + distance, i)]
    return lax.ppermute(array, axis, pairs)


def is_even(axis, distance):
    return (lax.axis_index(axis) // distance) % 2 == 0


def chosen(condition, first, second):
    return jnp.where(condition, first, second), jnp.where(condition, second, first)


def runs_of(first, count):
    runs, last = [], first + count
    while first < last:
        run = 8 if first % 8 == 0 and first + 8 <= last else 4
        runs.append((first, run))
        first += run
    return sorted(runs, key=lambda each: -each[1])


def hops_of(size, reach):
    hops = []
    while reach > 0:
        hops.append(min(size, reach))
        reach -= hops[-1]
    return hops


class CrossMessage:
    def __init__(self, layers, chunks, first, count):
        self.first, self.lanes, self.chunks = first, count // chunks, chunks
        self.share = LANES // self.lanes
        self.items = layers // 2 * chunks
        self.each = -(-self.items // self.share)
        self.size = 4 * self.each

    def place(self, layer_no, chunk):
        item = layer_no // 2 * self.chunks + chunk
        return item // self.share, item % self.share * self.lanes


class RowMessage:
    def __init__(self, layers, first, count, extra, tiles_of):
        self.parts, self.size = [], 0
        for which in range(2):
            for start, run in runs_of(first, count):
                self.parts.append((which, start, run, self.size))
                self.size += tiles_of(run)
        if extra is not None:
            self.parts.append((0, extra, 1, self.size))
            self.size += tiles_of(1)


class Plan:
    def __init__(self, cross_count, layers, rows, cols):
        self.coarsest = cross_count.bit_length()
        self.layers, self.own_rows, self.own_cols = layers, rows, cols
        self.row_reach = rounded_up(SWEEPS + 2 * self.coarsest, 4)
        reach = SWEEPS
        for _ in range(self.coarsest):
            reach = 2 * reach + 1
        self.col_reach = reach + 1
        chunks = 1
        while (chunks * LANES - cols) // 2 < self.col_reach:
            chunks *= 2
        self.chunks = chunks
        self.side_cols = (chunks * LANES - cols) // 2
        self.rows = rounded_up(rows + 2 * self.row_reach, 8)
        self.own_lane, self.own_lanes = self.side_cols // chunks, cols // chunks
        self.fold = LANES // self.own_lanes
        self.halves = chunks // self.fold
        hops = hops_of(cols, rounded_up(self.col_reach, chunks))
        self.cross_count = len(hops)
        self.cross = [CrossMessage(layers, chunks, cols - n, n) for n in hops]
        self.cross += [CrossMessage(layers, chunks, 0, n) for n in hops]
        self.cross_lane = [
            self.own_lane - hop * self.own_lanes - self.cross[hop].lanes for hop in range(len(hops))
        ] + [self.own_lane + (hop + 1) * self.own_lanes for hop in range(len(hops))]
        counts = hops_of(rows, self.row_reach)
        extra_hop, extra_row = divmod(self.row_reach, rows)
        counts += [0] * (extra_hop + 1 - len(counts))
        self.along_count = len(counts)
        self.along, self.corners, self.along_row = [], [], []
        for side in (-1, 1):
            for hop, n in enumerate(counts):
                first = rows - n if side < 0 else 0
                extra = None
                if hop == extra_hop:
                    extra = rows - 1 - extra_row if side < 0 else extra_row
                self.along.append(
                    RowMessage(layers, first, n, extra, lambda run: layers * run // 8 * self.halves)
                )
                self.corners.append(
                    RowMessage(
                        layers,
                        first,
                        n,
                        None,
                        lambda run: sum(each.each * run // 4 for each in self.cross),
                    )
                )
                self.along_row.append(self.row_reach + side * (hop + 1) * rows)

    def level_chunks(self, level_no):
        return max(1, self.chunks >> level_no)

    def spread(self, level_no):
        return max(1, (1 << level_no) // self.chunks)

    def own_tile(self, part, layer_no, half):
        share = 8 // part[2]
        return part[3] + layer_no // share * self.halves + half

    def corner_tile(self, part, message, parity, group):
        wide = part[2] // 4
        base = sum(each.each for each in self.cross[:message]) * wide
        return part[3] + base + (parity * self.cross[message].each if wide == 2 else 0) + group


def lane_numbers(rows):
    return lax.broadcasted_iota(jnp.int32, (rows, LANES), 1)


def taken(value, pick):
    return jnp.take_along_axis(value, pick, axis=1, mode="promise_in_bounds")


def edge_kernel(plan, both_ref, cells_ref, *out_refs):
    lane = lane_numbers(plan.own_rows)
    chunks, layers, cols = plan.chunks, plan.layers, plan.own_cols
    tiles = range(0, cols, LANES)
    cross_refs, along_refs = out_refs[: len(plan.cross)], out_refs[len(plan.cross) :]
    def packed(message, which, group, parity):
        lanes, share = message.lanes, message.share
        slot = lane // lanes
        low_item = group * share
        cell = message.first + chunks * (lane - slot * lanes)
        cell = cell + ((slot + low_item) & (chunks - 1))
        items = range(low_item, min(low_item + share, message.items))
        value = None
        for pair in sorted({item // chunks for item in items}):
            low = max(pair * chunks - low_item, 0)
            for start in tiles:
                if start + LANES <= message.first or start >= message.first + lanes * chunks:
                    continue
                each = both_ref[which, 2 * pair + parity, :, start : start + LANES]
                each = taken(each, cell & (LANES - 1))
                if value is None:
                    value = each
                else:
                    value = jnp.where((slot >= low) & (cell >= start), each, value)
        return value

    hops = plan.cross_count
    for hop in range(hops):
        even = is_even("cross", hop + 1)
        tail, head = plan.cross[hop], plan.cross[hops + hop]
        for which in range(2):
            for parity in range(2):
                for group in range(tail.each):
                    row = (which * 2 + parity) * tail.each + group
                    cross_refs[2 * hop + 1][row], cross_refs[2 * hop][row] = chosen(
                        even,
                        packed(tail, which, group, parity),
                        packed(head, which, group, parity),
                    )
    hops = plan.along_count
    evens = [is_even("along", hop + 1) for hop in range(hops)]
    place = (lane - plan.own_lane) & (LANES - 1)
    within = place & (plan.own_lanes - 1)
    for half in range(plan.halves):
        cell = chunks * within + half * plan.fold + place // plan.own_lanes
        pick = cell & (LANES - 1)
        for which in range(2):
            for layer_no in range(layers):
                value = None
                for start in tiles:
                    each = taken(both_ref[which, layer_no, :, start : start + LANES], pick)
                    value = each if value is None else jnp.where(cell >= start, each, value)
                cells_ref[which, layer_no, half] = value
                for hop in range(hops):
                    tail, head = plan.along[hop], plan.along[hops + hop]
                    for last, first in zip(tail.parts, head.parts):
                        if last[0] == which:
                            run = last[2]
                            low = layer_no % (8 // run) * run
                            tile = plan.own_tile(last, layer_no, half)
                            one, two = chosen(
                                evens[hop],
                                value[last[1] : last[1] + run],
                                value[first[1] : first[1] + run],
                            )
                            along_refs[2 * hop + 1][tile, low : low + run] = one
                            along_refs[2 * hop][tile, low : low + run] = two


def corner_kernel(plan, *refs):
    hops = plan.cross_count
    got_refs, halo_refs, out_refs = refs[: 2 * hops], refs[2 * hops : 4 * hops], refs[4 * hops :]
    for hop in range(hops):
        even = is_even("cross", hop + 1)
        halo_refs[hops + hop][...], halo_refs[hop][...] = chosen(
            even, got_refs[2 * hop + 1][...], got_refs[2 * hop][...]
        )
    hops = plan.along_count
    for hop in range(hops):
        tail, head = plan.corners[hop], plan.corners[hops + hop]
        if not tail.size:
            continue
        even = is_even("along", hop + 1)
        for last, first in zip(tail.parts, head.parts):
            which, run = last[0], last[2]
            for message, halo_ref in enumerate(halo_refs):
                each = plan.cross[message].each
                for parity in range(2):
                    low = parity * 4 if run == 4 else 0
                    for group in range(each):
                        tile = plan.corner_tile(last, message, parity, group)
                        row = (which * 2 + parity) * each + group
                        one, two = chosen(
                            even,
                            halo_ref[row, last[1] : last[1] + run],
                            halo_ref[row, first[1] : first[1] + run],
                        )
                        out_refs[2 * hop + 1][tile, low : low + run] = one
                        out_refs[2 * hop][tile, low : low + run] = two


def turned(value, by):
    by %= LANES
    return pltpu.roll(value, by, 1) if by else value


def with_halos(plan, value, layer_no, chunk, halo_of):
    lane = lane_numbers(value.shape[0])
    value = turned(value, -(chunk % plan.fold) * plan.own_lanes)
    for message, packed in enumerate(plan.cross):
        group, offset = packed.place(layer_no, chunk)
        first = plan.cross_lane[message]
        cells = turned(halo_of(message, group), first - offset)
        if message < plan.cross_count:
            inside = lane < first + packed.lanes
        else:
            inside = lane >= first
        value = jnp.where(inside, cells, value)
    return value


def reciprocal(value):
    guess = pl.reciprocal(value, approx=True)
    return guess * (2.0 - value * guess)


def ratio(first, second):
    return first * second * reciprocal(jnp.maximum(first + second, TINY))


def first_of_pair(value, spread):
    lane = lane_numbers(value.shape[0])
    return (lane & spread) == 0


def paired(cells, spread):
    if len(cells) > 1:
        return [cells[2 * k] + cells[2 * k + 1] for k in range(len(cells) // 2)]
    value = cells[0]
    return [value + taken(value, lane_numbers(value.shape[0]) ^ spread)]


def firsts(cells, spread):
    if len(cells) > 1:
        return cells[0::2]
    value = cells[0]
    return [jnp.where(first_of_pair(value, spread), value, pltpu.roll(value, spread, 1))]


def cycle_kernel(plan, cells_ref, *refs):
    halos, hops = len(plan.cross), len(plan.along)
    halo_refs, refs = refs[:halos], refs[halos:]
    along_refs, refs = refs[:hops], refs[hops:]
    sent = sum(each.size > 0 for each in plan.corners)
    corner_refs, refs = refs[:sent], refs[sent:]
    pressure_ref, residual_ref = refs[:2]
    upright, upper0, origin = refs[2:5]
    rest = refs[5:]
    levels = plan.coarsest + 1
    coarsest = plan.coarsest
    layers, rows = plan.layers, plan.rows
    reach, own_rows = plan.row_reach, plan.own_rows
    west, south, factor, inverse, value, forcing = [
        rest[i * levels : (i + 1) * levels] for i in range(6)
    ]
    upper = [upper0] + list(forcing[1:])
    density = value[0]
    count = [plan.level_chunks(m) for m in range(levels)]
    spread = [plan.spread(m) for m in range(levels)]

    origin[0] = 0
    start0 = origin[0]

    def span(low, high):
        if low % 8 == 0 and high % 8 == 0:
            return pl.ds(low, high - low)
        return pl.ds(start0 + low, high - low)

    for which, target, guard in ((0, density, GUARD), (1, forcing[0], 0)):
        for c in range(count[0]):
            half = c // plan.fold
            for layer_no in range(layers):
                parity = layer_no % 2
                target[layer_no, c, span(guard + reach, guard + reach + own_rows)] = with_halos(
                    plan,
                    cells_ref[which, layer_no, half],
                    layer_no,
                    c,
                    lambda k, group: halo_refs[k][
                        (which * 2 + parity) * plan.cross[k].each + group
                    ],
                )
            for side, (message, corner, row) in enumerate(
                zip(plan.along, plan.corners, plan.along_row)
            ):
                after, hop = divmod(side, plan.along_count)
                even = is_even("along", hop + 1)

                def got(pair, tile):
                    two, one = pair[2 * hop], pair[2 * hop + 1]
                    return jnp.where(even, one[tile], two[tile]) if after else jnp.where(
                        even, two[tile], one[tile]
                    )

                for index, part in enumerate(message.parts):
                    if part[0] != which:
                        continue
                    first, run = guard + row + part[1], part[2]
                    share = 8 // run
                    for layer_no in range(0, layers, share):
                        now = got(along_refs, plan.own_tile(part, layer_no, half))
                        if run == 1:
                            now = turned(now, -(c % plan.fold) * plan.own_lanes)
                        else:
                            now = with_halos(
                                plan,
                                now,
                                layer_no,
                                c,
                                lambda k, group: got(
                                    corner_refs,
                                    plan.corner_tile(corner.parts[index], k, layer_no % 2, group),
                                ),
                            )
                        for i in range(share):
                            target[layer_no + i, c, span(first, first + run)] = now[
                                i * run : (i + 1) * run
                            ]

    def faces(layer_no, first):
        cells = [density[layer_no, c, GUARD : GUARD + rows] for c in range(count[0])]
        souths = []
        for c in range(count[0]):
            behind = cells[c - 1] if c else pltpu.roll(cells[-1], 1, 1)
            souths.append(2.0 * cross_weight * ratio(cells[c], behind))
        for m in range(levels):
            if m > 0:
                souths = [0.5 * each for each in firsts(souths, spread[m - 1])]
            for c in range(count[m]):
                south[m][layer_no, c] = souths[c]
            south[m][layer_no, count[m]] = pltpu.roll(souths[0], LANES - spread[m], 1)
        uppers = []
        for c in range(count[0]):
            if first:
                uppers.append(2.0 * vertical_weight * cells[c])
            else:
                above = density[layer_no - 1, c, GUARD : GUARD + rows]
                uppers.append(2.0 * vertical_weight * ratio(cells[c], above))
        for m in range(levels):
            if m > 0:
                uppers = paired(uppers, spread[m - 1])
            for c in range(count[m]):
                upper[m][layer_no, c] = uppers[c]
        wests = []
        for c in range(count[0]):
            here = density[layer_no, c, GUARD : 2 * GUARD + rows]
            behind = density[layer_no, c, span(GUARD - 1, 2 * GUARD + rows - 1)]
            wests.append(2.0 * along_weight * ratio(here, behind))
        for m in range(levels):
            if m > 0:
                wests = paired(wests, spread[m - 1])
            for c in range(count[m]):
                west[m][layer_no, c] = wests[c]

    faces(0, True)
    pl.loop(1, layers, unroll=3)(lambda layer_no: faces(layer_no, False))
    for m in range(levels):
        for c in range(count[m]):
            upper[m][layers, c] = jnp.zeros((rows, LANES), jnp.float32)

    def clear_guards(layer_no):
        zeros = jnp.zeros((GUARD, LANES), jnp.float32)
        for m in range(levels):
            for c in range(count[m]):
                value[m][layer_no, c, 0:GUARD] = zeros
                value[m][layer_no, c, GUARD + rows : 2 * GUARD + rows] = zeros

    pl.loop(0, layers, unroll=4)(clear_guards)

    def pivots(some, layer_no, before, first):
        after = []
        for m in some:
            for c in range(count[m]):
                above = upper[m][layer_no, c]
                centre = (
                    west[m][layer_no, c, 0:rows]
                    + west[m][layer_no, c, span(1, rows + 1)]
                    + south[m][layer_no, c]
                    + south[m][layer_no, c + 1]
                    + above
                    + upper[m][layer_no + 1, c]
                )
                if first:
                    pivot = centre
                else:
                    share = above * before[len(after)]
                    factor[m][layer_no, c] = share
                    pivot = centre - above * share
                inverted = reciprocal(jnp.maximum(pivot, TINY))
                inverse[m][layer_no, c] = relaxation * inverted
                after.append(inverted)
        return tuple(after)

    for some in (range(1), range(1, levels)):
        lax.fori_loop(
            1,
            layers,
            lambda z, before: pivots(some, z, before, False),
            pivots(some, 0, None, True),
            unroll=3,
        )

    def around(m, layer_no, c, low, high):
        own = span(GUARD + low, GUARD + high)
        last = count[m] - 1
        behind = value[m][layer_no, c - 1 if c else last, own]
        ahead = value[m][layer_no, 0 if c == last else c + 1, own]
        if c == 0:
            behind = pltpu.roll(behind, spread[m], 1)
        if c == last:
            ahead = pltpu.roll(ahead, LANES - spread[m], 1)
        return (
            west[m][layer_no, c, span(low, high)]
            * value[m][layer_no, c, span(GUARD + low - 1, GUARD + high - 1)]
            + west[m][layer_no, c, span(low + 1, high + 1)]
            * value[m][layer_no, c, span(GUARD + low + 1, GUARD + high + 1)]
            + south[m][layer_no, c, span(low, high)] * behind
            + south[m][layer_no, c + 1, span(low, high)] * ahead
        )

    def solve(m, low, high, right_side, held, offset, store):
        place = slice(offset + low, offset + high)
        now = [None] * count[m]
        for layer_no in range(layers):
            for c in range(count[m]):
                each = right_side(layer_no, c)
                if layer_no:
                    each = each + factor[m][layer_no, c, low:high] * now[c]
                now[c] = each
                held[layer_no, c, place] = each * inverse[m][layer_no, c, low:high]
        for layer_no in range(layers - 1, -1, -1):
            for c in range(count[m]):
                each = held[layer_no, c, place]
                if layer_no < layers - 1:
                    each = each + factor[m][layer_no + 1, c, low:high] * now[c]
                now[c] = each
                store(layer_no, c, each)

    def first_sweep(m):
        def store(layer_no, c, now):
            value[m][layer_no, c, GUARD : GUARD + rows] = now

        solve(m, 0, rows, lambda z, c: forcing[m][z, c], value[m], GUARD, store)

    def later_sweep(m, low, high, prolong):
        place = slice(GUARD + low, GUARD + high)

        def right_side(layer_no, c):
            return forcing[m][layer_no, c, low:high] + around(m, layer_no, c, low, high)

        def store(layer_no, c, now):
            new = (1.0 - relaxation) * value[m][layer_no, c, place] + now
            value[m][layer_no, c, place] = new
            if prolong:
                children = (2 * c, 2 * c + 1) if count[m - 1] > count[m] else (c,)
                for child in children:
                    value[m - 1][layer_no, child, place] += new

        held = upright if m == coarsest else inverse[m]
        solve(m, low, high, right_side, held, 0, store)

    for m in range(coarsest):
        first_sweep(m)

        def remain_of(layer_no, c, m=m):
            kept = (1.0 - relaxation) * forcing[m][layer_no, c]
            return kept + around(m, layer_no, c, 0, rows)

        def restrict(layer_no, m=m, remain_of=remain_of):
            for c in range(count[m + 1]):
                if count[m] > 1:
                    both = remain_of(layer_no, 2 * c) + remain_of(layer_no, 2 * c + 1)
                else:
                    (both,) = paired([remain_of(layer_no, c)], spread[m])
                forcing[m + 1][layer_no, c] = both

        pl.loop(0, layers, unroll=layers if count[m] == 1 else 4)(restrict)

    first_sweep(coarsest)
    for sweep_no in range(1, SWEEPS):
        later_sweep(coarsest, 0, rows, sweep_no == SWEEPS - 1)

    for m in range(coarsest - 1, -1, -1):
        low = (reach - m - 1) // 8 * 8
        high = rounded_up(reach + own_rows + m + 1, 8)
        later_sweep(m, low, high, m > 0)

    chunks = count[0]
    lane = lane_numbers(own_rows)

    def in_order(cells, tile_no):
        start = (plan.side_cols + tile_no * LANES) // chunks
        pick = start + lane // chunks
        out = taken(cells[0], pick)
        for c in range(1, chunks):
            out = jnp.where((lane & (chunks - 1)) == c, taken(cells[c], pick), out)
        return out

    def finish(layer_no, top, bottom):
        low, high = reach, reach + own_rows
        own = span(GUARD + low, GUARD + high)
        plain = span(low, high)
        cells, remains = [], []
        for c in range(chunks):
            now = value[0][layer_no, c, own]
            centre = (
                west[0][layer_no, c, plain]
                + west[0][layer_no, c, span(low + 1, high + 1)]
                + south[0][layer_no, c, plain]
                + south[0][layer_no, c + 1, plain]
                + upper[0][layer_no, c, plain]
                + upper[0][layer_no + 1, c, plain]
            )
            remain = (
                forcing[0][layer_no, c, plain] - centre * now + around(0, layer_no, c, low, high)
            )
            if not top:
                remain += upper[0][layer_no, c, plain] * value[0][layer_no - 1, c, own]
            if not bottom:
                remain += upper[0][layer_no + 1, c, plain] * value[0][layer_no + 1, c, own]
            cells.append(now)
            remains.append(remain)
        for tile_no in range(plan.own_cols // LANES):
            columns = slice(tile_no * LANES, (tile_no + 1) * LANES)
            pressure_ref[layer_no, :, columns] = in_order(cells, tile_no)
            residual_ref[layer_no, :, columns] = in_order(remains, tile_no)

    finish(0, True, False)
    pl.loop(1, layers - 1, unroll=2)(lambda layer_no: finish(layer_no, False, False))
    finish(layers - 1, False, True)


def per_device(source, inv_density):
    layers, rows, cols = source.shape
    plan = Plan(lax.axis_size("cross"), layers, rows, cols)
    levels = plan.coarsest + 1
    vmem = pl.BlockSpec(memory_space=pltpu.VMEM)

    shape = functools.partial(jax.ShapeDtypeStruct, dtype=jnp.float32)

    def kernel(body, inputs, outputs):
        return pl.pallas_call(
            functools.partial(body, plan),
            out_shape=outputs,
            in_specs=[vmem] * len(inputs),
            out_specs=[vmem] * len(outputs),
            compiler_params=pltpu.CompilerParams(vmem_limit_bytes=16 << 20),
        )(*inputs)

    def exchanged(sent, axis):
        return [
            swapped(each, axis, index // 2 + 1, 1 - index % 2) for index, each in enumerate(sent)
        ]

    def pairs_of(messages, *tail):
        half = len(messages) // 2
        return [shape((each.size,) + tail) for each in messages[:half] if each.size for _ in range(2)]

    cross_shapes = pairs_of(plan.cross, rows, LANES)
    halo_shapes = [shape((each.size, rows, LANES)) for each in plan.cross]
    cells, *sent = kernel(
        edge_kernel,
        [jnp.stack([inv_density, source])],
        [shape((2, layers, plan.halves, rows, LANES))]
        + cross_shapes
        + pairs_of(plan.along, 8, LANES),
    )
    halos = exchanged(sent[: len(plan.cross)], "cross")
    beside = exchanged(sent[len(plan.cross) :], "along")
    sent = kernel(corner_kernel, halos, halo_shapes + pairs_of(plan.corners, 8, LANES))
    halos, sent = sent[: len(halos)], sent[len(halos) :]
    corners = exchanged(sent, "along")
    inputs = [cells, *halos, *beside, *corners]

    def room(*shape):
        return pltpu.VMEM(shape + (LANES,), jnp.float32)

    total, high = plan.rows, plan.rows + GUARD
    counts = [plan.level_chunks(m) for m in range(levels)]
    scratch = [
        room(layers, counts[-1], total),
        room(layers + 1, counts[0], total),
        pltpu.SMEM((1,), jnp.int32),
    ]
    scratch += [room(layers, n, high) for n in counts]
    scratch += [room(layers, n + 1, total) for n in counts]
    scratch += [room(layers, n, total) for n in counts]
    scratch += [room(layers, n, total) for n in counts]
    scratch += [room(layers, n, high + GUARD) for n in counts]
    scratch += [room(layers, counts[0], total)]
    scratch += [room(layers + 1, n, total) for n in counts[1:]]
    held = sum(math.prod(each.shape) for each in scratch) + sum(each.size for each in inputs)
    held = 4 * (held + 2 * source.size)
    return pl.pallas_call(
        functools.partial(cycle_kernel, plan),
        out_shape=[jax.ShapeDtypeStruct((layers, rows, cols), jnp.float32)] * 2,
        in_specs=[vmem] * len(inputs),
        out_specs=[vmem] * 2,
        scratch_shapes=scratch,
        compiler_params=pltpu.CompilerParams(vmem_limit_bytes=held + (3 << 20)),
    )(*inputs)


def solution(mesh):
    return jax.shard_map(
        per_device,
        mesh=mesh,
        in_specs=(P(None, "along", "cross"), P(None, "along", "cross")),
        out_specs=(P(None, "along", "cross"), P(None, "along", "cross")),
        check_vma=False,
    )
```

```python
import functools
import math

import jax
import jax.numpy as jnp
from jax import lax
from jax.experimental import pallas as pl
from jax.experimental.pallas import tpu as pltpu
from jax.sharding import PartitionSpec as P

SWEEPS = 4

along_weight = 0.25
cross_weight = 1.0
vertical_weight = 0.5
relaxation = 0.8

LANES = 128
GUARD = 8
TINY = 1e-30


def rounded_up(count, step):
    return -(-count // step) * step


def swapped(array, axis, distance, second):
    devices = lax.axis_size(axis)
    pairs = []
    for i in range(devices - distance):
        if i // distance % 2 == second:
            pairs += [(i, i + distance), (i + distance, i)]
    return lax.ppermute(array, axis, pairs)


def is_even(axis, distance):
    return (lax.axis_index(axis) // distance) % 2 == 0


def chosen(condition, first, second):
    return jnp.where(condition, first, second), jnp.where(condition, second, first)


def runs_of(first, count):
    runs, last = [], first + count
    while first < last:
        run = 8 if first % 8 == 0 and first + 8 <= last else 4
        runs.append((first, run))
        first += run
    return sorted(runs, key=lambda each: -each[1])


def hops_of(size, reach):
    hops = []
    while reach > 0:
        hops.append(min(size, reach))
        reach -= hops[-1]
    return hops


class CrossMessage:
    def __init__(self, layers, chunks, first, count):
        self.first, self.lanes, self.chunks = first, count // chunks, chunks
        self.share = LANES // self.lanes
        self.half = layers // 2 * chunks
        self.each = -(-2 * self.half // self.share)
        self.size = 2 * self.each

    def place(self, which, layer_no, chunk):
        item = which * self.half + layer_no // 2 * self.chunks + chunk
        return item // self.share, item % self.share * self.lanes


class RowMessage:
    def __init__(self, arrays, first, count, extra, tiles_of):
        self.parts, self.size = [], 0
        for which in range(arrays):
            for start, run in runs_of(first, count):
                self.parts.append((which, start, run, self.size))
                self.size += tiles_of(run)
        if extra is not None:
            self.parts.append((0, extra, 1, self.size))
            self.size += tiles_of(1)


class Plan:
    def __init__(self, cross_count, layers, rows, cols):
        self.coarsest = cross_count.bit_length()
        self.layers, self.own_rows, self.own_cols = layers, rows, cols
        self.row_reach = rounded_up(SWEEPS + 2 * self.coarsest, 4)
        reach = SWEEPS
        for _ in range(self.coarsest):
            reach = 2 * reach + 1
        self.col_reach = reach + 1
        chunks = 1
        while (chunks * LANES - cols) // 2 < self.col_reach:
            chunks *= 2
        self.chunks = chunks
        self.side_cols = (chunks * LANES - cols) // 2
        self.rows = rounded_up(rows + 2 * self.row_reach, 8)
        self.own_lane, self.own_lanes = self.side_cols // chunks, cols // chunks
        self.fold = LANES // self.own_lanes
        self.halves = chunks // self.fold
        hops = hops_of(cols, rounded_up(self.col_reach, chunks))
        self.cross_count = len(hops)
        self.cross = [CrossMessage(layers, chunks, cols - n, n) for n in hops]
        self.cross += [CrossMessage(layers, chunks, 0, n) for n in hops]
        self.cross_lane = [
            self.own_lane - hop * self.own_lanes - self.cross[hop].lanes for hop in range(len(hops))
        ] + [self.own_lane + (hop + 1) * self.own_lanes for hop in range(len(hops))]
        counts = hops_of(rows, self.row_reach)
        extra_hop, extra_row = divmod(self.row_reach, rows)
        counts += [0] * (extra_hop + 1 - len(counts))
        self.along_count = len(counts)
        self.along, self.corners, self.along_row = [], [], []
        for side in (-1, 1):
            for hop, n in enumerate(counts):
                first = rows - n if side < 0 else 0
                extra = None
                if hop == extra_hop:
                    extra = rows - 1 - extra_row if side < 0 else extra_row
                self.along.append(
                    RowMessage(2, first, n, extra, lambda run: layers * run // 8 * self.halves)
                )
                self.corners.append(
                    [
                        RowMessage(1, first, n, None, lambda run: each.each * run // 4)
                        for each in self.cross[: self.cross_count]
                    ]
                )
                self.along_row.append(self.row_reach + side * (hop + 1) * rows)

    def level_chunks(self, level_no):
        return max(1, self.chunks >> level_no)

    def spread(self, level_no):
        return max(1, (1 << level_no) // self.chunks)

    def own_tile(self, part, layer_no, half):
        share = 8 // part[2]
        return part[3] + layer_no // share * self.halves + half

    def corner_tile(self, part, cross_hop, parity, group):
        return part[3] + (parity * self.cross[cross_hop].each if part[2] == 8 else 0) + group


def lane_numbers(rows):
    return lax.broadcasted_iota(jnp.int32, (rows, LANES), 1)


def taken(value, pick):
    return jnp.take_along_axis(value, pick, axis=1, mode="promise_in_bounds")


def edge_kernel(plan, both_ref, cells_ref, *out_refs):
    lane = lane_numbers(plan.own_rows)
    chunks, layers, cols = plan.chunks, plan.layers, plan.own_cols
    tiles = range(0, cols, LANES)
    cross_refs, along_refs = out_refs[: len(plan.cross)], out_refs[len(plan.cross) :]
    def packed(message, group, parity):
        lanes, share = message.lanes, message.share
        slot = lane // lanes
        low_item = group * share
        cell = message.first + chunks * (lane - slot * lanes)
        cell = cell + ((slot + low_item) & (chunks - 1))
        items = range(low_item, min(low_item + share, 2 * message.half))
        value = None
        for first in sorted({item // chunks * chunks for item in items}):
            low = max(first - low_item, 0)
            which, pair = first // message.half, first % message.half // chunks
            for start in tiles:
                if start + LANES <= message.first or start >= message.first + lanes * chunks:
                    continue
                each = both_ref[which, 2 * pair + parity, :, start : start + LANES]
                each = taken(each, cell & (LANES - 1))
                if value is None:
                    value = each
                else:
                    value = jnp.where((slot >= low) & (cell >= start), each, value)
        return value

    hops = plan.cross_count
    for hop in range(hops):
        even = is_even("cross", hop + 1)
        tail, head = plan.cross[hop], plan.cross[hops + hop]
        for parity in range(2):
            for group in range(tail.each):
                row = parity * tail.each + group
                cross_refs[2 * hop + 1][row], cross_refs[2 * hop][row] = chosen(
                    even, packed(tail, group, parity), packed(head, group, parity)
                )
    hops = plan.along_count
    evens = [is_even("along", hop + 1) for hop in range(hops)]
    place = (lane - plan.own_lane) & (LANES - 1)
    within = place & (plan.own_lanes - 1)
    for half in range(plan.halves):
        cell = chunks * within + half * plan.fold + place // plan.own_lanes
        pick = cell & (LANES - 1)
        for which in range(2):
            for layer_no in range(layers):
                value = None
                for start in tiles:
                    each = taken(both_ref[which, layer_no, :, start : start + LANES], pick)
                    value = each if value is None else jnp.where(cell >= start, each, value)
                cells_ref[which, layer_no, half] = value
                for hop in range(hops):
                    tail, head = plan.along[hop], plan.along[hops + hop]
                    for last, first in zip(tail.parts, head.parts):
                        if last[0] == which:
                            run = last[2]
                            low = layer_no % (8 // run) * run
                            tile = plan.own_tile(last, layer_no, half)
                            one, two = chosen(
                                evens[hop],
                                value[last[1] : last[1] + run],
                                value[first[1] : first[1] + run],
                            )
                            along_refs[2 * hop + 1][tile, low : low + run] = one
                            along_refs[2 * hop][tile, low : low + run] = two


def corner_kernel(cross_hop, plan, halo_ref, *out_refs):
    each = plan.cross[cross_hop].each
    hops = plan.along_count
    for hop in range(hops):
        tail, head = plan.corners[hop][cross_hop], plan.corners[hops + hop][cross_hop]
        if not tail.size:
            continue
        even = is_even("along", hop + 1)
        for last, first in zip(tail.parts, head.parts):
            run = last[2]
            for parity in range(2):
                low = parity * 4 if run == 4 else 0
                for group in range(each):
                    tile = plan.corner_tile(last, cross_hop, parity, group)
                    row = parity * each + group
                    one, two = chosen(
                        even,
                        halo_ref[row, last[1] : last[1] + run],
                        halo_ref[row, first[1] : first[1] + run],
                    )
                    out_refs[2 * hop + 1][tile, low : low + run] = one
                    out_refs[2 * hop][tile, low : low + run] = two


def turned(value, by):
    by %= LANES
    return pltpu.roll(value, by, 1) if by else value


class Halos:
    def __init__(self, plan):
        self.plan, self.swaps, self.masks = plan, [], {}
        for hop in range(plan.cross_count):
            even = is_even("cross", hop + 1)
            for before in (even, jnp.logical_not(even)):
                low = jnp.where(before, 0, plan.cross_lane[plan.cross_count + hop])
                high = jnp.where(before, plan.cross_lane[hop] + plan.cross[hop].lanes, LANES)
                self.swaps.append((hop, before, low, high))

    def beside(self, value, which, layer_no, chunk, halo_of):
        plan = self.plan
        height = value.shape[0]
        if height not in self.masks:
            lane = lane_numbers(height)
            self.masks[height] = [
                (lane >= low) & (lane < high) for _, _, low, high in self.swaps
            ]
        value = turned(value, -(chunk % plan.fold) * plan.own_lanes)
        for swap, (hop, before, _, _) in enumerate(self.swaps):
            group, offset = plan.cross[hop].place(which, layer_no, chunk)
            by = jnp.where(
                before,
                (plan.cross_lane[hop] - offset) % LANES,
                (plan.cross_lane[plan.cross_count + hop] - offset) % LANES,
            )
            cells = pltpu.roll(halo_of(swap, group), by, 1)
            value = jnp.where(self.masks[height][swap], cells, value)
        return value


def own_kernel(plan, cells_ref, *refs):
    halos = Halos(plan)
    for which in range(2):
        for layer_no in range(plan.layers):
            for chunk in range(plan.chunks):

                def halo_of(swap, group):
                    return refs[swap][layer_no % 2 * plan.cross[swap // 2].each + group]

                refs[-1][which, layer_no, chunk] = halos.beside(
                    cells_ref[which, layer_no, chunk // plan.fold],
                    which,
                    layer_no,
                    chunk,
                    halo_of,
                )


def reciprocal(value):
    guess = pl.reciprocal(value, approx=True)
    return guess * (2.0 - value * guess)


def ratio(first, second):
    return first * second * reciprocal(jnp.maximum(first + second, TINY))


def first_of_pair(value, spread):
    lane = lane_numbers(value.shape[0])
    return (lane & spread) == 0


def paired(cells, spread):
    if len(cells) > 1:
        return [cells[2 * k] + cells[2 * k + 1] for k in range(len(cells) // 2)]
    value = cells[0]
    return [value + taken(value, lane_numbers(value.shape[0]) ^ spread)]


def firsts(cells, spread):
    if len(cells) > 1:
        return cells[0::2]
    value = cells[0]
    return [jnp.where(first_of_pair(value, spread), value, pltpu.roll(value, spread, 1))]


def cycle_kernel(plan, own_ref, *refs):
    hops, swaps = len(plan.along), 2 * plan.cross_count
    along_refs, refs = refs[:hops], refs[hops:]
    sent = 2 * sum(each[0].size > 0 for each in plan.corners[: plan.along_count])
    corner_refs = [refs[i * sent : (i + 1) * sent] for i in range(swaps)]
    refs = refs[swaps * sent :]
    pressure_ref, residual_ref = refs[:2]
    upright, upper0, origin = refs[2:5]
    rest = refs[5:]
    levels = plan.coarsest + 1
    coarsest = plan.coarsest
    layers, rows = plan.layers, plan.rows
    reach, own_rows = plan.row_reach, plan.own_rows
    west, south, factor, inverse, value, forcing = [
        rest[i * levels : (i + 1) * levels] for i in range(6)
    ]
    upper = [upper0] + list(forcing[1:])
    density = value[0]
    count = [plan.level_chunks(m) for m in range(levels)]
    spread = [plan.spread(m) for m in range(levels)]

    origin[0] = 0
    start0 = origin[0]

    def span(low, high):
        if low % 8 == 0 and high % 8 == 0:
            return pl.ds(low, high - low)
        return pl.ds(start0 + low, high - low)

    with_halos = Halos(plan)
    evens = [is_even("along", hop + 1) for hop in range(plan.along_count)]
    for which, target, guard in ((0, density, GUARD), (1, forcing[0], 0)):
        for c in range(count[0]):
            half = c // plan.fold
            for layer_no in range(layers):
                target[layer_no, c, span(guard + reach, guard + reach + own_rows)] = own_ref[
                    which, layer_no, c
                ]
            for side, (message, row) in enumerate(zip(plan.along, plan.along_row)):
                after, hop = divmod(side, plan.along_count)

                def got(pair, tile):
                    two, one = pair[2 * hop], pair[2 * hop + 1]
                    if after:
                        return jnp.where(evens[hop], one[tile], two[tile])
                    return jnp.where(evens[hop], two[tile], one[tile])

                parts = [part for part in message.parts if part[0] == which]
                for index, part in enumerate(parts):
                    first, run = guard + row + part[1], part[2]
                    share = 8 // run
                    for layer_no in range(0, layers, share):
                        now = got(along_refs, plan.own_tile(part, layer_no, half))
                        if run == 1:
                            now = turned(now, -(c % plan.fold) * plan.own_lanes)
                        else:

                            def halo_of(swap, group):
                                corner = plan.corners[side][swap // 2].parts[index]
                                tile = plan.corner_tile(corner, swap // 2, layer_no % 2, group)
                                return got(corner_refs[swap], tile)

                            now = with_halos.beside(now, which, layer_no, c, halo_of)
                        for i in range(share):
                            target[layer_no + i, c, span(first, first + run)] = now[
                                i * run : (i + 1) * run
                            ]

    def faces(layer_no, first):
        cells = [density[layer_no, c, GUARD : GUARD + rows] for c in range(count[0])]
        souths = []
        for c in range(count[0]):
            behind = cells[c - 1] if c else pltpu.roll(cells[-1], 1, 1)
            souths.append(2.0 * cross_weight * ratio(cells[c], behind))
        for m in range(levels):
            if m > 0:
                souths = [0.5 * each for each in firsts(souths, spread[m - 1])]
            for c in range(count[m]):
                south[m][layer_no, c] = souths[c]
            south[m][layer_no, count[m]] = pltpu.roll(souths[0], LANES - spread[m], 1)
        uppers = []
        for c in range(count[0]):
            if first:
                uppers.append(2.0 * vertical_weight * cells[c])
            else:
                above = density[layer_no - 1, c, GUARD : GUARD + rows]
                uppers.append(2.0 * vertical_weight * ratio(cells[c], above))
        for m in range(levels):
            if m > 0:
                uppers = paired(uppers, spread[m - 1])
            for c in range(count[m]):
                upper[m][layer_no, c] = uppers[c]
        wests = []
        for c in range(count[0]):
            here = density[layer_no, c, GUARD : 2 * GUARD + rows]
            behind = density[layer_no, c, span(GUARD - 1, 2 * GUARD + rows - 1)]
            wests.append(2.0 * along_weight * ratio(here, behind))
        for m in range(levels):
            if m > 0:
                wests = paired(wests, spread[m - 1])
            for c in range(count[m]):
                west[m][layer_no, c] = wests[c]

    faces(0, True)
    pl.loop(1, layers, unroll=3)(lambda layer_no: faces(layer_no, False))
    for m in range(levels):
        for c in range(count[m]):
            upper[m][layers, c] = jnp.zeros((rows, LANES), jnp.float32)

    def clear_guards(layer_no):
        zeros = jnp.zeros((GUARD, LANES), jnp.float32)
        for m in range(levels):
            for c in range(count[m]):
                value[m][layer_no, c, 0:GUARD] = zeros
                value[m][layer_no, c, GUARD + rows : 2 * GUARD + rows] = zeros

    pl.loop(0, layers, unroll=4)(clear_guards)

    def pivots(some, layer_no, before, first):
        after = []
        for m in some:
            for c in range(count[m]):
                above = upper[m][layer_no, c]
                centre = (
                    west[m][layer_no, c, 0:rows]
                    + west[m][layer_no, c, span(1, rows + 1)]
                    + south[m][layer_no, c]
                    + south[m][layer_no, c + 1]
                    + above
                    + upper[m][layer_no + 1, c]
                )
                if first:
                    pivot = centre
                else:
                    share = above * before[len(after)]
                    factor[m][layer_no, c] = share
                    pivot = centre - above * share
                inverted = reciprocal(jnp.maximum(pivot, TINY))
                inverse[m][layer_no, c] = relaxation * inverted
                after.append(inverted)
        return tuple(after)

    for some in (range(1), range(1, levels)):
        lax.fori_loop(
            1,
            layers,
            lambda z, before: pivots(some, z, before, False),
            pivots(some, 0, None, True),
            unroll=3,
        )

    def around(m, layer_no, c, low, high):
        own = span(GUARD + low, GUARD + high)
        last = count[m] - 1
        behind = value[m][layer_no, c - 1 if c else last, own]
        ahead = value[m][layer_no, 0 if c == last else c + 1, own]
        if c == 0:
            behind = pltpu.roll(behind, spread[m], 1)
        if c == last:
            ahead = pltpu.roll(ahead, LANES - spread[m], 1)
        return (
            west[m][layer_no, c, span(low, high)]
            * value[m][layer_no, c, span(GUARD + low - 1, GUARD + high - 1)]
            + west[m][layer_no, c, span(low + 1, high + 1)]
            * value[m][layer_no, c, span(GUARD + low + 1, GUARD + high + 1)]
            + south[m][layer_no, c, span(low, high)] * behind
            + south[m][layer_no, c + 1, span(low, high)] * ahead
        )

    def solve(m, low, high, right_side, held, offset, store):
        place = slice(offset + low, offset + high)
        now = [None] * count[m]
        for layer_no in range(layers):
            for c in range(count[m]):
                each = right_side(layer_no, c)
                if layer_no:
                    each = each + factor[m][layer_no, c, low:high] * now[c]
                now[c] = each
                held[layer_no, c, place] = each * inverse[m][layer_no, c, low:high]
        for layer_no in range(layers - 1, -1, -1):
            for c in range(count[m]):
                each = held[layer_no, c, place]
                if layer_no < layers - 1:
                    each = each + factor[m][layer_no + 1, c, low:high] * now[c]
                now[c] = each
                store(layer_no, c, each)

    def first_sweep(m):
        def store(layer_no, c, now):
            value[m][layer_no, c, GUARD : GUARD + rows] = now

        solve(m, 0, rows, lambda z, c: forcing[m][z, c], value[m], GUARD, store)

    def later_sweep(m, low, high, prolong):
        place = slice(GUARD + low, GUARD + high)

        def right_side(layer_no, c):
            return forcing[m][layer_no, c, low:high] + around(m, layer_no, c, low, high)

        def store(layer_no, c, now):
            new = (1.0 - relaxation) * value[m][layer_no, c, place] + now
            value[m][layer_no, c, place] = new
            if prolong:
                children = (2 * c, 2 * c + 1) if count[m - 1] > count[m] else (c,)
                for child in children:
                    value[m - 1][layer_no, child, place] += new

        held = upright if m == coarsest else inverse[m]
        solve(m, low, high, right_side, held, 0, store)

    for m in range(coarsest):
        first_sweep(m)

        def remain_of(layer_no, c, m=m):
            kept = (1.0 - relaxation) * forcing[m][layer_no, c]
            return kept + around(m, layer_no, c, 0, rows)

        def restrict(layer_no, m=m, remain_of=remain_of):
            for c in range(count[m + 1]):
                if count[m] > 1:
                    both = remain_of(layer_no, 2 * c) + remain_of(layer_no, 2 * c + 1)
                else:
                    (both,) = paired([remain_of(layer_no, c)], spread[m])
                forcing[m + 1][layer_no, c] = both

        pl.loop(0, layers, unroll=layers if count[m] == 1 else 4)(restrict)

    first_sweep(coarsest)
    for sweep_no in range(1, SWEEPS):
        later_sweep(coarsest, 0, rows, sweep_no == SWEEPS - 1)

    for m in range(coarsest - 1, -1, -1):
        low = (reach - m - 1) // 8 * 8
        high = rounded_up(reach + own_rows + m + 1, 8)
        later_sweep(m, low, high, m > 0)

    chunks = count[0]
    lane = lane_numbers(own_rows)

    def in_order(cells, tile_no):
        start = (plan.side_cols + tile_no * LANES) // chunks
        pick = start + lane // chunks
        out = taken(cells[0], pick)
        for c in range(1, chunks):
            out = jnp.where((lane & (chunks - 1)) == c, taken(cells[c], pick), out)
        return out

    def finish(layer_no, top, bottom):
        low, high = reach, reach + own_rows
        own = span(GUARD + low, GUARD + high)
        plain = span(low, high)
        cells, remains = [], []
        for c in range(chunks):
            now = value[0][layer_no, c, own]
            centre = (
                west[0][layer_no, c, plain]
                + west[0][layer_no, c, span(low + 1, high + 1)]
                + south[0][layer_no, c, plain]
                + south[0][layer_no, c + 1, plain]
                + upper[0][layer_no, c, plain]
                + upper[0][layer_no + 1, c, plain]
            )
            remain = (
                forcing[0][layer_no, c, plain] - centre * now + around(0, layer_no, c, low, high)
            )
            if not top:
                remain += upper[0][layer_no, c, plain] * value[0][layer_no - 1, c, own]
            if not bottom:
                remain += upper[0][layer_no + 1, c, plain] * value[0][layer_no + 1, c, own]
            cells.append(now)
            remains.append(remain)
        for tile_no in range(plan.own_cols // LANES):
            columns = slice(tile_no * LANES, (tile_no + 1) * LANES)
            pressure_ref[layer_no, :, columns] = in_order(cells, tile_no)
            residual_ref[layer_no, :, columns] = in_order(remains, tile_no)

    finish(0, True, False)
    pl.loop(1, layers - 1, unroll=2)(lambda layer_no: finish(layer_no, False, False))
    finish(layers - 1, False, True)


def per_device(source, inv_density):
    layers, rows, cols = source.shape
    plan = Plan(lax.axis_size("cross"), layers, rows, cols)
    levels = plan.coarsest + 1
    vmem = pl.BlockSpec(memory_space=pltpu.VMEM)

    shape = functools.partial(jax.ShapeDtypeStruct, dtype=jnp.float32)

    def kernel(body, inputs, outputs):
        return pl.pallas_call(
            functools.partial(body, plan),
            out_shape=outputs,
            in_specs=[vmem] * len(inputs),
            out_specs=[vmem] * len(outputs),
            compiler_params=pltpu.CompilerParams(vmem_limit_bytes=16 << 20),
        )(*inputs)

    def exchanged(sent, axis):
        return [
            swapped(each, axis, index // 2 + 1, 1 - index % 2) for index, each in enumerate(sent)
        ]

    def pairs_of(messages, *tail):
        half = len(messages) // 2
        return [shape((each.size,) + tail) for each in messages[:half] if each.size for _ in range(2)]

    cross_shapes = pairs_of(plan.cross, rows, LANES)
    cells, *sent = kernel(
        edge_kernel,
        [jnp.stack([inv_density, source])],
        [shape((2, layers, plan.halves, rows, LANES))]
        + cross_shapes
        + pairs_of(plan.along, 8, LANES),
    )
    halos = exchanged(sent[: len(plan.cross)], "cross")
    beside = exchanged(sent[len(plan.cross) :], "along")
    corners = []
    for swap, halo in enumerate(halos):
        messages = [each[swap // 2] for each in plan.corners]
        sent = kernel(
            functools.partial(corner_kernel, swap // 2), [halo], pairs_of(messages, 8, LANES)
        )
        corners += exchanged(sent, "along")
    (own,) = kernel(
        own_kernel, [cells, *halos], [shape((2, layers, plan.chunks, rows, LANES))]
    )
    inputs = [own, *beside, *corners]

    def room(*shape):
        return pltpu.VMEM(shape + (LANES,), jnp.float32)

    total, high = plan.rows, plan.rows + GUARD
    counts = [plan.level_chunks(m) for m in range(levels)]
    scratch = [
        room(layers, counts[-1], total),
        room(layers + 1, counts[0], total),
        pltpu.SMEM((1,), jnp.int32),
    ]
    scratch += [room(layers, n, high) for n in counts]
    scratch += [room(layers, n + 1, total) for n in counts]
    scratch += [room(layers, n, total) for n in counts]
    scratch += [room(layers, n, total) for n in counts]
    scratch += [room(layers, n, high + GUARD) for n in counts]
    scratch += [room(layers, counts[0], total)]
    scratch += [room(layers + 1, n, total) for n in counts[1:]]
    held = sum(math.prod(each.shape) for each in scratch) + sum(each.size for each in inputs)
    held = 4 * (held + 2 * source.size)
    return pl.pallas_call(
        functools.partial(cycle_kernel, plan),
        out_shape=[jax.ShapeDtypeStruct((layers, rows, cols), jnp.float32)] * 2,
        in_specs=[vmem] * len(inputs),
        out_specs=[vmem] * 2,
        scratch_shapes=scratch,
        compiler_params=pltpu.CompilerParams(vmem_limit_bytes=held + (3 << 20)),
    )(*inputs)


def solution(mesh):
    return jax.shard_map(
        per_device,
        mesh=mesh,
        in_specs=(P(None, "along", "cross"), P(None, "along", "cross")),
        out_specs=(P(None, "along", "cross"), P(None, "along", "cross")),
        check_vma=False,
    )
```

```python
import functools
import math

import jax
import jax.numpy as jnp
from jax import lax
from jax.experimental import pallas as pl
from jax.experimental.pallas import tpu as pltpu
from jax.sharding import PartitionSpec as P

SWEEPS = 4

along_weight = 0.25
cross_weight = 1.0
vertical_weight = 0.5
relaxation = 0.8

LANES = 128
GUARD = 8
TINY = 1e-30


def rounded_up(count, step):
    return -(-count // step) * step


def swapped(array, axis, distance, second):
    devices = lax.axis_size(axis)
    pairs = []
    for i in range(devices - distance):
        if i // distance % 2 == second:
            pairs += [(i, i + distance), (i + distance, i)]
    return lax.ppermute(array, axis, pairs)


def is_even(axis, distance):
    return (lax.axis_index(axis) // distance) % 2 == 0


def chosen(condition, first, second):
    return jnp.where(condition, first, second), jnp.where(condition, second, first)


def runs_of(first, count):
    runs, last = [], first + count
    while first < last:
        run = 8 if first % 8 == 0 and first + 8 <= last else 4
        runs.append((first, run))
        first += run
    return sorted(runs, key=lambda each: -each[1])


def hops_of(size, reach):
    hops = []
    while reach > 0:
        hops.append(min(size, reach))
        reach -= hops[-1]
    return hops


class CrossMessage:
    def __init__(self, layers, chunks, first, count):
        self.first, self.lanes, self.chunks = first, count // chunks, chunks
        self.share = LANES // self.lanes
        self.half = layers // 2 * chunks
        self.each = -(-2 * self.half // self.share)
        self.size = 2 * self.each

    def place(self, which, layer_no, chunk):
        item = which * self.half + layer_no // 2 * self.chunks + chunk
        return item // self.share, item % self.share * self.lanes


class RowMessage:
    def __init__(self, arrays, first, count, extra, tiles_of):
        self.parts, self.size = [], 0
        for which in range(arrays):
            for start, run in runs_of(first, count):
                self.parts.append((which, start, run, self.size))
                self.size += tiles_of(run)
        if extra is not None:
            self.parts.append((0, extra, 1, self.size))
            self.size += tiles_of(1)


class Plan:
    def __init__(self, cross_count, layers, rows, cols):
        self.coarsest = cross_count.bit_length()
        self.layers, self.own_rows, self.own_cols = layers, rows, cols
        self.row_reach = rounded_up(SWEEPS + 2 * self.coarsest, 4)
        reach = SWEEPS
        for _ in range(self.coarsest):
            reach = 2 * reach + 1
        self.col_reach = reach + 1
        chunks = 1
        while (chunks * LANES - cols) // 2 < self.col_reach:
            chunks *= 2
        self.chunks = chunks
        self.side_cols = (chunks * LANES - cols) // 2
        self.rows = rounded_up(rows + 2 * self.row_reach, 8)
        self.own_lane, self.own_lanes = self.side_cols // chunks, cols // chunks
        self.fold = LANES // self.own_lanes
        self.halves = chunks // self.fold
        hops = hops_of(cols, rounded_up(self.col_reach, chunks))
        self.cross_count = len(hops)
        self.cross = [CrossMessage(layers, chunks, cols - n, n) for n in hops]
        self.cross += [CrossMessage(layers, chunks, 0, n) for n in hops]
        self.cross_lane = [
            self.own_lane - hop * self.own_lanes - self.cross[hop].lanes for hop in range(len(hops))
        ] + [self.own_lane + (hop + 1) * self.own_lanes for hop in range(len(hops))]
        counts = hops_of(rows, self.row_reach)
        extra_hop, extra_row = divmod(self.row_reach, rows)
        counts += [0] * (extra_hop + 1 - len(counts))
        self.along_count = len(counts)
        self.along, self.corners, self.along_row = [], [], []
        for side in (-1, 1):
            for hop, n in enumerate(counts):
                first = rows - n if side < 0 else 0
                extra = None
                if hop == extra_hop:
                    extra = rows - 1 - extra_row if side < 0 else extra_row
                self.along.append(
                    RowMessage(2, first, n, extra, lambda run: layers * run // 8 * self.halves)
                )
                self.corners.append(
                    [
                        RowMessage(1, first, n, None, lambda run: each.each * run // 4)
                        for each in self.cross[: self.cross_count]
                    ]
                )
                self.along_row.append(self.row_reach + side * (hop + 1) * rows)

    def level_chunks(self, level_no):
        return max(1, self.chunks >> level_no)

    def spread(self, level_no):
        return max(1, (1 << level_no) // self.chunks)

    def own_tile(self, part, layer_no, half):
        share = 8 // part[2]
        return part[3] + layer_no // share * self.halves + half

    def side_tile(self, side, index, layer_no, chunk):
        parts = self.along[side].parts
        base = sum(self.layers * part[2] // 8 for part in parts[:index])
        return (base + layer_no * parts[index][2] // 8) * self.chunks + chunk

    def side_size(self, side):
        return sum(self.layers * part[2] // 8 for part in self.along[side].parts) * self.chunks

    def corner_tile(self, part, cross_hop, parity, group):
        return part[3] + (parity * self.cross[cross_hop].each if part[2] == 8 else 0) + group


def lane_numbers(rows):
    return lax.broadcasted_iota(jnp.int32, (rows, LANES), 1)


def taken(value, pick):
    return jnp.take_along_axis(value, pick, axis=1, mode="promise_in_bounds")


def edge_kernel(plan, both_ref, *cross_refs):
    lane = lane_numbers(plan.own_rows)
    chunks = plan.chunks
    tiles = range(0, plan.own_cols, LANES)

    def packed(message, group, parity):
        lanes, share = message.lanes, message.share
        slot = lane // lanes
        low_item = group * share
        cell = message.first + chunks * (lane - slot * lanes)
        cell = cell + ((slot + low_item) & (chunks - 1))
        items = range(low_item, min(low_item + share, 2 * message.half))
        value = None
        for first in sorted({item // chunks * chunks for item in items}):
            low = max(first - low_item, 0)
            which, pair = first // message.half, first % message.half // chunks
            for start in tiles:
                if start + LANES <= message.first or start >= message.first + lanes * chunks:
                    continue
                each = both_ref[which, 2 * pair + parity, :, start : start + LANES]
                each = taken(each, cell & (LANES - 1))
                if value is None:
                    value = each
                else:
                    value = jnp.where((slot >= low) & (cell >= start), each, value)
        return value

    hops = plan.cross_count
    for hop in range(hops):
        even = is_even("cross", hop + 1)
        tail, head = plan.cross[hop], plan.cross[hops + hop]
        for parity in range(2):
            for group in range(tail.each):
                row = parity * tail.each + group
                cross_refs[2 * hop + 1][row], cross_refs[2 * hop][row] = chosen(
                    even, packed(tail, group, parity), packed(head, group, parity)
                )


def cells_kernel(plan, both_ref, cells_ref, *along_refs):
    lane = lane_numbers(plan.own_rows)
    chunks, layers = plan.chunks, plan.layers
    tiles = range(0, plan.own_cols, LANES)
    hops = plan.along_count
    evens = [is_even("along", hop + 1) for hop in range(hops)]
    place = (lane - plan.own_lane) & (LANES - 1)
    within = place & (plan.own_lanes - 1)
    for half in range(plan.halves):
        cell = chunks * within + half * plan.fold + place // plan.own_lanes
        pick = cell & (LANES - 1)
        for which in range(2):
            for layer_no in range(layers):
                value = None
                for start in tiles:
                    each = taken(both_ref[which, layer_no, :, start : start + LANES], pick)
                    value = each if value is None else jnp.where(cell >= start, each, value)
                cells_ref[which, layer_no, half] = value
                for hop in range(hops):
                    tail, head = plan.along[hop], plan.along[hops + hop]
                    for last, first in zip(tail.parts, head.parts):
                        if last[0] == which:
                            run = last[2]
                            low = layer_no % (8 // run) * run
                            tile = plan.own_tile(last, layer_no, half)
                            one, two = chosen(
                                evens[hop],
                                value[last[1] : last[1] + run],
                                value[first[1] : first[1] + run],
                            )
                            along_refs[2 * hop + 1][tile, low : low + run] = one
                            along_refs[2 * hop][tile, low : low + run] = two


def corner_kernel(cross_hop, plan, halo_ref, *out_refs):
    each = plan.cross[cross_hop].each
    hops = plan.along_count
    for hop in range(hops):
        tail, head = plan.corners[hop][cross_hop], plan.corners[hops + hop][cross_hop]
        if not tail.size:
            continue
        even = is_even("along", hop + 1)
        for last, first in zip(tail.parts, head.parts):
            run = last[2]
            for parity in range(2):
                low = parity * 4 if run == 4 else 0
                for group in range(each):
                    tile = plan.corner_tile(last, cross_hop, parity, group)
                    row = parity * each + group
                    one, two = chosen(
                        even,
                        halo_ref[row, last[1] : last[1] + run],
                        halo_ref[row, first[1] : first[1] + run],
                    )
                    out_refs[2 * hop + 1][tile, low : low + run] = one
                    out_refs[2 * hop][tile, low : low + run] = two


def turned(value, by):
    by %= LANES
    return pltpu.roll(value, by, 1) if by else value


class Halos:
    def __init__(self, plan):
        self.plan, self.swaps, self.masks = plan, [], {}
        for hop in range(plan.cross_count):
            even = is_even("cross", hop + 1)
            for before in (even, jnp.logical_not(even)):
                low = jnp.where(before, 0, plan.cross_lane[plan.cross_count + hop])
                high = jnp.where(before, plan.cross_lane[hop] + plan.cross[hop].lanes, LANES)
                self.swaps.append((hop, before, low, high))

    def beside(self, value, which, layer_no, chunk, halo_of, swaps):
        plan = self.plan
        height = value.shape[0]
        if height not in self.masks:
            lane = lane_numbers(height)
            self.masks[height] = [
                (lane >= low) & (lane < high) for _, _, low, high in self.swaps
            ]
        for swap in swaps:
            hop, before, _, _ = self.swaps[swap]
            group, offset = plan.cross[hop].place(which, layer_no, chunk)
            by = jnp.where(
                before,
                (plan.cross_lane[hop] - offset) % LANES,
                (plan.cross_lane[plan.cross_count + hop] - offset) % LANES,
            )
            cells = pltpu.roll(halo_of(swap, group), by, 1)
            value = jnp.where(self.masks[height][swap], cells, value)
        return value


def from_swaps(plan, hop, after, pair, tile):
    even = is_even("along", hop + 1)
    two, one = pair[2 * hop], pair[2 * hop + 1]
    return jnp.where(even, one[tile], two[tile]) if after else jnp.where(even, two[tile], one[tile])


def corner_of(plan, side, index, layer_no, corner_refs):
    after, hop = divmod(side, plan.along_count)
    index = [part for part in plan.along[side].parts if part[2] > 1].index(
        plan.along[side].parts[index]
    )

    def halo_of(swap, group):
        parts = plan.corners[side][swap // 2].parts
        tile = plan.corner_tile(parts[index % len(parts)], swap // 2, layer_no % 2, group)
        return from_swaps(plan, hop, after, corner_refs[swap], tile)

    return halo_of


def window_kernel(plan, cells_ref, *refs):
    halos, swaps, hops = Halos(plan), 2 * plan.cross_count, len(plan.along)
    halo_refs, along_refs = refs[:swaps], refs[swaps : swaps + hops]
    corner_refs = refs[swaps + hops : -1 - hops]
    own_ref, side_refs = refs[-1 - hops], refs[-hops:]
    turns = [-(chunk % plan.fold) * plan.own_lanes for chunk in range(plan.chunks)]
    for which in range(2):
        for layer_no in range(plan.layers):
            for chunk in range(plan.chunks):

                def halo_of(swap, group):
                    return halo_refs[swap][layer_no % 2 * plan.cross[swap // 2].each + group]

                value = turned(cells_ref[which, layer_no, chunk // plan.fold], turns[chunk])
                own_ref[which, layer_no, chunk] = halos.beside(
                    value, which, layer_no, chunk, halo_of, range(swaps)
                )
    for side, message in enumerate(plan.along):
        after, hop = divmod(side, plan.along_count)
        for index, part in enumerate(message.parts):
            which, _, run, _ = part
            for layer_no in range(0, plan.layers, 8 // run):
                for chunk in range(plan.chunks):
                    tile = plan.own_tile(part, layer_no, chunk // plan.fold)
                    value = from_swaps(plan, hop, after, along_refs, tile)
                    value = turned(value, turns[chunk])
                    if run > 1:
                        halo_of = corner_of(plan, side, index, layer_no, [corner_refs])
                        value = halos.beside(value, which, layer_no, chunk, halo_of, range(1))
                    side_refs[side][plan.side_tile(side, index, layer_no, chunk)] = value


def reciprocal(value):
    guess = pl.reciprocal(value, approx=True)
    return guess * (2.0 - value * guess)


def ratio(first, second):
    return first * second * reciprocal(jnp.maximum(first + second, TINY))


def first_of_pair(value, spread):
    lane = lane_numbers(value.shape[0])
    return (lane & spread) == 0


def paired(cells, spread):
    if len(cells) > 1:
        return [cells[2 * k] + cells[2 * k + 1] for k in range(len(cells) // 2)]
    value = cells[0]
    return [value + taken(value, lane_numbers(value.shape[0]) ^ spread)]


def firsts(cells, spread):
    if len(cells) > 1:
        return cells[0::2]
    value = cells[0]
    return [jnp.where(first_of_pair(value, spread), value, pltpu.roll(value, spread, 1))]


def cycle_kernel(plan, own_ref, *refs):
    hops, swaps = len(plan.along), 2 * plan.cross_count
    side_refs, refs = refs[:hops], refs[hops:]
    sent = 2 * sum(each[0].size > 0 for each in plan.corners[: plan.along_count])
    corner_refs = [None] + [refs[i * sent : (i + 1) * sent] for i in range(swaps - 1)]
    refs = refs[(swaps - 1) * sent :]
    out_refs, staged = refs[:2], refs[2:4]
    upright, upper0, origin, semaphore = refs[4:8]
    rest = refs[8:]
    levels = plan.coarsest + 1
    coarsest = plan.coarsest
    layers, rows = plan.layers, plan.rows
    reach, own_rows = plan.row_reach, plan.own_rows
    west, south, factor, inverse, value, forcing = [
        rest[i * levels : (i + 1) * levels] for i in range(6)
    ]
    upper = [upper0] + list(forcing[1:])
    density = value[0]
    count = [plan.level_chunks(m) for m in range(levels)]
    spread = [plan.spread(m) for m in range(levels)]

    origin[0] = 0
    start0 = origin[0]

    def span(low, high):
        if low % 8 == 0 and high % 8 == 0:
            return pl.ds(low, high - low)
        return pl.ds(start0 + low, high - low)

    halos = Halos(plan)
    targets = ((density, GUARD), (forcing[0], 0))
    for which, (target, guard) in enumerate(targets):
        for layer_no in range(layers):
            for c in range(count[0]):
                target[layer_no, c, span(guard + reach, guard + reach + own_rows)] = own_ref[
                    which, layer_no, c
                ]
    for side, message in enumerate(plan.along):
        for index, part in enumerate(message.parts):
            which, start, run, _ = part
            target, guard = targets[which]
            first = guard + plan.along_row[side] + start
            share = 8 // run
            for layer_no in range(0, layers, share):
                for c in range(count[0]):
                    now = side_refs[side][plan.side_tile(side, index, layer_no, c)]
                    if run > 1:
                        halo_of = corner_of(plan, side, index, layer_no, corner_refs)
                        now = halos.beside(now, which, layer_no, c, halo_of, range(1, swaps))
                    for i in range(share):
                        target[layer_no + i, c, span(first, first + run)] = now[
                            i * run : (i + 1) * run
                        ]

    def faces(layer_no, first):
        cells = [density[layer_no, c, GUARD : GUARD + rows] for c in range(count[0])]
        souths = []
        for c in range(count[0]):
            behind = cells[c - 1] if c else pltpu.roll(cells[-1], 1, 1)
            souths.append(2.0 * cross_weight * ratio(cells[c], behind))
        for m in range(levels):
            if m > 0:
                souths = [0.5 * each for each in firsts(souths, spread[m - 1])]
            for c in range(count[m]):
                south[m][layer_no, c] = souths[c]
            south[m][layer_no, count[m]] = pltpu.roll(souths[0], LANES - spread[m], 1)
        uppers = []
        for c in range(count[0]):
            if first:
                uppers.append(2.0 * vertical_weight * cells[c])
            else:
                above = density[layer_no - 1, c, GUARD : GUARD + rows]
                uppers.append(2.0 * vertical_weight * ratio(cells[c], above))
        for m in range(levels):
            if m > 0:
                uppers = paired(uppers, spread[m - 1])
            for c in range(count[m]):
                upper[m][layer_no, c] = uppers[c]
        wests = []
        for c in range(count[0]):
            here = density[layer_no, c, GUARD : 2 * GUARD + rows]
            behind = density[layer_no, c, span(GUARD - 1, 2 * GUARD + rows - 1)]
            wests.append(2.0 * along_weight * ratio(here, behind))
        for m in range(levels):
            if m > 0:
                wests = paired(wests, spread[m - 1])
            for c in range(count[m]):
                west[m][layer_no, c] = wests[c]

    faces(0, True)
    pl.loop(1, layers, unroll=3)(lambda layer_no: faces(layer_no, False))
    for m in range(levels):
        for c in range(count[m]):
            upper[m][layers, c] = jnp.zeros((rows, LANES), jnp.float32)

    def pivots(some, layer_no, before, first):
        after = []
        for m in some:
            for c in range(count[m]):
                above = upper[m][layer_no, c]
                centre = (
                    west[m][layer_no, c, 0:rows]
                    + west[m][layer_no, c, span(1, rows + 1)]
                    + south[m][layer_no, c]
                    + south[m][layer_no, c + 1]
                    + above
                    + upper[m][layer_no + 1, c]
                )
                if first:
                    pivot = centre
                else:
                    share = above * before[len(after)]
                    factor[m][layer_no, c] = share
                    pivot = centre - above * share
                inverted = reciprocal(jnp.maximum(pivot, TINY))
                inverse[m][layer_no, c] = relaxation * inverted
                after.append(inverted)
        return tuple(after)

    for some in (range(1), range(1, levels)):
        lax.fori_loop(
            1,
            layers,
            lambda z, before: pivots(some, z, before, False),
            pivots(some, 0, None, True),
            unroll=3,
        )

    def around(m, layer_no, c, low, high):
        own = span(GUARD + low, GUARD + high)
        last = count[m] - 1
        behind = value[m][layer_no, c - 1 if c else last, own]
        ahead = value[m][layer_no, 0 if c == last else c + 1, own]
        if c == 0:
            behind = pltpu.roll(behind, spread[m], 1)
        if c == last:
            ahead = pltpu.roll(ahead, LANES - spread[m], 1)
        return (
            west[m][layer_no, c, span(low, high)]
            * value[m][layer_no, c, span(GUARD + low - 1, GUARD + high - 1)]
            + west[m][layer_no, c, span(low + 1, high + 1)]
            * value[m][layer_no, c, span(GUARD + low + 1, GUARD + high + 1)]
            + south[m][layer_no, c, span(low, high)] * behind
            + south[m][layer_no, c + 1, span(low, high)] * ahead
        )

    def solve(m, low, high, right_side, held, offset, store):
        place = slice(offset + low, offset + high)
        now = [None] * count[m]
        for layer_no in range(layers):
            for c in range(count[m]):
                each = right_side(layer_no, c)
                if layer_no:
                    each = each + factor[m][layer_no, c, low:high] * now[c]
                now[c] = each
                held[layer_no, c, place] = each * inverse[m][layer_no, c, low:high]
        for layer_no in range(layers - 1, -1, -1):
            for c in range(count[m]):
                each = held[layer_no, c, place]
                if layer_no < layers - 1:
                    each = each + factor[m][layer_no + 1, c, low:high] * now[c]
                now[c] = each
                store(layer_no, c, each)

    def first_sweep(m):
        def store(layer_no, c, now):
            value[m][layer_no, c, GUARD : GUARD + rows] = now

        solve(m, 0, rows, lambda z, c: forcing[m][z, c], value[m], GUARD, store)

    def later_sweep(m, low, high, prolong):
        place = slice(GUARD + low, GUARD + high)

        def right_side(layer_no, c):
            return forcing[m][layer_no, c, low:high] + around(m, layer_no, c, low, high)

        def store(layer_no, c, now):
            new = (1.0 - relaxation) * value[m][layer_no, c, place] + now
            value[m][layer_no, c, place] = new
            if prolong:
                children = (2 * c, 2 * c + 1) if count[m - 1] > count[m] else (c,)
                for child in children:
                    value[m - 1][layer_no, child, place] += new

        held = upright if m == coarsest else inverse[m]
        solve(m, low, high, right_side, held, 0, store)

    for m in range(coarsest):
        first_sweep(m)

        def remain_of(layer_no, c, m=m):
            kept = (1.0 - relaxation) * forcing[m][layer_no, c]
            return kept + around(m, layer_no, c, 0, rows)

        def restrict(layer_no, m=m, remain_of=remain_of):
            for c in range(count[m + 1]):
                if count[m] > 1:
                    both = remain_of(layer_no, 2 * c) + remain_of(layer_no, 2 * c + 1)
                else:
                    (both,) = paired([remain_of(layer_no, c)], spread[m])
                forcing[m + 1][layer_no, c] = both

        pl.loop(0, layers, unroll=layers if count[m] == 1 else 4)(restrict)

    first_sweep(coarsest)
    for sweep_no in range(1, SWEEPS):
        later_sweep(coarsest, 0, rows, sweep_no == SWEEPS - 1)

    for m in range(coarsest - 1, -1, -1):
        low = (reach - m - 1) // 8 * 8
        high = rounded_up(reach + own_rows + m + 1, 8)
        later_sweep(m, low, high, m > 0)

    chunks = count[0]
    lane = lane_numbers(own_rows)

    lanes = LANES // chunks
    back = (lane & (chunks - 1)) * lanes + lane // chunks

    def in_order(cells, tile_no):
        start = (plan.side_cols + tile_no * LANES) // chunks
        out = turned(cells[0], -start)
        for c in range(1, chunks):
            out = jnp.where(lane >= c * lanes, turned(cells[c], c * lanes - start), out)
        return taken(out, back)

    def finish(layer_no, top, bottom):
        low, high = reach, reach + own_rows
        own = span(GUARD + low, GUARD + high)
        plain = span(low, high)
        cells, remains = [], []
        for c in range(chunks):
            now = value[0][layer_no, c, own]
            centre = (
                west[0][layer_no, c, plain]
                + west[0][layer_no, c, span(low + 1, high + 1)]
                + south[0][layer_no, c, plain]
                + south[0][layer_no, c + 1, plain]
                + upper[0][layer_no, c, plain]
                + upper[0][layer_no + 1, c, plain]
            )
            remain = (
                forcing[0][layer_no, c, plain] - centre * now + around(0, layer_no, c, low, high)
            )
            if not top:
                remain += upper[0][layer_no, c, plain] * value[0][layer_no - 1, c, own]
            if not bottom:
                remain += upper[0][layer_no + 1, c, plain] * value[0][layer_no + 1, c, own]
            cells.append(now)
            remains.append(remain)
        for tile_no in range(plan.own_cols // LANES):
            columns = slice(tile_no * LANES, (tile_no + 1) * LANES)
            staged[0][layer_no, :, columns] = in_order(cells, tile_no)
            staged[1][layer_no, :, columns] = in_order(remains, tile_no)

    copies = []
    for layer_no in range(layers):
        finish(layer_no, layer_no == 0, layer_no == layers - 1)
        if layer_no % 4 == 3:
            block = pl.ds(layer_no - 3, 4)
            for i in range(2):
                copy = pltpu.make_async_copy(
                    staged[i].at[block], out_refs[i].at[block], semaphore.at[i, layer_no // 4]
                )
                copy.start()
                copies.append(copy)
    for copy in copies:
        copy.wait()


def per_device(source, inv_density):
    layers, rows, cols = source.shape
    plan = Plan(lax.axis_size("cross"), layers, rows, cols)
    levels = plan.coarsest + 1
    vmem = pl.BlockSpec(memory_space=pltpu.VMEM)

    shape = functools.partial(jax.ShapeDtypeStruct, dtype=jnp.float32)

    def kernel(body, inputs, outputs):
        return pl.pallas_call(
            functools.partial(body, plan),
            out_shape=outputs,
            in_specs=[vmem] * len(inputs),
            out_specs=[vmem] * len(outputs),
            compiler_params=pltpu.CompilerParams(vmem_limit_bytes=24 << 20),
        )(*inputs)

    def exchanged(sent, axis):
        return [
            swapped(each, axis, index // 2 + 1, 1 - index % 2) for index, each in enumerate(sent)
        ]

    def pairs_of(messages, *tail):
        half = len(messages) // 2
        return [shape((each.size,) + tail) for each in messages[:half] if each.size for _ in range(2)]

    cross_shapes = pairs_of(plan.cross, rows, LANES)
    both = jnp.stack([inv_density, source])
    halos = exchanged(kernel(edge_kernel, [both], cross_shapes), "cross")
    cells, *sent = kernel(
        cells_kernel,
        [both],
        [shape((2, layers, plan.halves, rows, LANES))] + pairs_of(plan.along, 8, LANES),
    )
    beside = exchanged(sent, "along")
    corners = []
    for swap, halo in enumerate(halos):
        messages = [each[swap // 2] for each in plan.corners]
        sent = kernel(
            functools.partial(corner_kernel, swap // 2), [halo], pairs_of(messages, 8, LANES)
        )
        corners.append(exchanged(sent, "along"))
    window = kernel(
        window_kernel,
        [cells, *halos, *beside, *corners[0]],
        [shape((2, layers, plan.chunks, rows, LANES))]
        + [shape((plan.side_size(side), 8, LANES)) for side in range(len(plan.along))],
    )
    inputs = [*window, *sum(corners[1:], [])]

    def room(*shape):
        return pltpu.VMEM(shape + (LANES,), jnp.float32)

    total, high = plan.rows, plan.rows + GUARD
    counts = [plan.level_chunks(m) for m in range(levels)]
    scratch = [pltpu.VMEM((layers, rows, cols), jnp.float32)] * 2
    scratch += [
        room(layers, counts[-1], total),
        room(layers + 1, counts[0], total),
        pltpu.SMEM((1,), jnp.int32),
        pltpu.SemaphoreType.DMA((2, layers // 4)),
    ]
    scratch += [room(layers, n, high) for n in counts]
    scratch += [room(layers, n + 1, total) for n in counts]
    scratch += [room(layers, n, total) for n in counts]
    scratch += [room(layers, n, total) for n in counts]
    scratch += [room(layers, n, high + GUARD) for n in counts]
    scratch += [room(layers, counts[0], total)]
    scratch += [room(layers + 1, n, total) for n in counts[1:]]
    held = sum(math.prod(each.shape) for each in scratch) + sum(each.size for each in inputs)
    held = 4 * held
    return pl.pallas_call(
        functools.partial(cycle_kernel, plan),
        out_shape=[jax.ShapeDtypeStruct((layers, rows, cols), jnp.float32)] * 2,
        in_specs=[vmem] * len(inputs),
        out_specs=[pl.BlockSpec(memory_space=pl.ANY)] * 2,
        scratch_shapes=scratch,
        compiler_params=pltpu.CompilerParams(vmem_limit_bytes=held + (3 << 20)),
    )(*inputs)


def solution(mesh):
    return jax.shard_map(
        per_device,
        mesh=mesh,
        in_specs=(P(None, "along", "cross"), P(None, "along", "cross")),
        out_specs=(P(None, "along", "cross"), P(None, "along", "cross")),
        check_vma=False,
    )
```

```python
import functools
import math

import jax
import jax.numpy as jnp
from jax import lax
from jax.experimental import pallas as pl
from jax.experimental.pallas import tpu as pltpu
from jax.sharding import PartitionSpec as P

SWEEPS = 4

along_weight = 0.25
cross_weight = 1.0
vertical_weight = 0.5
relaxation = 0.8

LANES = 128
GUARD = 8
TINY = 1e-30


def rounded_up(count, step):
    return -(-count // step) * step


def swapped(array, axis, distance, second):
    devices = lax.axis_size(axis)
    pairs = []
    for i in range(devices - distance):
        if i // distance % 2 == second:
            pairs += [(i, i + distance), (i + distance, i)]
    return lax.ppermute(array, axis, pairs)


def is_even(axis, distance):
    return (lax.axis_index(axis) // distance) % 2 == 0


def chosen(condition, first, second):
    return jnp.where(condition, first, second), jnp.where(condition, second, first)


def runs_of(first, count):
    runs, last = [], first + count
    while first < last:
        run = 8 if first % 8 == 0 and first + 8 <= last else 4
        runs.append((first, run))
        first += run
    return sorted(runs, key=lambda each: -each[1])


def hops_of(size, reach):
    hops = []
    while reach > 0:
        hops.append(min(size, reach))
        reach -= hops[-1]
    return hops


class CrossMessage:
    def __init__(self, layers, chunks, first, count):
        self.first, self.lanes, self.chunks = first, count // chunks, chunks
        self.share = LANES // self.lanes
        self.half = layers // 2 * chunks
        self.each = -(-2 * self.half // self.share)
        self.size = 2 * self.each

    def place(self, which, layer_no, chunk):
        item = which * self.half + layer_no // 2 * self.chunks + chunk
        return item // self.share, item % self.share * self.lanes


class RowMessage:
    def __init__(self, arrays, first, count, extra, tiles_of):
        self.parts, self.size = [], 0
        for which in range(arrays):
            for start, run in runs_of(first, count):
                self.parts.append((which, start, run, self.size))
                self.size += tiles_of(run)
        if extra is not None:
            self.parts.append((0, extra, 1, self.size))
            self.size += tiles_of(1)


class Plan:
    def __init__(self, cross_count, layers, rows, cols):
        self.coarsest = cross_count.bit_length()
        self.layers, self.own_rows, self.own_cols = layers, rows, cols
        self.row_reach = rounded_up(SWEEPS + 2 * self.coarsest, 4)
        reach = SWEEPS
        for _ in range(self.coarsest):
            reach = 2 * reach + 1
        self.col_reach = reach + 1
        chunks = 1
        while (chunks * LANES - cols) // 2 < self.col_reach:
            chunks *= 2
        self.chunks = chunks
        self.side_cols = (chunks * LANES - cols) // 2
        self.rows = rounded_up(rows + 2 * self.row_reach, 8)
        self.own_lane, self.own_lanes = self.side_cols // chunks, cols // chunks
        self.fold = LANES // self.own_lanes
        self.halves = chunks // self.fold
        hops = hops_of(cols, rounded_up(self.col_reach, chunks))
        self.cross_count = len(hops)
        self.cross = [CrossMessage(layers, chunks, cols - n, n) for n in hops]
        self.cross += [CrossMessage(layers, chunks, 0, n) for n in hops]
        self.cross_lane = [
            self.own_lane - hop * self.own_lanes - self.cross[hop].lanes for hop in range(len(hops))
        ] + [self.own_lane + (hop + 1) * self.own_lanes for hop in range(len(hops))]
        counts = hops_of(rows, self.row_reach)
        extra_hop, extra_row = divmod(self.row_reach, rows)
        counts += [0] * (extra_hop + 1 - len(counts))
        self.along_count = len(counts)
        self.along, self.corners, self.along_row = [], [], []
        for side in (-1, 1):
            for hop, n in enumerate(counts):
                first = rows - n if side < 0 else 0
                extra = None
                if hop == extra_hop:
                    extra = rows - 1 - extra_row if side < 0 else extra_row
                self.along.append(
                    RowMessage(2, first, n, extra, lambda run: layers * run // 8 * self.halves)
                )
                self.corners.append(
                    [
                        RowMessage(1, first, n, None, lambda run: each.each * run // 4)
                        for each in self.cross[: self.cross_count]
                    ]
                )
                self.along_row.append(self.row_reach + side * (hop + 1) * rows)

    def level_chunks(self, level_no):
        return max(1, self.chunks >> level_no)

    def spread(self, level_no):
        return max(1, (1 << level_no) // self.chunks)

    def own_tile(self, part, layer_no, half):
        share = 8 // part[2]
        return part[3] + layer_no // share * self.halves + half

    def side_tile(self, side, index, layer_no, chunk):
        parts = self.along[side].parts
        base = sum(self.layers * part[2] // 8 for part in parts[:index])
        return (base + layer_no * parts[index][2] // 8) * self.chunks + chunk

    def side_size(self, side):
        return sum(self.layers * part[2] // 8 for part in self.along[side].parts) * self.chunks

    def corner_tile(self, part, cross_hop, parity, group):
        return part[3] + (parity * self.cross[cross_hop].each if part[2] == 8 else 0) + group


def lane_numbers(rows):
    return lax.broadcasted_iota(jnp.int32, (rows, LANES), 1)


def taken(value, pick):
    return jnp.take_along_axis(value, pick, axis=1, mode="promise_in_bounds")


def edge_kernel(plan, both_ref, *cross_refs):
    lane = lane_numbers(plan.own_rows)
    chunks = plan.chunks
    tiles = range(0, plan.own_cols, LANES)

    def packed(message, group, parity):
        lanes, share = message.lanes, message.share
        slot = lane // lanes
        low_item = group * share
        cell = message.first + chunks * (lane - slot * lanes)
        cell = cell + ((slot + low_item) & (chunks - 1))
        items = range(low_item, min(low_item + share, 2 * message.half))
        value = None
        for first in sorted({item // chunks * chunks for item in items}):
            low = max(first - low_item, 0)
            which, pair = first // message.half, first % message.half // chunks
            for start in tiles:
                if start + LANES <= message.first or start >= message.first + lanes * chunks:
                    continue
                each = both_ref[which, 2 * pair + parity, :, start : start + LANES]
                each = taken(each, cell & (LANES - 1))
                if value is None:
                    value = each
                else:
                    value = jnp.where((slot >= low) & (cell >= start), each, value)
        return value

    hops = plan.cross_count
    for hop in range(hops):
        even = is_even("cross", hop + 1)
        tail, head = plan.cross[hop], plan.cross[hops + hop]
        for parity in range(2):
            for group in range(tail.each):
                row = parity * tail.each + group
                cross_refs[2 * hop + 1][row], cross_refs[2 * hop][row] = chosen(
                    even, packed(tail, group, parity), packed(head, group, parity)
                )


def cells_kernel(plan, both_ref, cells_ref, *along_refs):
    lane = lane_numbers(plan.own_rows)
    chunks, layers = plan.chunks, plan.layers
    tiles = range(0, plan.own_cols, LANES)
    hops = plan.along_count
    evens = [is_even("along", hop + 1) for hop in range(hops)]
    place = (lane - plan.own_lane) & (LANES - 1)
    within = place & (plan.own_lanes - 1)
    for half in range(plan.halves):
        cell = chunks * within + half * plan.fold + place // plan.own_lanes
        pick = cell & (LANES - 1)
        for which in range(2):
            for layer_no in range(layers):
                value = None
                for start in tiles:
                    each = taken(both_ref[which, layer_no, :, start : start + LANES], pick)
                    value = each if value is None else jnp.where(cell >= start, each, value)
                cells_ref[which, layer_no, half] = value
                for hop in range(hops):
                    tail, head = plan.along[hop], plan.along[hops + hop]
                    for last, first in zip(tail.parts, head.parts):
                        if last[0] == which:
                            run = last[2]
                            low = layer_no % (8 // run) * run
                            tile = plan.own_tile(last, layer_no, half)
                            one, two = chosen(
                                evens[hop],
                                value[last[1] : last[1] + run],
                                value[first[1] : first[1] + run],
                            )
                            along_refs[2 * hop + 1][tile, low : low + run] = one
                            along_refs[2 * hop][tile, low : low + run] = two


def corner_kernel(cross_hop, plan, halo_ref, *out_refs):
    each = plan.cross[cross_hop].each
    hops = plan.along_count
    for hop in range(hops):
        tail, head = plan.corners[hop][cross_hop], plan.corners[hops + hop][cross_hop]
        if not tail.size:
            continue
        even = is_even("along", hop + 1)
        for last, first in zip(tail.parts, head.parts):
            run = last[2]
            for parity in range(2):
                low = parity * 4 if run == 4 else 0
                for group in range(each):
                    tile = plan.corner_tile(last, cross_hop, parity, group)
                    row = parity * each + group
                    one, two = chosen(
                        even,
                        halo_ref[row, last[1] : last[1] + run],
                        halo_ref[row, first[1] : first[1] + run],
                    )
                    out_refs[2 * hop + 1][tile, low : low + run] = one
                    out_refs[2 * hop][tile, low : low + run] = two


def turned(value, by):
    by %= LANES
    return pltpu.roll(value, by, 1) if by else value


class Halos:
    def __init__(self, plan):
        self.plan, self.swaps, self.masks = plan, [], {}
        for hop in range(plan.cross_count):
            even = is_even("cross", hop + 1)
            for before in (even, jnp.logical_not(even)):
                low = jnp.where(before, 0, plan.cross_lane[plan.cross_count + hop])
                high = jnp.where(before, plan.cross_lane[hop] + plan.cross[hop].lanes, LANES)
                self.swaps.append((hop, before, low, high))

    def beside(self, value, which, layer_no, chunk, halo_of, swaps):
        plan = self.plan
        height = value.shape[0]
        if height not in self.masks:
            lane = lane_numbers(height)
            self.masks[height] = [
                (lane >= low) & (lane < high) for _, _, low, high in self.swaps
            ]
        for swap in swaps:
            hop, before, _, _ = self.swaps[swap]
            group, offset = plan.cross[hop].place(which, layer_no, chunk)
            by = jnp.where(
                before,
                (plan.cross_lane[hop] - offset) % LANES,
                (plan.cross_lane[plan.cross_count + hop] - offset) % LANES,
            )
            cells = pltpu.roll(halo_of(swap, group), by, 1)
            value = jnp.where(self.masks[height][swap], cells, value)
        return value


def from_swaps(plan, hop, after, pair, tile):
    even = is_even("along", hop + 1)
    two, one = pair[2 * hop], pair[2 * hop + 1]
    return jnp.where(even, one[tile], two[tile]) if after else jnp.where(even, two[tile], one[tile])


def corner_of(plan, side, index, layer_no, corner_refs):
    after, hop = divmod(side, plan.along_count)
    index = [part for part in plan.along[side].parts if part[2] > 1].index(
        plan.along[side].parts[index]
    )

    def halo_of(swap, group):
        parts = plan.corners[side][swap // 2].parts
        tile = plan.corner_tile(parts[index % len(parts)], swap // 2, layer_no % 2, group)
        return from_swaps(plan, hop, after, corner_refs[swap], tile)

    return halo_of


def window_kernel(plan, cells_ref, *refs):
    halos, swaps, hops = Halos(plan), 2 * plan.cross_count, len(plan.along)
    halo_refs, along_refs = refs[:swaps], refs[swaps : swaps + hops]
    corner_refs = refs[swaps + hops : -1 - hops]
    own_ref, side_refs = refs[-1 - hops], refs[-hops:]
    turns = [-(chunk % plan.fold) * plan.own_lanes for chunk in range(plan.chunks)]
    for which in range(2):
        for layer_no in range(plan.layers):
            for chunk in range(plan.chunks):

                def halo_of(swap, group):
                    return halo_refs[swap][layer_no % 2 * plan.cross[swap // 2].each + group]

                value = turned(cells_ref[which, layer_no, chunk // plan.fold], turns[chunk])
                own_ref[which, layer_no, chunk] = halos.beside(
                    value, which, layer_no, chunk, halo_of, range(swaps)
                )
    for side, message in enumerate(plan.along):
        after, hop = divmod(side, plan.along_count)
        for index, part in enumerate(message.parts):
            which, _, run, _ = part
            for layer_no in range(0, plan.layers, 8 // run):
                for chunk in range(plan.chunks):
                    tile = plan.own_tile(part, layer_no, chunk // plan.fold)
                    value = from_swaps(plan, hop, after, along_refs, tile)
                    value = turned(value, turns[chunk])
                    if run > 1:
                        halo_of = corner_of(plan, side, index, layer_no, [corner_refs])
                        value = halos.beside(value, which, layer_no, chunk, halo_of, range(1))
                    side_refs[side][plan.side_tile(side, index, layer_no, chunk)] = value


def reciprocal(value):
    guess = pl.reciprocal(value, approx=True)
    return guess * (2.0 - value * guess)


def ratio(first, second):
    return first * second * reciprocal(jnp.maximum(first + second, TINY))


def first_of_pair(value, spread):
    lane = lane_numbers(value.shape[0])
    return (lane & spread) == 0


def paired(cells, spread):
    if len(cells) > 1:
        return [cells[2 * k] + cells[2 * k + 1] for k in range(len(cells) // 2)]
    value = cells[0]
    return [value + taken(value, lane_numbers(value.shape[0]) ^ spread)]


def firsts(cells, spread):
    if len(cells) > 1:
        return cells[0::2]
    value = cells[0]
    return [jnp.where(first_of_pair(value, spread), value, pltpu.roll(value, spread, 1))]


def cycle_kernel(plan, own_ref, *refs):
    hops, swaps = len(plan.along), 2 * plan.cross_count
    side_refs, refs = refs[:hops], refs[hops:]
    sent = 2 * sum(each[0].size > 0 for each in plan.corners[: plan.along_count])
    corner_refs = [None] + [refs[i * sent : (i + 1) * sent] for i in range(swaps - 1)]
    refs = refs[(swaps - 1) * sent :]
    out_refs, staged = refs[:2], refs[2:4]
    upright, upper0, origin, semaphore = refs[4:8]
    rest = refs[8:]
    levels = plan.coarsest + 1
    coarsest = plan.coarsest
    layers, rows = plan.layers, plan.rows
    reach, own_rows = plan.row_reach, plan.own_rows
    west, south, factor, inverse, value, forcing = [
        rest[i * levels : (i + 1) * levels] for i in range(6)
    ]
    upper = [upper0] + list(forcing[1:])
    density = value[0]
    count = [plan.level_chunks(m) for m in range(levels)]
    spread = [plan.spread(m) for m in range(levels)]

    origin[0] = 0
    start0 = origin[0]

    def span(low, high):
        if low % 8 == 0 and high % 8 == 0:
            return pl.ds(low, high - low)
        return pl.ds(start0 + low, high - low)

    halos = Halos(plan)
    targets = ((density, GUARD), (forcing[0], 0))
    for which, (target, guard) in enumerate(targets):
        for layer_no in range(layers):
            for c in range(count[0]):
                target[layer_no, c, span(guard + reach, guard + reach + own_rows)] = own_ref[
                    which, layer_no, c
                ]
    for side, message in enumerate(plan.along):
        for index, part in enumerate(message.parts):
            which, start, run, _ = part
            target, guard = targets[which]
            first = guard + plan.along_row[side] + start
            share = 8 // run
            for layer_no in range(0, layers, share):
                for c in range(count[0]):
                    now = side_refs[side][plan.side_tile(side, index, layer_no, c)]
                    if run > 1:
                        halo_of = corner_of(plan, side, index, layer_no, corner_refs)
                        now = halos.beside(now, which, layer_no, c, halo_of, range(1, swaps))
                    for i in range(share):
                        target[layer_no + i, c, span(first, first + run)] = now[
                            i * run : (i + 1) * run
                        ]

    def faces(layer_no, first):
        cells = [density[layer_no, c, GUARD : GUARD + rows] for c in range(count[0])]
        souths = []
        for c in range(count[0]):
            behind = cells[c - 1] if c else pltpu.roll(cells[-1], 1, 1)
            souths.append(2.0 * cross_weight * ratio(cells[c], behind))
        for m in range(levels):
            if m > 0:
                souths = [0.5 * each for each in firsts(souths, spread[m - 1])]
            for c in range(count[m]):
                south[m][layer_no, c] = souths[c]
            south[m][layer_no, count[m]] = pltpu.roll(souths[0], LANES - spread[m], 1)
        uppers = []
        for c in range(count[0]):
            if first:
                uppers.append(2.0 * vertical_weight * cells[c])
            else:
                above = density[layer_no - 1, c, GUARD : GUARD + rows]
                uppers.append(2.0 * vertical_weight * ratio(cells[c], above))
        for m in range(levels):
            if m > 0:
                uppers = paired(uppers, spread[m - 1])
            for c in range(count[m]):
                upper[m][layer_no, c] = uppers[c]
        wests = []
        for c in range(count[0]):
            here = density[layer_no, c, GUARD : 2 * GUARD + rows]
            behind = density[layer_no, c, span(GUARD - 1, 2 * GUARD + rows - 1)]
            wests.append(2.0 * along_weight * ratio(here, behind))
        for m in range(levels):
            if m > 0:
                wests = paired(wests, spread[m - 1])
            for c in range(count[m]):
                west[m][layer_no, c] = wests[c]

    faces(0, True)
    pl.loop(1, layers, unroll=3)(lambda layer_no: faces(layer_no, False))
    for m in range(levels):
        for c in range(count[m]):
            upper[m][layers, c] = jnp.zeros((rows, LANES), jnp.float32)

    def pivots(some, layer_no, before, first):
        after = []
        for m in some:
            for c in range(count[m]):
                above = upper[m][layer_no, c]
                centre = (
                    west[m][layer_no, c, 0:rows]
                    + west[m][layer_no, c, span(1, rows + 1)]
                    + south[m][layer_no, c]
                    + south[m][layer_no, c + 1]
                    + above
                    + upper[m][layer_no + 1, c]
                )
                if first:
                    pivot = centre
                else:
                    share = above * before[len(after)]
                    factor[m][layer_no, c] = share
                    pivot = centre - above * share
                inverted = reciprocal(jnp.maximum(pivot, TINY))
                inverse[m][layer_no, c] = relaxation * inverted
                after.append(inverted)
        return tuple(after)

    for some in (range(1), range(1, levels)):
        lax.fori_loop(
            1,
            layers,
            lambda z, before: pivots(some, z, before, False),
            pivots(some, 0, None, True),
            unroll=3,
        )

    def around(m, layer_no, c, low, high):
        own = span(GUARD + low, GUARD + high)
        last = count[m] - 1
        behind = value[m][layer_no, c - 1 if c else last, own]
        ahead = value[m][layer_no, 0 if c == last else c + 1, own]
        if c == 0:
            behind = pltpu.roll(behind, spread[m], 1)
        if c == last:
            ahead = pltpu.roll(ahead, LANES - spread[m], 1)
        return (
            west[m][layer_no, c, span(low, high)]
            * value[m][layer_no, c, span(GUARD + low - 1, GUARD + high - 1)]
            + west[m][layer_no, c, span(low + 1, high + 1)]
            * value[m][layer_no, c, span(GUARD + low + 1, GUARD + high + 1)]
            + south[m][layer_no, c, span(low, high)] * behind
            + south[m][layer_no, c + 1, span(low, high)] * ahead
        )

    def solve(m, low, high, right_side, held, offset, store):
        place = slice(offset + low, offset + high)

        def down(layer_no, before):
            now = []
            for c in range(count[m]):
                each = right_side(layer_no, c)
                if before is not None:
                    each = each + factor[m][layer_no, c, low:high] * before[c]
                now.append(each)
                held[layer_no, c, place] = each * inverse[m][layer_no, c, low:high]
            return tuple(now)

        def up(step, below):
            layer_no = layers - 1 - step
            now = []
            for c in range(count[m]):
                each = held[layer_no, c, place]
                if below is not None:
                    each = each + factor[m][layer_no + 1, c, low:high] * below[c]
                now.append(each)
                store(layer_no, c, each)
            return tuple(now)

        for body in (down, up):
            now = body(0, None)
            if count[m] > 1:
                lax.fori_loop(1, layers, body, now, unroll=3 if count[m] == count[0] else 5)
            else:
                for step in range(1, layers):
                    now = body(step, now)

    def first_sweep(m):
        def store(layer_no, c, now):
            value[m][layer_no, c, GUARD : GUARD + rows] = now

        solve(m, 0, rows, lambda z, c: forcing[m][z, c], value[m], GUARD, store)

    def later_sweep(m, low, high, prolong):
        place = slice(GUARD + low, GUARD + high)

        def right_side(layer_no, c):
            return forcing[m][layer_no, c, low:high] + around(m, layer_no, c, low, high)

        def store(layer_no, c, now):
            new = (1.0 - relaxation) * value[m][layer_no, c, place] + now
            value[m][layer_no, c, place] = new
            if prolong:
                children = (2 * c, 2 * c + 1) if count[m - 1] > count[m] else (c,)
                for child in children:
                    value[m - 1][layer_no, child, place] += new

        held = upright if m == coarsest else inverse[m]
        solve(m, low, high, right_side, held, 0, store)

    for m in range(coarsest):
        first_sweep(m)

        def remain_of(layer_no, c, m=m):
            kept = (1.0 - relaxation) * forcing[m][layer_no, c]
            return kept + around(m, layer_no, c, 0, rows)

        def restrict(layer_no, m=m, remain_of=remain_of):
            for c in range(count[m + 1]):
                if count[m] > 1:
                    both = remain_of(layer_no, 2 * c) + remain_of(layer_no, 2 * c + 1)
                else:
                    (both,) = paired([remain_of(layer_no, c)], spread[m])
                forcing[m + 1][layer_no, c] = both

        pl.loop(0, layers, unroll=layers if count[m] == 1 else 4)(restrict)

    first_sweep(coarsest)
    for sweep_no in range(1, SWEEPS):
        later_sweep(coarsest, 0, rows, sweep_no == SWEEPS - 1)

    for m in range(coarsest - 1, -1, -1):
        low = (reach - m - 1) // 8 * 8
        high = rounded_up(reach + own_rows + m + 1, 8)
        later_sweep(m, low, high, m > 0)

    chunks = count[0]
    lane = lane_numbers(own_rows)

    lanes = LANES // chunks
    back = (lane & (chunks - 1)) * lanes + lane // chunks

    def in_order(cells, tile_no):
        start = (plan.side_cols + tile_no * LANES) // chunks
        out = turned(cells[0], -start)
        for c in range(1, chunks):
            out = jnp.where(lane >= c * lanes, turned(cells[c], c * lanes - start), out)
        return taken(out, back)

    def finish(layer_no):
        low, high = reach, reach + own_rows
        own = span(GUARD + low, GUARD + high)
        plain = span(low, high)
        cells, remains = [], []
        for c in range(chunks):
            now = value[0][layer_no, c, own]
            centre = (
                west[0][layer_no, c, plain]
                + west[0][layer_no, c, span(low + 1, high + 1)]
                + south[0][layer_no, c, plain]
                + south[0][layer_no, c + 1, plain]
                + upper[0][layer_no, c, plain]
                + upper[0][layer_no + 1, c, plain]
            )
            remain = (
                forcing[0][layer_no, c, plain] - centre * now + around(0, layer_no, c, low, high)
            )
            above = upper[0][layer_no, c, plain] * value[0][jnp.maximum(layer_no - 1, 0), c, own]
            remain += jnp.where(layer_no > 0, above, 0.0)
            beneath = value[0][jnp.minimum(layer_no + 1, layers - 1), c, own]
            remain += upper[0][layer_no + 1, c, plain] * beneath
            cells.append(now)
            remains.append(remain)
        for tile_no in range(plan.own_cols // LANES):
            columns = slice(tile_no * LANES, (tile_no + 1) * LANES)
            staged[0][layer_no, :, columns] = in_order(cells, tile_no)
            staged[1][layer_no, :, columns] = in_order(remains, tile_no)

    def leave(group):
        block = pl.ds(4 * group, 4)
        return [
            pltpu.make_async_copy(
                staged[i].at[block], out_refs[i].at[block], semaphore.at[i, group]
            )
            for i in range(2)
        ]

    def finish_group(group):
        for i in range(4):
            finish(4 * group + i)
        for copy in leave(group):
            copy.start()

    pl.loop(0, layers // 4)(finish_group)
    for group in range(layers // 4):
        for copy in leave(group):
            copy.wait()


def per_device(source, inv_density):
    layers, rows, cols = source.shape
    plan = Plan(lax.axis_size("cross"), layers, rows, cols)
    levels = plan.coarsest + 1
    vmem = pl.BlockSpec(memory_space=pltpu.VMEM)

    shape = functools.partial(jax.ShapeDtypeStruct, dtype=jnp.float32)

    def kernel(body, inputs, outputs):
        return pl.pallas_call(
            functools.partial(body, plan),
            out_shape=outputs,
            in_specs=[vmem] * len(inputs),
            out_specs=[vmem] * len(outputs),
            compiler_params=pltpu.CompilerParams(vmem_limit_bytes=24 << 20),
        )(*inputs)

    def exchanged(sent, axis):
        return [
            swapped(each, axis, index // 2 + 1, 1 - index % 2) for index, each in enumerate(sent)
        ]

    def pairs_of(messages, *tail):
        half = len(messages) // 2
        return [shape((each.size,) + tail) for each in messages[:half] if each.size for _ in range(2)]

    cross_shapes = pairs_of(plan.cross, rows, LANES)
    both = jnp.stack([inv_density, source])
    halos = exchanged(kernel(edge_kernel, [both], cross_shapes), "cross")
    cells, *sent = kernel(
        cells_kernel,
        [both],
        [shape((2, layers, plan.halves, rows, LANES))] + pairs_of(plan.along, 8, LANES),
    )
    beside = exchanged(sent, "along")
    corners = []
    for swap, halo in enumerate(halos):
        messages = [each[swap // 2] for each in plan.corners]
        sent = kernel(
            functools.partial(corner_kernel, swap // 2), [halo], pairs_of(messages, 8, LANES)
        )
        corners.append(exchanged(sent, "along"))
    window = kernel(
        window_kernel,
        [cells, *halos, *beside, *corners[0]],
        [shape((2, layers, plan.chunks, rows, LANES))]
        + [shape((plan.side_size(side), 8, LANES)) for side in range(len(plan.along))],
    )
    inputs = [*window, *sum(corners[1:], [])]

    def room(*shape):
        return pltpu.VMEM(shape + (LANES,), jnp.float32)

    total, high = plan.rows, plan.rows + GUARD
    counts = [plan.level_chunks(m) for m in range(levels)]
    scratch = [pltpu.VMEM((layers, rows, cols), jnp.float32)] * 2
    scratch += [
        room(layers, counts[-1], total),
        room(layers + 1, counts[0], total),
        pltpu.SMEM((1,), jnp.int32),
        pltpu.SemaphoreType.DMA((2, layers // 4)),
    ]
    scratch += [room(layers, n, high) for n in counts]
    scratch += [room(layers, n + 1, total) for n in counts]
    scratch += [room(layers, n, total) for n in counts]
    scratch += [room(layers, n, total) for n in counts]
    scratch += [room(layers, n, high + GUARD) for n in counts]
    scratch += [room(layers, counts[0], total)]
    scratch += [room(layers + 1, n, total) for n in counts[1:]]
    held = sum(math.prod(each.shape) for each in scratch) + sum(each.size for each in inputs)
    held = 4 * held
    return pl.pallas_call(
        functools.partial(cycle_kernel, plan),
        out_shape=[jax.ShapeDtypeStruct((layers, rows, cols), jnp.float32)] * 2,
        in_specs=[vmem] * len(inputs),
        out_specs=[pl.BlockSpec(memory_space=pl.ANY)] * 2,
        scratch_shapes=scratch,
        compiler_params=pltpu.CompilerParams(vmem_limit_bytes=held + (3 << 20)),
    )(*inputs)


def solution(mesh):
    return jax.shard_map(
        per_device,
        mesh=mesh,
        in_specs=(P(None, "along", "cross"), P(None, "along", "cross")),
        out_specs=(P(None, "along", "cross"), P(None, "along", "cross")),
        check_vma=False,
    )
```

```python
import functools
import math

import jax
import jax.numpy as jnp
from jax import lax
from jax.experimental import pallas as pl
from jax.experimental.pallas import tpu as pltpu
from jax.sharding import PartitionSpec as P

SWEEPS = 4

along_weight = 0.25
cross_weight = 1.0
vertical_weight = 0.5
relaxation = 0.8

LANES = 128
GUARD = 8
TINY = 1e-30


def rounded_up(count, step):
    return -(-count // step) * step


def swapped(array, axis, distance, second):
    devices = lax.axis_size(axis)
    pairs = []
    for i in range(devices - distance):
        if i // distance % 2 == second:
            pairs += [(i, i + distance), (i + distance, i)]
    return lax.ppermute(array, axis, pairs)


def is_even(axis, distance):
    return (lax.axis_index(axis) // distance) % 2 == 0


def chosen(condition, first, second):
    return jnp.where(condition, first, second), jnp.where(condition, second, first)


def runs_of(first, count):
    runs, last = [], first + count
    while first < last:
        run = 8 if first % 8 == 0 and first + 8 <= last else 4
        runs.append((first, run))
        first += run
    return sorted(runs, key=lambda each: -each[1])


def hops_of(size, reach):
    hops = []
    while reach > 0:
        hops.append(min(size, reach))
        reach -= hops[-1]
    return hops


class CrossMessage:
    def __init__(self, layers, chunks, first, count):
        self.first, self.lanes, self.chunks = first, count // chunks, chunks
        self.share = LANES // self.lanes
        self.half = layers // 2 * chunks
        self.each = -(-2 * self.half // self.share)
        self.size = 2 * self.each

    def place(self, which, layer_no, chunk):
        item = which * self.half + layer_no // 2 * self.chunks + chunk
        return item // self.share, item % self.share * self.lanes


class RowMessage:
    def __init__(self, arrays, first, count, extra, tiles_of):
        self.parts, self.size = [], 0
        for which in range(arrays):
            for start, run in runs_of(first, count):
                self.parts.append((which, start, run, self.size))
                self.size += tiles_of(run)
        if extra is not None:
            self.parts.append((0, extra, 1, self.size))
            self.size += tiles_of(1)


class Plan:
    def __init__(self, cross_count, layers, rows, cols):
        self.coarsest = cross_count.bit_length()
        self.layers, self.own_rows, self.own_cols = layers, rows, cols
        self.row_reach = rounded_up(SWEEPS + 2 * self.coarsest, 4)
        reach = SWEEPS
        for _ in range(self.coarsest):
            reach = 2 * reach + 1
        self.col_reach = reach + 1
        chunks = 1
        while (chunks * LANES - cols) // 2 < self.col_reach:
            chunks *= 2
        self.chunks = chunks
        self.side_cols = (chunks * LANES - cols) // 2
        self.rows = rounded_up(rows + 2 * self.row_reach, 8)
        self.own_lane, self.own_lanes = self.side_cols // chunks, cols // chunks
        self.fold = LANES // self.own_lanes
        self.halves = chunks // self.fold
        hops = hops_of(cols, rounded_up(self.col_reach, chunks))
        self.cross_count = len(hops)
        self.cross = [CrossMessage(layers, chunks, cols - n, n) for n in hops]
        self.cross += [CrossMessage(layers, chunks, 0, n) for n in hops]
        self.cross_lane = [
            self.own_lane - hop * self.own_lanes - self.cross[hop].lanes for hop in range(len(hops))
        ] + [self.own_lane + (hop + 1) * self.own_lanes for hop in range(len(hops))]
        counts = hops_of(rows, self.row_reach)
        extra_hop, extra_row = divmod(self.row_reach, rows)
        counts += [0] * (extra_hop + 1 - len(counts))
        self.along_count = len(counts)
        self.along, self.corners, self.along_row = [], [], []
        for side in (-1, 1):
            for hop, n in enumerate(counts):
                first = rows - n if side < 0 else 0
                extra = None
                if hop == extra_hop:
                    extra = rows - 1 - extra_row if side < 0 else extra_row
                self.along.append(
                    RowMessage(2, first, n, extra, lambda run: layers * run // 8 * self.halves)
                )
                self.corners.append(
                    [
                        RowMessage(1, first, n, None, lambda run: each.each * run // 4)
                        for each in self.cross[: self.cross_count]
                    ]
                )
                self.along_row.append(self.row_reach + side * (hop + 1) * rows)

    def level_chunks(self, level_no):
        return max(1, self.chunks >> level_no)

    def spread(self, level_no):
        return max(1, (1 << level_no) // self.chunks)

    def own_tile(self, part, layer_no, half):
        share = 8 // part[2]
        return part[3] + layer_no // share * self.halves + half

    def side_tile(self, side, index, layer_no, chunk):
        parts = self.along[side].parts
        base = sum(self.layers * part[2] // 8 for part in parts[:index])
        return (base + layer_no * parts[index][2] // 8) * self.chunks + chunk

    def side_size(self, side):
        return sum(self.layers * part[2] // 8 for part in self.along[side].parts) * self.chunks

    def corner_tile(self, part, cross_hop, parity, group):
        return part[3] + (parity * self.cross[cross_hop].each if part[2] == 8 else 0) + group


def lane_numbers(rows):
    return lax.broadcasted_iota(jnp.int32, (rows, LANES), 1)


def taken(value, pick):
    return jnp.take_along_axis(value, pick, axis=1, mode="promise_in_bounds")


def edge_kernel(plan, both_ref, *cross_refs):
    lane = lane_numbers(plan.own_rows)
    chunks = plan.chunks
    tiles = range(0, plan.own_cols, LANES)

    def packed(message, group, parity):
        lanes, share = message.lanes, message.share
        slot = lane // lanes
        low_item = group * share
        cell = message.first + chunks * (lane - slot * lanes)
        cell = cell + ((slot + low_item) & (chunks - 1))
        items = range(low_item, min(low_item + share, 2 * message.half))
        value = None
        for first in sorted({item // chunks * chunks for item in items}):
            low = max(first - low_item, 0)
            which, pair = first // message.half, first % message.half // chunks
            for start in tiles:
                if start + LANES <= message.first or start >= message.first + lanes * chunks:
                    continue
                each = both_ref[which, 2 * pair + parity, :, start : start + LANES]
                each = taken(each, cell & (LANES - 1))
                if value is None:
                    value = each
                else:
                    value = jnp.where((slot >= low) & (cell >= start), each, value)
        return value

    hops = plan.cross_count
    for hop in range(hops):
        even = is_even("cross", hop + 1)
        tail, head = plan.cross[hop], plan.cross[hops + hop]
        for parity in range(2):
            for group in range(tail.each):
                row = parity * tail.each + group
                cross_refs[2 * hop + 1][row], cross_refs[2 * hop][row] = chosen(
                    even, packed(tail, group, parity), packed(head, group, parity)
                )


def cells_kernel(plan, both_ref, cells_ref, *along_refs):
    lane = lane_numbers(plan.own_rows)
    chunks, layers = plan.chunks, plan.layers
    tiles = range(0, plan.own_cols, LANES)
    hops = plan.along_count
    evens = [is_even("along", hop + 1) for hop in range(hops)]
    place = (lane - plan.own_lane) & (LANES - 1)
    within = place & (plan.own_lanes - 1)
    for half in range(plan.halves):
        cell = chunks * within + half * plan.fold + place // plan.own_lanes
        pick = cell & (LANES - 1)
        for which in range(2):
            for layer_no in range(layers):
                value = None
                for start in tiles:
                    each = taken(both_ref[which, layer_no, :, start : start + LANES], pick)
                    value = each if value is None else jnp.where(cell >= start, each, value)
                cells_ref[which, layer_no, half] = value
                for hop in range(hops):
                    tail, head = plan.along[hop], plan.along[hops + hop]
                    for last, first in zip(tail.parts, head.parts):
                        if last[0] == which:
                            run = last[2]
                            low = layer_no % (8 // run) * run
                            tile = plan.own_tile(last, layer_no, half)
                            one, two = chosen(
                                evens[hop],
                                value[last[1] : last[1] + run],
                                value[first[1] : first[1] + run],
                            )
                            along_refs[2 * hop + 1][tile, low : low + run] = one
                            along_refs[2 * hop][tile, low : low + run] = two


def corner_kernel(cross_hop, plan, halo_ref, *out_refs):
    each = plan.cross[cross_hop].each
    hops = plan.along_count
    for hop in range(hops):
        tail, head = plan.corners[hop][cross_hop], plan.corners[hops + hop][cross_hop]
        if not tail.size:
            continue
        even = is_even("along", hop + 1)
        for last, first in zip(tail.parts, head.parts):
            run = last[2]
            for parity in range(2):
                low = parity * 4 if run == 4 else 0
                for group in range(each):
                    tile = plan.corner_tile(last, cross_hop, parity, group)
                    row = parity * each + group
                    one, two = chosen(
                        even,
                        halo_ref[row, last[1] : last[1] + run],
                        halo_ref[row, first[1] : first[1] + run],
                    )
                    out_refs[2 * hop + 1][tile, low : low + run] = one
                    out_refs[2 * hop][tile, low : low + run] = two


def turned(value, by):
    by %= LANES
    return pltpu.roll(value, by, 1) if by else value


class Halos:
    def __init__(self, plan):
        self.plan, self.swaps, self.masks = plan, [], {}
        for hop in range(plan.cross_count):
            even = is_even("cross", hop + 1)
            for before in (even, jnp.logical_not(even)):
                low = jnp.where(before, 0, plan.cross_lane[plan.cross_count + hop])
                high = jnp.where(before, plan.cross_lane[hop] + plan.cross[hop].lanes, LANES)
                self.swaps.append((hop, before, low, high))

    def beside(self, value, which, layer_no, chunk, halo_of, swaps):
        plan = self.plan
        height = value.shape[0]
        if height not in self.masks:
            lane = lane_numbers(height)
            self.masks[height] = [
                (lane >= low) & (lane < high) for _, _, low, high in self.swaps
            ]
        for swap in swaps:
            hop, before, _, _ = self.swaps[swap]
            group, offset = plan.cross[hop].place(which, layer_no, chunk)
            by = jnp.where(
                before,
                (plan.cross_lane[hop] - offset) % LANES,
                (plan.cross_lane[plan.cross_count + hop] - offset) % LANES,
            )
            cells = pltpu.roll(halo_of(swap, group), by, 1)
            value = jnp.where(self.masks[height][swap], cells, value)
        return value


def from_swaps(plan, hop, after, pair, tile):
    even = is_even("along", hop + 1)
    two, one = pair[2 * hop], pair[2 * hop + 1]
    return jnp.where(even, one[tile], two[tile]) if after else jnp.where(even, two[tile], one[tile])


def corner_of(plan, side, index, layer_no, corner_refs):
    after, hop = divmod(side, plan.along_count)
    index = [part for part in plan.along[side].parts if part[2] > 1].index(
        plan.along[side].parts[index]
    )

    def halo_of(swap, group):
        parts = plan.corners[side][swap // 2].parts
        tile = plan.corner_tile(parts[index % len(parts)], swap // 2, layer_no % 2, group)
        return from_swaps(plan, hop, after, corner_refs[swap], tile)

    return halo_of


def window_kernel(plan, cells_ref, *refs):
    halos, swaps, hops = Halos(plan), 2 * plan.cross_count, len(plan.along)
    halo_refs, along_refs = refs[:swaps], refs[swaps : swaps + hops]
    corner_refs = refs[swaps + hops : -1 - hops]
    own_ref, side_refs = refs[-1 - hops], refs[-hops:]
    turns = [-(chunk % plan.fold) * plan.own_lanes for chunk in range(plan.chunks)]
    for which in range(2):
        for layer_no in range(plan.layers):
            for chunk in range(plan.chunks):

                def halo_of(swap, group):
                    return halo_refs[swap][layer_no % 2 * plan.cross[swap // 2].each + group]

                value = turned(cells_ref[which, layer_no, chunk // plan.fold], turns[chunk])
                own_ref[which, layer_no, chunk] = halos.beside(
                    value, which, layer_no, chunk, halo_of, range(swaps)
                )
    for side, message in enumerate(plan.along):
        after, hop = divmod(side, plan.along_count)
        for index, part in enumerate(message.parts):
            which, _, run, _ = part
            for layer_no in range(0, plan.layers, 8 // run):
                for chunk in range(plan.chunks):
                    tile = plan.own_tile(part, layer_no, chunk // plan.fold)
                    value = from_swaps(plan, hop, after, along_refs, tile)
                    value = turned(value, turns[chunk])
                    if run > 1:
                        halo_of = corner_of(plan, side, index, layer_no, [corner_refs])
                        value = halos.beside(value, which, layer_no, chunk, halo_of, range(1))
                    side_refs[side][plan.side_tile(side, index, layer_no, chunk)] = value


def reciprocal(value):
    guess = pl.reciprocal(value, approx=True)
    return guess * (2.0 - value * guess)


def ratio(first, second):
    return first * second * reciprocal(jnp.maximum(first + second, TINY))


def first_of_pair(value, spread):
    lane = lane_numbers(value.shape[0])
    return (lane & spread) == 0


def paired(cells, spread):
    if len(cells) > 1:
        return [cells[2 * k] + cells[2 * k + 1] for k in range(len(cells) // 2)]
    value = cells[0]
    return [value + taken(value, lane_numbers(value.shape[0]) ^ spread)]


def firsts(cells, spread):
    if len(cells) > 1:
        return cells[0::2]
    value = cells[0]
    return [jnp.where(first_of_pair(value, spread), value, pltpu.roll(value, spread, 1))]


def cycle_kernel(plan, own_ref, *refs):
    hops, swaps = len(plan.along), 2 * plan.cross_count
    side_refs, refs = refs[:hops], refs[hops:]
    sent = 2 * sum(each[0].size > 0 for each in plan.corners[: plan.along_count])
    corner_refs = [None] + [refs[i * sent : (i + 1) * sent] for i in range(swaps - 1)]
    refs = refs[(swaps - 1) * sent :]
    out_refs, staged = refs[:2], refs[2:4]
    upright, upper0, origin, semaphore = refs[4:8]
    rest = refs[8:]
    levels = plan.coarsest + 1
    coarsest = plan.coarsest
    layers, rows = plan.layers, plan.rows
    reach, own_rows = plan.row_reach, plan.own_rows
    west, south, factor, inverse, value, forcing = [
        rest[i * levels : (i + 1) * levels] for i in range(6)
    ]
    upper = [upper0] + list(forcing[1:])
    density = value[0]
    count = [plan.level_chunks(m) for m in range(levels)]
    spread = [plan.spread(m) for m in range(levels)]

    origin[0] = 0
    start0 = origin[0]

    def span(low, high):
        if low % 8 == 0 and high % 8 == 0:
            return pl.ds(low, high - low)
        return pl.ds(start0 + low, high - low)

    halos = Halos(plan)
    targets = ((density, GUARD), (forcing[0], 0))

    def copy_own(layer_no):
        for which, (target, guard) in enumerate(targets):
            for c in range(count[0]):
                target[layer_no, c, span(guard + reach, guard + reach + own_rows)] = own_ref[
                    which, layer_no, c
                ]

    pl.loop(0, layers, unroll=2)(copy_own)
    for side, message in enumerate(plan.along):
        for index, part in enumerate(message.parts):
            which, start, run, _ = part
            target, guard = targets[which]
            first = guard + plan.along_row[side] + start
            share = 8 // run
            for layer_no in range(0, layers, share):
                for c in range(count[0]):
                    now = side_refs[side][plan.side_tile(side, index, layer_no, c)]
                    if run > 1:
                        halo_of = corner_of(plan, side, index, layer_no, corner_refs)
                        now = halos.beside(now, which, layer_no, c, halo_of, range(1, swaps))
                    for i in range(share):
                        target[layer_no + i, c, span(first, first + run)] = now[
                            i * run : (i + 1) * run
                        ]

    def faces(layer_no, first):
        cells = [density[layer_no, c, GUARD : GUARD + rows] for c in range(count[0])]
        souths = []
        for c in range(count[0]):
            behind = cells[c - 1] if c else pltpu.roll(cells[-1], 1, 1)
            souths.append(2.0 * cross_weight * ratio(cells[c], behind))
        for m in range(levels):
            if m > 0:
                souths = [0.5 * each for each in firsts(souths, spread[m - 1])]
            for c in range(count[m]):
                south[m][layer_no, c] = souths[c]
            south[m][layer_no, count[m]] = pltpu.roll(souths[0], LANES - spread[m], 1)
        uppers = []
        for c in range(count[0]):
            if first:
                uppers.append(2.0 * vertical_weight * cells[c])
            else:
                above = density[layer_no - 1, c, GUARD : GUARD + rows]
                uppers.append(2.0 * vertical_weight * ratio(cells[c], above))
        for m in range(levels):
            if m > 0:
                uppers = paired(uppers, spread[m - 1])
            for c in range(count[m]):
                upper[m][layer_no, c] = uppers[c]
        wests = []
        for c in range(count[0]):
            here = density[layer_no, c, GUARD : 2 * GUARD + rows]
            behind = density[layer_no, c, span(GUARD - 1, 2 * GUARD + rows - 1)]
            wests.append(2.0 * along_weight * ratio(here, behind))
        for m in range(levels):
            if m > 0:
                wests = paired(wests, spread[m - 1])
            for c in range(count[m]):
                west[m][layer_no, c] = wests[c]

    faces(0, True)
    pl.loop(1, layers, unroll=3)(lambda layer_no: faces(layer_no, False))
    for m in range(levels):
        for c in range(count[m]):
            upper[m][layers, c] = jnp.zeros((rows, LANES), jnp.float32)

    def pivots(some, layer_no, before, first):
        after = []
        for m in some:
            for c in range(count[m]):
                above = upper[m][layer_no, c]
                centre = (
                    west[m][layer_no, c, 0:rows]
                    + west[m][layer_no, c, span(1, rows + 1)]
                    + south[m][layer_no, c]
                    + south[m][layer_no, c + 1]
                    + above
                    + upper[m][layer_no + 1, c]
                )
                if first:
                    pivot = centre
                else:
                    share = above * before[len(after)]
                    factor[m][layer_no, c] = share
                    pivot = centre - above * share
                inverted = reciprocal(jnp.maximum(pivot, TINY))
                inverse[m][layer_no, c] = relaxation * inverted
                after.append(inverted)
        return tuple(after)

    for some in (range(1), range(1, levels)):
        lax.fori_loop(
            1,
            layers,
            lambda z, before: pivots(some, z, before, False),
            pivots(some, 0, None, True),
            unroll=3,
        )

    def around(m, layer_no, c, low, high):
        own = span(GUARD + low, GUARD + high)
        last = count[m] - 1
        behind = value[m][layer_no, c - 1 if c else last, own]
        ahead = value[m][layer_no, 0 if c == last else c + 1, own]
        if c == 0:
            behind = pltpu.roll(behind, spread[m], 1)
        if c == last:
            ahead = pltpu.roll(ahead, LANES - spread[m], 1)
        return (
            west[m][layer_no, c, span(low, high)]
            * value[m][layer_no, c, span(GUARD + low - 1, GUARD + high - 1)]
            + west[m][layer_no, c, span(low + 1, high + 1)]
            * value[m][layer_no, c, span(GUARD + low + 1, GUARD + high + 1)]
            + south[m][layer_no, c, span(low, high)] * behind
            + south[m][layer_no, c + 1, span(low, high)] * ahead
        )

    def solve(m, low, high, right_side, held, offset, store):
        place = slice(offset + low, offset + high)

        def down(layer_no, before):
            now = []
            for c in range(count[m]):
                each = right_side(layer_no, c)
                if before is not None:
                    each = each + factor[m][layer_no, c, low:high] * before[c]
                now.append(each)
                held[layer_no, c, place] = each * inverse[m][layer_no, c, low:high]
            return tuple(now)

        def up(step, below):
            layer_no = layers - 1 - step
            now = []
            for c in range(count[m]):
                each = held[layer_no, c, place]
                if below is not None:
                    each = each + factor[m][layer_no + 1, c, low:high] * below[c]
                now.append(each)
                store(layer_no, c, each)
            return tuple(now)

        for body in (down, up):
            now = body(0, None)
            if count[m] > 1:
                lax.fori_loop(1, layers, body, now, unroll=3 if count[m] == count[0] else 5)
            else:
                for step in range(1, layers):
                    now = body(step, now)

    def first_sweep(m):
        def store(layer_no, c, now):
            value[m][layer_no, c, GUARD : GUARD + rows] = now

        solve(m, 0, rows, lambda z, c: forcing[m][z, c], value[m], GUARD, store)

    def later_sweep(m, low, high, prolong):
        place = slice(GUARD + low, GUARD + high)

        def right_side(layer_no, c):
            return forcing[m][layer_no, c, low:high] + around(m, layer_no, c, low, high)

        def store(layer_no, c, now):
            new = (1.0 - relaxation) * value[m][layer_no, c, place] + now
            value[m][layer_no, c, place] = new
            if prolong:
                children = (2 * c, 2 * c + 1) if count[m - 1] > count[m] else (c,)
                for child in children:
                    value[m - 1][layer_no, child, place] += new

        held = upright if m == coarsest else inverse[m]
        solve(m, low, high, right_side, held, 0, store)

    for m in range(coarsest):
        first_sweep(m)

        def remain_of(layer_no, c, m=m):
            kept = (1.0 - relaxation) * forcing[m][layer_no, c]
            return kept + around(m, layer_no, c, 0, rows)

        def restrict(layer_no, m=m, remain_of=remain_of):
            for c in range(count[m + 1]):
                if count[m] > 1:
                    both = remain_of(layer_no, 2 * c) + remain_of(layer_no, 2 * c + 1)
                else:
                    (both,) = paired([remain_of(layer_no, c)], spread[m])
                forcing[m + 1][layer_no, c] = both

        pl.loop(0, layers, unroll=layers if count[m] == 1 else 4)(restrict)

    first_sweep(coarsest)
    pl.loop(1, SWEEPS)(lambda sweep_no: later_sweep(coarsest, 0, rows, False))

    def prolong_coarsest(layer_no):
        place = slice(GUARD, GUARD + rows)
        for c in range(count[coarsest - 1]):
            parent = c * count[coarsest] // count[coarsest - 1]
            value[coarsest - 1][layer_no, c, place] += value[coarsest][layer_no, parent, place]

    pl.loop(0, layers, unroll=4)(prolong_coarsest)

    for m in range(coarsest - 1, -1, -1):
        low = (reach - m - 1) // 8 * 8
        high = rounded_up(reach + own_rows + m + 1, 8)
        later_sweep(m, low, high, m > 0)

    chunks = count[0]
    lane = lane_numbers(own_rows)

    lanes = LANES // chunks
    back = (lane & (chunks - 1)) * lanes + lane // chunks

    def in_order(cells, tile_no):
        start = (plan.side_cols + tile_no * LANES) // chunks
        out = turned(cells[0], -start)
        for c in range(1, chunks):
            out = jnp.where(lane >= c * lanes, turned(cells[c], c * lanes - start), out)
        return taken(out, back)

    def finish(layer_no):
        low, high = reach, reach + own_rows
        own = span(GUARD + low, GUARD + high)
        plain = span(low, high)
        cells, remains = [], []
        for c in range(chunks):
            now = value[0][layer_no, c, own]
            centre = (
                west[0][layer_no, c, plain]
                + west[0][layer_no, c, span(low + 1, high + 1)]
                + south[0][layer_no, c, plain]
                + south[0][layer_no, c + 1, plain]
                + upper[0][layer_no, c, plain]
                + upper[0][layer_no + 1, c, plain]
            )
            remain = (
                forcing[0][layer_no, c, plain] - centre * now + around(0, layer_no, c, low, high)
            )
            above = upper[0][layer_no, c, plain] * value[0][jnp.maximum(layer_no - 1, 0), c, own]
            remain += jnp.where(layer_no > 0, above, 0.0)
            beneath = value[0][jnp.minimum(layer_no + 1, layers - 1), c, own]
            remain += upper[0][layer_no + 1, c, plain] * beneath
            cells.append(now)
            remains.append(remain)
        for tile_no in range(plan.own_cols // LANES):
            columns = slice(tile_no * LANES, (tile_no + 1) * LANES)
            staged[0][layer_no, :, columns] = in_order(cells, tile_no)
            staged[1][layer_no, :, columns] = in_order(remains, tile_no)

    def leave(group):
        block = pl.ds(4 * group, 4)
        return [
            pltpu.make_async_copy(
                staged[i].at[block], out_refs[i].at[block], semaphore.at[i, group]
            )
            for i in range(2)
        ]

    def finish_group(group):
        for i in range(4):
            finish(4 * group + i)
        for copy in leave(group):
            copy.start()

    pl.loop(0, layers // 4)(finish_group)
    for group in range(layers // 4):
        for copy in leave(group):
            copy.wait()


def per_device(source, inv_density):
    layers, rows, cols = source.shape
    plan = Plan(lax.axis_size("cross"), layers, rows, cols)
    levels = plan.coarsest + 1
    vmem = pl.BlockSpec(memory_space=pltpu.VMEM)

    shape = functools.partial(jax.ShapeDtypeStruct, dtype=jnp.float32)

    def kernel(body, inputs, outputs):
        return pl.pallas_call(
            functools.partial(body, plan),
            out_shape=outputs,
            in_specs=[vmem] * len(inputs),
            out_specs=[vmem] * len(outputs),
            compiler_params=pltpu.CompilerParams(vmem_limit_bytes=24 << 20),
        )(*inputs)

    def exchanged(sent, axis):
        return [
            swapped(each, axis, index // 2 + 1, 1 - index % 2) for index, each in enumerate(sent)
        ]

    def pairs_of(messages, *tail):
        half = len(messages) // 2
        return [shape((each.size,) + tail) for each in messages[:half] if each.size for _ in range(2)]

    cross_shapes = pairs_of(plan.cross, rows, LANES)
    both = jnp.stack([inv_density, source])
    halos = exchanged(kernel(edge_kernel, [both], cross_shapes), "cross")
    cells, *sent = kernel(
        cells_kernel,
        [both],
        [shape((2, layers, plan.halves, rows, LANES))] + pairs_of(plan.along, 8, LANES),
    )
    beside = exchanged(sent, "along")
    corners = []
    for swap, halo in enumerate(halos):
        messages = [each[swap // 2] for each in plan.corners]
        sent = kernel(
            functools.partial(corner_kernel, swap // 2), [halo], pairs_of(messages, 8, LANES)
        )
        corners.append(exchanged(sent, "along"))
    window = kernel(
        window_kernel,
        [cells, *halos, *beside, *corners[0]],
        [shape((2, layers, plan.chunks, rows, LANES))]
        + [shape((plan.side_size(side), 8, LANES)) for side in range(len(plan.along))],
    )
    inputs = [*window, *sum(corners[1:], [])]

    def room(*shape):
        return pltpu.VMEM(shape + (LANES,), jnp.float32)

    total, high = plan.rows, plan.rows + GUARD
    counts = [plan.level_chunks(m) for m in range(levels)]
    scratch = [pltpu.VMEM((layers, rows, cols), jnp.float32)] * 2
    scratch += [
        room(layers, counts[-1], total),
        room(layers + 1, counts[0], total),
        pltpu.SMEM((1,), jnp.int32),
        pltpu.SemaphoreType.DMA((2, layers // 4)),
    ]
    scratch += [room(layers, n, high) for n in counts]
    scratch += [room(layers, n + 1, total) for n in counts]
    scratch += [room(layers, n, total) for n in counts]
    scratch += [room(layers, n, total) for n in counts]
    scratch += [room(layers, n, high + GUARD) for n in counts]
    scratch += [room(layers, counts[0], total)]
    scratch += [room(layers + 1, n, total) for n in counts[1:]]
    held = sum(math.prod(each.shape) for each in scratch) + sum(each.size for each in inputs)
    held = 4 * held
    return pl.pallas_call(
        functools.partial(cycle_kernel, plan),
        out_shape=[jax.ShapeDtypeStruct((layers, rows, cols), jnp.float32)] * 2,
        in_specs=[vmem] * len(inputs),
        out_specs=[pl.BlockSpec(memory_space=pl.ANY)] * 2,
        scratch_shapes=scratch,
        compiler_params=pltpu.CompilerParams(vmem_limit_bytes=held + (3 << 20)),
    )(*inputs)


def solution(mesh):
    return jax.shard_map(
        per_device,
        mesh=mesh,
        in_specs=(P(None, "along", "cross"), P(None, "along", "cross")),
        out_specs=(P(None, "along", "cross"), P(None, "along", "cross")),
        check_vma=False,
    )
```

```python
import functools
import math

import jax
import jax.numpy as jnp
from jax import lax
from jax.experimental import pallas as pl
from jax.experimental.pallas import tpu as pltpu
from jax.sharding import PartitionSpec as P

SWEEPS = 4

along_weight = 0.25
cross_weight = 1.0
vertical_weight = 0.5
relaxation = 0.8

LANES = 128
GUARD = 8
TINY = 1e-30


def rounded_up(count, step):
    return -(-count // step) * step


def swapped(array, axis, distance, second):
    devices = lax.axis_size(axis)
    pairs = []
    for i in range(devices - distance):
        if i // distance % 2 == second:
            pairs += [(i, i + distance), (i + distance, i)]
    return lax.ppermute(array, axis, pairs)


def is_even(axis, distance):
    return (lax.axis_index(axis) // distance) % 2 == 0


def chosen(condition, first, second):
    return jnp.where(condition, first, second), jnp.where(condition, second, first)


def runs_of(first, count):
    runs, last = [], first + count
    while first < last:
        run = 8 if first % 8 == 0 and first + 8 <= last else 4
        runs.append((first, run))
        first += run
    return sorted(runs, key=lambda each: -each[1])


def hops_of(size, reach):
    hops = []
    while reach > 0:
        hops.append(min(size, reach))
        reach -= hops[-1]
    return hops


class CrossMessage:
    def __init__(self, layers, chunks, first, count):
        self.first, self.lanes, self.chunks = first, count // chunks, chunks
        self.share = LANES // self.lanes
        self.half = layers // 2 * chunks
        self.each = -(-2 * self.half // self.share)
        self.size = 2 * self.each

    def place(self, which, layer_no, chunk):
        item = which * self.half + layer_no // 2 * self.chunks + chunk
        return item // self.share, item % self.share * self.lanes


class RowMessage:
    def __init__(self, arrays, first, count, extra, tiles_of):
        self.parts, self.size = [], 0
        for which in range(arrays):
            for start, run in runs_of(first, count):
                self.parts.append((which, start, run, self.size))
                self.size += tiles_of(run)
        if extra is not None:
            self.parts.append((0, extra, 1, self.size))
            self.size += tiles_of(1)


class Plan:
    def __init__(self, cross_count, layers, rows, cols):
        self.coarsest = cross_count.bit_length()
        self.layers, self.own_rows, self.own_cols = layers, rows, cols
        self.row_reach = rounded_up(SWEEPS + 2 * self.coarsest, 4)
        reach = SWEEPS
        for _ in range(self.coarsest):
            reach = 2 * reach + 1
        self.col_reach = reach + 1
        chunks = 1
        while (chunks * LANES - cols) // 2 < self.col_reach:
            chunks *= 2
        self.chunks = chunks
        self.side_cols = (chunks * LANES - cols) // 2
        self.rows = rounded_up(rows + 2 * self.row_reach, 8)
        self.own_lane, self.own_lanes = self.side_cols // chunks, cols // chunks
        self.fold = LANES // self.own_lanes
        self.halves = chunks // self.fold
        hops = hops_of(cols, rounded_up(self.col_reach, chunks))
        self.cross_count = len(hops)
        self.cross = [CrossMessage(layers, chunks, cols - n, n) for n in hops]
        self.cross += [CrossMessage(layers, chunks, 0, n) for n in hops]
        self.cross_lane = [
            self.own_lane - hop * self.own_lanes - self.cross[hop].lanes for hop in range(len(hops))
        ] + [self.own_lane + (hop + 1) * self.own_lanes for hop in range(len(hops))]
        counts = hops_of(rows, self.row_reach)
        extra_hop, extra_row = divmod(self.row_reach, rows)
        counts += [0] * (extra_hop + 1 - len(counts))
        self.along_count = len(counts)
        self.along, self.corners, self.along_row = [], [], []
        for side in (-1, 1):
            for hop, n in enumerate(counts):
                first = rows - n if side < 0 else 0
                extra = None
                if hop == extra_hop:
                    extra = rows - 1 - extra_row if side < 0 else extra_row
                self.along.append(
                    RowMessage(2, first, n, extra, lambda run: layers * run // 8 * self.halves)
                )
                self.corners.append(
                    [
                        RowMessage(1, first, n, None, lambda run: each.each * run // 4)
                        for each in self.cross[: self.cross_count]
                    ]
                )
                self.along_row.append(self.row_reach + side * (hop + 1) * rows)

    def level_chunks(self, level_no):
        return max(1, self.chunks >> level_no)

    def spread(self, level_no):
        return max(1, (1 << level_no) // self.chunks)

    def own_tile(self, part, layer_no, half):
        share = 8 // part[2]
        return part[3] + layer_no // share * self.halves + half

    def side_tile(self, side, index, layer_no, chunk):
        parts = self.along[side].parts
        base = sum(self.layers * part[2] // 8 for part in parts[:index])
        return (base + layer_no * parts[index][2] // 8) * self.chunks + chunk

    def side_size(self, side):
        return sum(self.layers * part[2] // 8 for part in self.along[side].parts) * self.chunks

    def corner_tile(self, part, cross_hop, parity, group):
        return part[3] + (parity * self.cross[cross_hop].each if part[2] == 8 else 0) + group


def lane_numbers(rows):
    return lax.broadcasted_iota(jnp.int32, (rows, LANES), 1)


def taken(value, pick):
    return jnp.take_along_axis(value, pick, axis=1, mode="promise_in_bounds")


def edge_kernel(plan, both_ref, *cross_refs):
    lane = lane_numbers(plan.own_rows)
    chunks = plan.chunks
    tiles = range(0, plan.own_cols, LANES)

    def packed(message, group, parity):
        lanes, share = message.lanes, message.share
        slot = lane // lanes
        low_item = group * share
        cell = message.first + chunks * (lane - slot * lanes)
        cell = cell + ((slot + low_item) & (chunks - 1))
        items = range(low_item, min(low_item + share, 2 * message.half))
        value = None
        for first in sorted({item // chunks * chunks for item in items}):
            low = max(first - low_item, 0)
            which, pair = first // message.half, first % message.half // chunks
            for start in tiles:
                if start + LANES <= message.first or start >= message.first + lanes * chunks:
                    continue
                each = both_ref[which, 2 * pair + parity, :, start : start + LANES]
                each = taken(each, cell & (LANES - 1))
                if value is None:
                    value = each
                else:
                    value = jnp.where((slot >= low) & (cell >= start), each, value)
        return value

    hops = plan.cross_count
    for hop in range(hops):
        even = is_even("cross", hop + 1)
        tail, head = plan.cross[hop], plan.cross[hops + hop]
        for parity in range(2):
            for group in range(tail.each):
                row = parity * tail.each + group
                cross_refs[2 * hop + 1][row], cross_refs[2 * hop][row] = chosen(
                    even, packed(tail, group, parity), packed(head, group, parity)
                )


def cells_kernel(plan, both_ref, cells_ref, *along_refs):
    lane = lane_numbers(plan.own_rows)
    chunks, layers = plan.chunks, plan.layers
    tiles = range(0, plan.own_cols, LANES)
    hops = plan.along_count
    evens = [is_even("along", hop + 1) for hop in range(hops)]
    place = (lane - plan.own_lane) & (LANES - 1)
    within = place & (plan.own_lanes - 1)
    for half in range(plan.halves):
        cell = chunks * within + half * plan.fold + place // plan.own_lanes
        pick = cell & (LANES - 1)
        for which in range(2):
            for layer_no in range(layers):
                value = None
                for start in tiles:
                    each = taken(both_ref[which, layer_no, :, start : start + LANES], pick)
                    value = each if value is None else jnp.where(cell >= start, each, value)
                cells_ref[which, layer_no, half] = value
                for hop in range(hops):
                    tail, head = plan.along[hop], plan.along[hops + hop]
                    for last, first in zip(tail.parts, head.parts):
                        if last[0] == which:
                            run = last[2]
                            low = layer_no % (8 // run) * run
                            tile = plan.own_tile(last, layer_no, half)
                            one, two = chosen(
                                evens[hop],
                                value[last[1] : last[1] + run],
                                value[first[1] : first[1] + run],
                            )
                            along_refs[2 * hop + 1][tile, low : low + run] = one
                            along_refs[2 * hop][tile, low : low + run] = two


def corner_kernel(cross_hop, plan, halo_ref, *out_refs):
    each = plan.cross[cross_hop].each
    hops = plan.along_count
    for hop in range(hops):
        tail, head = plan.corners[hop][cross_hop], plan.corners[hops + hop][cross_hop]
        if not tail.size:
            continue
        even = is_even("along", hop + 1)
        for last, first in zip(tail.parts, head.parts):
            run = last[2]
            for parity in range(2):
                low = parity * 4 if run == 4 else 0
                for group in range(each):
                    tile = plan.corner_tile(last, cross_hop, parity, group)
                    row = parity * each + group
                    one, two = chosen(
                        even,
                        halo_ref[row, last[1] : last[1] + run],
                        halo_ref[row, first[1] : first[1] + run],
                    )
                    out_refs[2 * hop + 1][tile, low : low + run] = one
                    out_refs[2 * hop][tile, low : low + run] = two


def turned(value, by):
    by %= LANES
    return pltpu.roll(value, by, 1) if by else value


class Halos:
    def __init__(self, plan):
        self.plan, self.swaps, self.masks = plan, [], {}
        for hop in range(plan.cross_count):
            even = is_even("cross", hop + 1)
            for before in (even, jnp.logical_not(even)):
                low = jnp.where(before, 0, plan.cross_lane[plan.cross_count + hop])
                high = jnp.where(before, plan.cross_lane[hop] + plan.cross[hop].lanes, LANES)
                self.swaps.append((hop, before, low, high))

    def beside(self, value, which, layer_no, chunk, halo_of, swaps):
        plan = self.plan
        height = value.shape[0]
        if height not in self.masks:
            lane = lane_numbers(height)
            self.masks[height] = [
                (lane >= low) & (lane < high) for _, _, low, high in self.swaps
            ]
        for swap in swaps:
            hop, before, _, _ = self.swaps[swap]
            group, offset = plan.cross[hop].place(which, layer_no, chunk)
            by = jnp.where(
                before,
                (plan.cross_lane[hop] - offset) % LANES,
                (plan.cross_lane[plan.cross_count + hop] - offset) % LANES,
            )
            cells = pltpu.roll(halo_of(swap, group), by, 1)
            value = jnp.where(self.masks[height][swap], cells, value)
        return value


def from_swaps(plan, hop, after, pair, tile):
    even = is_even("along", hop + 1)
    two, one = pair[2 * hop], pair[2 * hop + 1]
    return jnp.where(even, one[tile], two[tile]) if after else jnp.where(even, two[tile], one[tile])


def corner_of(plan, side, index, layer_no, corner_refs):
    after, hop = divmod(side, plan.along_count)
    index = [part for part in plan.along[side].parts if part[2] > 1].index(
        plan.along[side].parts[index]
    )

    def halo_of(swap, group):
        parts = plan.corners[side][swap // 2].parts
        tile = plan.corner_tile(parts[index % len(parts)], swap // 2, layer_no % 2, group)
        return from_swaps(plan, hop, after, corner_refs[swap], tile)

    return halo_of


def window_kernel(plan, cells_ref, *refs):
    halos, swaps, hops = Halos(plan), 2 * plan.cross_count, len(plan.along)
    halo_refs, along_refs = refs[:swaps], refs[swaps : swaps + hops]
    corner_refs = refs[swaps + hops : -1 - hops]
    own_ref, side_refs = refs[-1 - hops], refs[-hops:]
    turns = [-(chunk % plan.fold) * plan.own_lanes for chunk in range(plan.chunks)]
    for which in range(2):
        for layer_no in range(plan.layers):
            for chunk in range(plan.chunks):

                def halo_of(swap, group):
                    return halo_refs[swap][layer_no % 2 * plan.cross[swap // 2].each + group]

                value = turned(cells_ref[which, layer_no, chunk // plan.fold], turns[chunk])
                own_ref[which, layer_no, chunk] = halos.beside(
                    value, which, layer_no, chunk, halo_of, range(swaps)
                )
    for side, message in enumerate(plan.along):
        after, hop = divmod(side, plan.along_count)
        for index, part in enumerate(message.parts):
            which, _, run, _ = part
            for layer_no in range(0, plan.layers, 8 // run):
                for chunk in range(plan.chunks):
                    tile = plan.own_tile(part, layer_no, chunk // plan.fold)
                    value = from_swaps(plan, hop, after, along_refs, tile)
                    value = turned(value, turns[chunk])
                    if run > 1:
                        halo_of = corner_of(plan, side, index, layer_no, [corner_refs])
                        value = halos.beside(value, which, layer_no, chunk, halo_of, range(1))
                    side_refs[side][plan.side_tile(side, index, layer_no, chunk)] = value


def reciprocal(value):
    guess = pl.reciprocal(value, approx=True)
    return guess * (2.0 - value * guess)


def ratio(first, second):
    return first * second * reciprocal(jnp.maximum(first + second, TINY))


def first_of_pair(value, spread):
    lane = lane_numbers(value.shape[0])
    return (lane & spread) == 0


def paired(cells, spread):
    if len(cells) > 1:
        return [cells[2 * k] + cells[2 * k + 1] for k in range(len(cells) // 2)]
    value = cells[0]
    return [value + taken(value, lane_numbers(value.shape[0]) ^ spread)]


def firsts(cells, spread):
    if len(cells) > 1:
        return cells[0::2]
    value = cells[0]
    return [jnp.where(first_of_pair(value, spread), value, pltpu.roll(value, spread, 1))]


def cycle_kernel(plan, own_ref, *refs):
    hops, swaps = len(plan.along), 2 * plan.cross_count
    side_refs, refs = refs[:hops], refs[hops:]
    sent = 2 * sum(each[0].size > 0 for each in plan.corners[: plan.along_count])
    corner_refs = [None] + [refs[i * sent : (i + 1) * sent] for i in range(swaps - 1)]
    refs = refs[(swaps - 1) * sent :]
    out_refs, staged = refs[:2], refs[2:4]
    upright, upper0, origin, semaphore = refs[4:8]
    rest = refs[8:]
    levels = plan.coarsest + 1
    coarsest = plan.coarsest
    layers, rows = plan.layers, plan.rows
    reach, own_rows = plan.row_reach, plan.own_rows
    west, south, factor, inverse, value, forcing = [
        rest[i * levels : (i + 1) * levels] for i in range(6)
    ]
    upper = [upper0] + list(forcing[1:])
    density = value[0]
    count = [plan.level_chunks(m) for m in range(levels)]
    spread = [plan.spread(m) for m in range(levels)]

    origin[0] = 0
    start0 = origin[0]

    def span(low, high):
        if low % 8 == 0 and high % 8 == 0:
            return pl.ds(low, high - low)
        return pl.ds(start0 + low, high - low)

    halos = Halos(plan)
    targets = ((density, GUARD), (forcing[0], 0))

    def copy_own(layer_no):
        for which, (target, guard) in enumerate(targets):
            for c in range(count[0]):
                target[layer_no, c, span(guard + reach, guard + reach + own_rows)] = own_ref[
                    which, layer_no, c
                ]

    pl.loop(0, layers, unroll=2)(copy_own)
    for side, message in enumerate(plan.along):
        for index, part in enumerate(message.parts):
            which, start, run, _ = part
            target, guard = targets[which]
            first = guard + plan.along_row[side] + start
            share = 8 // run
            for layer_no in range(0, layers, share):
                for c in range(count[0]):
                    now = side_refs[side][plan.side_tile(side, index, layer_no, c)]
                    if run > 1:
                        halo_of = corner_of(plan, side, index, layer_no, corner_refs)
                        now = halos.beside(now, which, layer_no, c, halo_of, range(1, swaps))
                    for i in range(share):
                        target[layer_no + i, c, span(first, first + run)] = now[
                            i * run : (i + 1) * run
                        ]

    def faces(layer_no, first):
        cells = [density[layer_no, c, GUARD : GUARD + rows] for c in range(count[0])]
        souths = []
        for c in range(count[0]):
            behind = cells[c - 1] if c else pltpu.roll(cells[-1], 1, 1)
            souths.append(2.0 * cross_weight * ratio(cells[c], behind))
        for m in range(levels):
            if m > 0:
                souths = [0.5 * each for each in firsts(souths, spread[m - 1])]
            for c in range(count[m]):
                south[m][layer_no, c] = souths[c]
            south[m][layer_no, count[m]] = pltpu.roll(souths[0], LANES - spread[m], 1)
        uppers = []
        for c in range(count[0]):
            if first:
                uppers.append(2.0 * vertical_weight * cells[c])
            else:
                above = density[layer_no - 1, c, GUARD : GUARD + rows]
                uppers.append(2.0 * vertical_weight * ratio(cells[c], above))
        for m in range(levels):
            if m > 0:
                uppers = paired(uppers, spread[m - 1])
            for c in range(count[m]):
                upper[m][layer_no, c] = uppers[c]
        wests = []
        for c in range(count[0]):
            here = density[layer_no, c, GUARD : 2 * GUARD + rows]
            behind = density[layer_no, c, span(GUARD - 1, 2 * GUARD + rows - 1)]
            wests.append(2.0 * along_weight * ratio(here, behind))
        for m in range(levels):
            if m > 0:
                wests = paired(wests, spread[m - 1])
            for c in range(count[m]):
                west[m][layer_no, c] = wests[c]

    faces(0, True)
    pl.loop(1, layers, unroll=3)(lambda layer_no: faces(layer_no, False))
    for m in range(levels):
        for c in range(count[m]):
            upper[m][layers, c] = jnp.zeros((rows, LANES), jnp.float32)

    def pivots(some, layer_no, before, first):
        after, lefts = [], []
        number = sum(count[m] for m in some)
        for m in some:
            for c in range(count[m]):
                above = upper[m][layer_no, c]
                centre = (
                    west[m][layer_no, c, 0:rows]
                    + west[m][layer_no, c, span(1, rows + 1)]
                    + south[m][layer_no, c]
                    + south[m][layer_no, c + 1]
                    + above
                    + upper[m][layer_no + 1, c]
                )
                if first:
                    pivot = centre
                else:
                    share = above * before[len(after)]
                    factor[m][layer_no, c] = share
                    pivot = centre - above * share
                inverted = reciprocal(jnp.maximum(pivot, TINY))
                scaled = relaxation * inverted
                inverse[m][layer_no, c] = scaled
                after.append(inverted)
                if m == 0:
                    left = forcing[0][layer_no, c, 0:rows]
                    if not first:
                        left = left + share * before[number + c]
                    value[0][layer_no, c, GUARD : GUARD + rows] = left * scaled
                    lefts.append(left)
        return tuple(after + lefts)

    for some in (range(1), range(1, levels)):
        lax.fori_loop(
            1,
            layers,
            lambda z, before: pivots(some, z, before, False),
            pivots(some, 0, None, True),
            unroll=3,
        )

    def around(m, layer_no, c, low, high):
        own = span(GUARD + low, GUARD + high)
        last = count[m] - 1
        behind = value[m][layer_no, c - 1 if c else last, own]
        ahead = value[m][layer_no, 0 if c == last else c + 1, own]
        if c == 0:
            behind = pltpu.roll(behind, spread[m], 1)
        if c == last:
            ahead = pltpu.roll(ahead, LANES - spread[m], 1)
        return (
            west[m][layer_no, c, span(low, high)]
            * value[m][layer_no, c, span(GUARD + low - 1, GUARD + high - 1)]
            + west[m][layer_no, c, span(low + 1, high + 1)]
            * value[m][layer_no, c, span(GUARD + low + 1, GUARD + high + 1)]
            + south[m][layer_no, c, span(low, high)] * behind
            + south[m][layer_no, c + 1, span(low, high)] * ahead
        )

    def solve(m, low, high, right_side, held, offset, store, forward=True):
        place = slice(offset + low, offset + high)

        def down(layer_no, before):
            now = []
            for c in range(count[m]):
                each = right_side(layer_no, c)
                if before is not None:
                    each = each + factor[m][layer_no, c, low:high] * before[c]
                now.append(each)
                held[layer_no, c, place] = each * inverse[m][layer_no, c, low:high]
            return tuple(now)

        def up(step, below):
            layer_no = layers - 1 - step
            now = []
            for c in range(count[m]):
                each = held[layer_no, c, place]
                if below is not None:
                    each = each + factor[m][layer_no + 1, c, low:high] * below[c]
                now.append(each)
                store(layer_no, c, each)
            return tuple(now)

        for body in (down, up) if forward else (up,):
            now = body(0, None)
            if count[m] > 1:
                lax.fori_loop(1, layers, body, now, unroll=3 if count[m] == count[0] else 5)
            else:
                for step in range(1, layers):
                    now = body(step, now)

    def first_sweep(m):
        def store(layer_no, c, now):
            value[m][layer_no, c, GUARD : GUARD + rows] = now

        solve(m, 0, rows, lambda z, c: forcing[m][z, c], value[m], GUARD, store, m > 0)

    def later_sweep(m, low, high, prolong):
        place = slice(GUARD + low, GUARD + high)

        def right_side(layer_no, c):
            return forcing[m][layer_no, c, low:high] + around(m, layer_no, c, low, high)

        def store(layer_no, c, now):
            new = (1.0 - relaxation) * value[m][layer_no, c, place] + now
            value[m][layer_no, c, place] = new
            if prolong:
                children = (2 * c, 2 * c + 1) if count[m - 1] > count[m] else (c,)
                for child in children:
                    value[m - 1][layer_no, child, place] += new

        held = upright if m == coarsest else inverse[m]
        solve(m, low, high, right_side, held, 0, store)

    for m in range(coarsest):
        first_sweep(m)

        def remain_of(layer_no, c, m=m):
            kept = (1.0 - relaxation) * forcing[m][layer_no, c, 0:rows]
            return kept + around(m, layer_no, c, 0, rows)

        def restrict(layer_no, m=m, remain_of=remain_of):
            for c in range(count[m + 1]):
                if count[m] > 1:
                    both = remain_of(layer_no, 2 * c) + remain_of(layer_no, 2 * c + 1)
                else:
                    (both,) = paired([remain_of(layer_no, c)], spread[m])
                forcing[m + 1][layer_no, c] = both

        pl.loop(0, layers, unroll=layers if count[m] == 1 else 4)(restrict)

    first_sweep(coarsest)
    pl.loop(1, SWEEPS)(lambda sweep_no: later_sweep(coarsest, 0, rows, False))

    def prolong_coarsest(layer_no):
        place = slice(GUARD, GUARD + rows)
        for c in range(count[coarsest - 1]):
            parent = c * count[coarsest] // count[coarsest - 1]
            value[coarsest - 1][layer_no, c, place] += value[coarsest][layer_no, parent, place]

    pl.loop(0, layers, unroll=4)(prolong_coarsest)

    for m in range(coarsest - 1, -1, -1):
        low = (reach - m - 1) // 8 * 8
        high = rounded_up(reach + own_rows + m + 1, 8)
        later_sweep(m, low, high, m > 0)

    chunks = count[0]
    lane = lane_numbers(own_rows)

    lanes = LANES // chunks
    back = (lane & (chunks - 1)) * lanes + lane // chunks

    def in_order(cells, tile_no):
        start = (plan.side_cols + tile_no * LANES) // chunks
        out = turned(cells[0], -start)
        for c in range(1, chunks):
            out = jnp.where(lane >= c * lanes, turned(cells[c], c * lanes - start), out)
        return taken(out, back)

    def finish(layer_no):
        low, high = reach, reach + own_rows
        own = span(GUARD + low, GUARD + high)
        plain = span(low, high)
        cells, remains = [], []
        for c in range(chunks):
            now = value[0][layer_no, c, own]
            centre = (
                west[0][layer_no, c, plain]
                + west[0][layer_no, c, span(low + 1, high + 1)]
                + south[0][layer_no, c, plain]
                + south[0][layer_no, c + 1, plain]
                + upper[0][layer_no, c, plain]
                + upper[0][layer_no + 1, c, plain]
            )
            remain = (
                forcing[0][layer_no, c, plain] - centre * now + around(0, layer_no, c, low, high)
            )
            above = upper[0][layer_no, c, plain] * value[0][jnp.maximum(layer_no - 1, 0), c, own]
            remain += jnp.where(layer_no > 0, above, 0.0)
            beneath = value[0][jnp.minimum(layer_no + 1, layers - 1), c, own]
            remain += upper[0][layer_no + 1, c, plain] * beneath
            cells.append(now)
            remains.append(remain)
        for tile_no in range(plan.own_cols // LANES):
            columns = slice(tile_no * LANES, (tile_no + 1) * LANES)
            staged[0][layer_no, :, columns] = in_order(cells, tile_no)
            staged[1][layer_no, :, columns] = in_order(remains, tile_no)

    def leave(group):
        block = pl.ds(4 * group, 4)
        return [
            pltpu.make_async_copy(
                staged[i].at[block], out_refs[i].at[block], semaphore.at[i, group]
            )
            for i in range(2)
        ]

    def finish_group(group):
        for i in range(4):
            finish(4 * group + i)
        for copy in leave(group):
            copy.start()

    pl.loop(0, layers // 4)(finish_group)
    for group in range(layers // 4):
        for copy in leave(group):
            copy.wait()


def per_device(source, inv_density):
    layers, rows, cols = source.shape
    plan = Plan(lax.axis_size("cross"), layers, rows, cols)
    levels = plan.coarsest + 1
    vmem = pl.BlockSpec(memory_space=pltpu.VMEM)

    shape = functools.partial(jax.ShapeDtypeStruct, dtype=jnp.float32)

    def kernel(body, inputs, outputs):
        return pl.pallas_call(
            functools.partial(body, plan),
            out_shape=outputs,
            in_specs=[vmem] * len(inputs),
            out_specs=[vmem] * len(outputs),
            compiler_params=pltpu.CompilerParams(vmem_limit_bytes=24 << 20),
        )(*inputs)

    def exchanged(sent, axis):
        return [
            swapped(each, axis, index // 2 + 1, 1 - index % 2) for index, each in enumerate(sent)
        ]

    def pairs_of(messages, *tail):
        half = len(messages) // 2
        return [shape((each.size,) + tail) for each in messages[:half] if each.size for _ in range(2)]

    cross_shapes = pairs_of(plan.cross, rows, LANES)
    both = jnp.stack([inv_density, source])
    halos = exchanged(kernel(edge_kernel, [both], cross_shapes), "cross")
    cells, *sent = kernel(
        cells_kernel,
        [both],
        [shape((2, layers, plan.halves, rows, LANES))] + pairs_of(plan.along, 8, LANES),
    )
    beside = exchanged(sent, "along")
    corners = []
    for swap, halo in enumerate(halos):
        messages = [each[swap // 2] for each in plan.corners]
        sent = kernel(
            functools.partial(corner_kernel, swap // 2), [halo], pairs_of(messages, 8, LANES)
        )
        corners.append(exchanged(sent, "along"))
    window = kernel(
        window_kernel,
        [cells, *halos, *beside, *corners[0]],
        [shape((2, layers, plan.chunks, rows, LANES))]
        + [shape((plan.side_size(side), 8, LANES)) for side in range(len(plan.along))],
    )
    inputs = [*window, *sum(corners[1:], [])]

    def room(*shape):
        return pltpu.VMEM(shape + (LANES,), jnp.float32)

    total, high = plan.rows, plan.rows + GUARD
    counts = [plan.level_chunks(m) for m in range(levels)]
    scratch = [pltpu.VMEM((layers, rows, cols), jnp.float32)] * 2
    scratch += [
        room(layers, counts[-1], total),
        room(layers + 1, counts[0], total),
        pltpu.SMEM((1,), jnp.int32),
        pltpu.SemaphoreType.DMA((2, layers // 4)),
    ]
    scratch += [room(layers, n, high) for n in counts]
    scratch += [room(layers, n + 1, total) for n in counts]
    scratch += [room(layers, n, total) for n in counts]
    scratch += [room(layers, n, total) for n in counts]
    scratch += [room(layers, n, high + GUARD) for n in counts]
    scratch += [room(layers, counts[0], total + 8)]
    scratch += [room(layers + 1, n, total) for n in counts[1:]]
    held = sum(math.prod(each.shape) for each in scratch) + sum(each.size for each in inputs)
    held = 4 * held
    return pl.pallas_call(
        functools.partial(cycle_kernel, plan),
        out_shape=[jax.ShapeDtypeStruct((layers, rows, cols), jnp.float32)] * 2,
        in_specs=[vmem] * len(inputs),
        out_specs=[pl.BlockSpec(memory_space=pl.ANY)] * 2,
        scratch_shapes=scratch,
        compiler_params=pltpu.CompilerParams(vmem_limit_bytes=held + (3 << 20)),
    )(*inputs)


def solution(mesh):
    return jax.shard_map(
        per_device,
        mesh=mesh,
        in_specs=(P(None, "along", "cross"), P(None, "along", "cross")),
        out_specs=(P(None, "along", "cross"), P(None, "along", "cross")),
        check_vma=False,
    )
```
